32 devices in a mesh: band: 16 (over z, y, core), member: 2 (over x).
Axes of the slice: x: 2, y: 2, z: 4, core: 2. Of those that a mesh axis runs over, the one named last changes fastest.
Arguments:
- grid_latent: bfloat16 [2, 16384, 512], P('member', 'band'), may hold values from -6 to 6
- mesh_latent: bfloat16 [2, 16384, 512], P('member', 'band'), may hold values from -6 to 6
- edge_attr: bfloat16 [4, 4, 16384], P(None, None, 'band'), may hold values from -5 to 5
- neighbours: int32 [16384, 4], P('band'), may hold values from 0 to 2047, as said below
- send_rows: int32 [32, 512], P('band'), may hold values from 0 to 1023, as said below
- target: float32 [100, 16384], P(None, 'band'), may hold values from -6 to 6
- field_weight: float32 [100], replicated, may hold values from 1 to 10
- w_src: bfloat16 [512, 512], replicated, may hold values from -0.25 to 0.25
- w_dst: bfloat16 [512, 512], replicated, may hold values from -0.25 to 0.25
- w_edge: bfloat16 [4, 512], replicated, may hold values from -3 to 3
- w_msg: bfloat16 [512, 512], replicated, may hold values from -0.25 to 0.25
- ln_gain: float32 [512], replicated, may hold values from 0.1 to 1.9
- w_out: bfloat16 [512, 100], replicated, may hold values from -0.25 to 0.25
Outputs:
- d_grid: bfloat16 [2, 16384, 512], P('member', 'band')
- d_mesh: bfloat16 [2, 16384, 512], P('member', 'band')
The draws below stay inside these ranges and needn't reach their ends.
Inputs may be any that keep to these rules, and one draw needn't show every extreme that they name: `neighbours`: grid points of band index 0 never name slots 1024 to 1535, those of the last band index never name slots 1024 + 512 and up. `send_rows`: the two lists of one band index hold 1024 distinct rows together.
All inputs are finite; a program needn't handle non-finite values.
Results may differ from the reference program's by a relative error of at most 0.04.
Values may be sent and summed in bfloat16 or wider, within the bound.
No kernel may reach another device: no remote copies, remote signals or barrier semaphores. Data moves between devices by JAX's collectives and lax.ppermute only.
A program may use at most 128 MiB of HBM per device.

```python
import math
import jax
import jax.numpy as jnp
from jax import lax

LATENT = 512
FIELDS = 100
EDGES = 4
EDGE_FEATS = 4
GRID_DEV = 1024
MESH_DEV = 1024
HALO = 512
SLOTS = 2048
MEMBERS = 2
GRID = 16384
MESH = 16384
SENDS = 32
N_BAND = 16


def draw_send_rows(key, part):
    key = jax.random.fold_in(key, 11)
    bands = SENDS // 2

    def one_band(index):
        shuffled = jax.random.permutation(jax.random.fold_in(key, index), MESH_DEV)
        return shuffled[:2 * HALO].reshape(2, HALO)
    lists = jax.vmap(one_band)(jnp.arange(bands, dtype=jnp.int32))
    return lists.reshape(SENDS, HALO).astype(jnp.int32)


def draw_neighbours(key, part):
    key = jax.random.fold_in(key, 17)
    bands = GRID // GRID_DEV
    key_kind, key_local, key_rim = jax.random.split(key, 3)
    kind = jax.random.randint(key_kind, (GRID, EDGES), 0, 4)
    local = jax.random.randint(key_local, (GRID, EDGES), 0, MESH_DEV)
    rim = jax.random.randint(key_rim, (GRID, EDGES), 0, HALO)
    device = (jnp.arange(GRID, dtype=jnp.int32) // GRID_DEV)[:, None]
    below = (kind == 2) & (device > 0)
    above = (kind == 3) & (device < bands - 1)
    slots = jnp.where(below, MESH_DEV + rim, jnp.where(above, MESH_DEV + HALO + rim, local))
    return slots.astype(jnp.int32)


def shard_levels(stream_key, shape, cuts, low, high):
    def one(dim, parts):
        steps = jax.random.uniform(jax.random.fold_in(jax.random.fold_in(stream_key, 6), dim), (parts,), jnp.float32, low / len(cuts), high / len(cuts))
        return jnp.repeat(jnp.exp(steps), shape[dim] // parts).reshape((-1,) + (1,) * (len(shape) - dim - 1))

    loudness = one(*cuts[0])
    for cut in cuts[1:]:
        loudness = loudness * one(*cut)
    return loudness


def noise(own_key, dims, deviation, reach, shards=(), held_as=jnp.bfloat16):
    values = deviation * jax.random.normal(own_key, dims, jnp.float32)
    if shards:
        values = values * shard_levels(own_key, dims, shards, -0.22, 0.18)
    return jnp.clip(values, -reach, reach).astype(held_as)


def setup_inputs(seed: int = 0) -> dict:
    key_of = jax.random.split(jax.random.key(seed), 14)
    grid_latent = noise(key_of[0], (MEMBERS, GRID, LATENT), 1.0, 6.0, ((0, 2), (1, 16)))
    mesh_latent = noise(key_of[1], (MEMBERS, MESH, LATENT), 1.0, 6.0, ((0, 2), (1, 16)))
    edge_attr = noise(key_of[2], (EDGE_FEATS, EDGES, GRID), 1.0, 5.0, ((2, 16),))
    neighbours = draw_neighbours(jax.random.fold_in(key_of[13], 71), 0)
    send_rows = draw_send_rows(jax.random.fold_in(key_of[13], 71), 0)
    target = noise(key_of[5], (FIELDS, GRID), 1.0, 6.0, ((1, 16),), jnp.float32)
    field_weight = jnp.clip(jnp.exp(jax.random.uniform(key_of[6], (FIELDS,), jnp.float32, math.log(1.0), math.log(10.0))), 1.0, 10.0)
    w_src = noise(key_of[7], (LATENT, LATENT), LATENT ** -0.5, 0.25)
    w_dst = noise(key_of[8], (LATENT, LATENT), LATENT ** -0.5, 0.25)
    w_edge = noise(key_of[9], (EDGE_FEATS, LATENT), EDGE_FEATS ** -0.5, 3.0)
    w_msg = noise(key_of[10], (LATENT, LATENT), LATENT ** -0.5, 0.25)
    ln_gain = jnp.clip(1.0 + 0.18 * jax.random.normal(key_of[11], (LATENT,), jnp.float32), 0.1, 1.9)
    w_out = noise(key_of[12], (LATENT, FIELDS), LATENT ** -0.5, 0.25)
    return {"grid_latent": grid_latent, "mesh_latent": mesh_latent, "edge_attr": edge_attr, "neighbours": neighbours, "send_rows": send_rows, "target": target, "field_weight": field_weight, "w_src": w_src, "w_dst": w_dst, "w_edge": w_edge, "w_msg": w_msg, "ln_gain": ln_gain, "w_out": w_out}


DELTA_SQ = 0.0625
ALPHA = 0.95
LN_EPS = 1e-05

def slope(diff):
    return diff / jnp.sqrt(diff * diff + DELTA_SQ)

def as_wide(value):
    return value.astype(jnp.float32)

def times_transposed(left, weight):
    return lax.dot_general(as_wide(left), as_wide(weight), (((1,), (1,)), ((), ())), preferred_element_type=jnp.float32)

def slot_tables(neighbours, send_rows):
    sends = send_rows.reshape(N_BAND, 2, HALO)
    device = jnp.arange(N_BAND, dtype=jnp.int32)
    below = jnp.maximum(device - 1, 0)
    above = jnp.minimum(device + 1, N_BAND - 1)
    own_rows = device[:, None] * MESH_DEV + jnp.arange(MESH_DEV, dtype=jnp.int32)[None, :]
    from_below = below[:, None] * MESH_DEV + sends[below, 1]
    from_above = above[:, None] * MESH_DEV + sends[above, 0]
    table = jnp.concatenate([own_rows, from_below, from_above], axis=1).astype(jnp.int32)
    local_slots = neighbours.reshape(N_BAND, GRID_DEV * EDGES).astype(jnp.int32)
    nodes = jnp.take_along_axis(table, local_slots, axis=1).reshape(GRID, EDGES)
    return (table, local_slots, nodes)

def forward_member(grid_rows, mesh_rows, nodes, edge_embed, w_src, w_dst, w_msg, ln_gain, w_out):
    src = jnp.dot(as_wide(mesh_rows), as_wide(w_src), preferred_element_type=jnp.float32).astype(jnp.bfloat16)
    dst = jnp.dot(as_wide(grid_rows), as_wide(w_dst), preferred_element_type=jnp.float32)
    pre = src[nodes].astype(jnp.float32) + dst[:, None, :] + edge_embed
    act = jax.nn.silu(pre).astype(jnp.bfloat16)
    agg = jnp.dot(as_wide(act.reshape(GRID * EDGES, LATENT)), as_wide(w_msg), preferred_element_type=jnp.float32)
    z_rows = grid_rows.astype(jnp.float32) + agg.reshape(GRID, EDGES, LATENT).sum(axis=1)
    centre = z_rows - lax.optimization_barrier(jnp.mean(z_rows, axis=1, keepdims=True))
    rstd = 1.0 / jnp.sqrt(lax.optimization_barrier(jnp.mean(centre * centre, axis=1, keepdims=True)) + LN_EPS)
    zhat = centre * rstd
    normed = (zhat * ln_gain[None, :]).astype(jnp.bfloat16)
    pred = lax.dot_general(as_wide(w_out), as_wide(normed), (((0,), (1,)), ((), ())), preferred_element_type=jnp.float32)
    return (pred, pre, zhat, rstd)

def reference(grid_latent, mesh_latent, edge_attr, neighbours, send_rows, target, field_weight, w_src, w_dst, w_edge, w_msg, ln_gain, w_out):
    table, local_slots, nodes = slot_tables(neighbours, send_rows)
    edge_embed = jnp.einsum('ekg,eh->gkh', as_wide(edge_attr), as_wide(w_edge), preferred_element_type=jnp.float32)

    def run_forward(pair):
        return forward_member(pair[0], pair[1], nodes, edge_embed, w_src, w_dst, w_msg, ln_gain, w_out)[0]
    preds = lax.map(run_forward, (grid_latent, mesh_latent))
    coeff = ALPHA / (MEMBERS - 1) + (1.0 - ALPHA) / MEMBERS

    def member_grad(own_pred):
        spread = lax.optimization_barrier(jnp.sum(slope(own_pred[None, :, :] - preds), axis=0))
        return (field_weight[:, None] * (slope(own_pred - target) - coeff * spread)).astype(jnp.bfloat16)
    d_preds = lax.map(member_grad, preds)

    def run_backward(triple):
        grid_rows, mesh_rows, d_pred = triple
        pred, pre, zhat, rstd = forward_member(grid_rows, mesh_rows, nodes, edge_embed, w_src, w_dst, w_msg, ln_gain, w_out)
        d_u = lax.dot_general(as_wide(d_pred), as_wide(w_out), (((0,), (1,)), ((), ())), preferred_element_type=jnp.float32)
        scaled = d_u * ln_gain[None, :]
        d_z = rstd * (scaled - lax.optimization_barrier(jnp.mean(scaled, axis=1, keepdims=True)) - zhat * lax.optimization_barrier(jnp.mean(scaled * zhat, axis=1, keepdims=True)))
        d_act = times_transposed(d_z.astype(jnp.bfloat16), w_msg)
        sigma = jax.nn.sigmoid(pre)
        d_pre = (d_act[:, None, :] * (sigma * (1.0 + pre * (1.0 - sigma)))).astype(jnp.bfloat16)
        d_sum = lax.optimization_barrier(jnp.sum(d_pre.astype(jnp.float32), axis=1)).astype(jnp.bfloat16)
        d_grid = (d_z + times_transposed(d_sum, w_dst)).astype(jnp.bfloat16)
        per_device = d_pre.reshape(N_BAND, GRID_DEV * EDGES, LATENT).astype(jnp.float32)
        device = jnp.arange(N_BAND, dtype=jnp.int32)[:, None]
        slot_grad = jnp.zeros((N_BAND, SLOTS, LATENT), jnp.float32).at[device, local_slots].add(per_device)
        slot_grad = slot_grad.astype(jnp.bfloat16)
        contrib = times_transposed(slot_grad.reshape(N_BAND * SLOTS, LATENT), w_src)
        d_mesh = jnp.zeros((MESH, LATENT), jnp.float32).at[table.reshape(-1)].add(contrib)
        return (d_grid, d_mesh.astype(jnp.bfloat16))
    d_grid, d_mesh = lax.map(run_backward, (grid_latent, mesh_latent, d_preds))
    return (d_grid, d_mesh)
```

```python
import functools

import jax
import jax.numpy as jnp
from jax import lax
from jax.experimental import pallas as pl
from jax.experimental.pallas import tpu as pltpu
from jax.sharding import PartitionSpec as P

DELTA_SQ = 0.0625
ALPHA = 0.95
LN_EPS = 1e-05
F32 = jnp.float32
BF16 = jnp.bfloat16
VMEM_LIMIT = 48 * 1024 * 1024


def slope(diff):
    return diff * lax.rsqrt(diff * diff + DELTA_SQ)


def mm(left, right):
    return jnp.dot(left, right, preferred_element_type=F32)


def mm_t(left, right):
    return lax.dot_general(left, right, (((1,), (1,)), ((), ())), preferred_element_type=F32)


def one_hot(ids, shape, dim):
    return jnp.where(ids == lax.broadcasted_iota(jnp.int32, shape, dim), 1.0, 0.0).astype(BF16)


def whole(*shape):
    return pl.BlockSpec(shape, lambda *_: (0,) * len(shape))


def padded(array, dim, size):
    widths = [(0, 0)] * array.ndim
    widths[dim] = (0, size - array.shape[dim])
    return jnp.pad(array, widths)


def call(body, grid, in_specs, out_specs, out_shape, flops, nbytes, scratch=()):
    return pl.pallas_call(
        body,
        grid=grid,
        in_specs=in_specs,
        out_specs=out_specs,
        out_shape=out_shape,
        scratch_shapes=scratch,
        compiler_params=pltpu.CompilerParams(vmem_limit_bytes=VMEM_LIMIT),
        cost_estimate=pl.CostEstimate(flops=flops, bytes_accessed=nbytes, transcendentals=0),
    )


def send_kernel(mesh_ref, w_src_ref, send_ref, src_ref, low_ref, high_ref):
    src = mm(mesh_ref[...], w_src_ref[...]).astype(BF16)
    src_ref[...] = src
    owned = src.shape[0]
    half = low_ref.shape[0]
    for part, out in ((0, low_ref), (1, high_ref)):
        ids = send_ref[part * half : (part + 1) * half, :]
        out[...] = mm(one_hot(ids, (half, owned), 1), src).astype(BF16)


def own_kernel(edges, nb_ref, src_ref, grid_ref, w_dst_ref, attr_ref, w_edge_ref, pre_ref, dst_ref):
    rows = grid_ref.shape[0]
    owned = src_ref.shape[0]
    dst_ref[...] = mm(grid_ref[...], w_dst_ref[...])
    for k in range(edges):
        hot = one_hot(nb_ref[:, k : k + 1], (rows, owned), 1)
        embed = mm(attr_ref[...], w_edge_ref[k])
        pre_ref[k] = mm(hot, src_ref[...]) + embed + dst_ref[...]


def forward_kernel(
    edges,
    owned,
    nb_ref,
    pre_ref,
    below_ref,
    above_ref,
    grid_ref,
    w_msg_ref,
    gain_ref,
    w_out_ref,
    pred_ref,
    pred_bf_ref,
    sg_ref,
    zhat_ref,
    rstd_ref,
):
    rows = grid_ref.shape[0]
    halo = below_ref.shape[0]
    total = jnp.zeros(grid_ref.shape, F32)
    for k in range(edges):
        ids = nb_ref[:, k : k + 1] - owned
        pre = (
            pre_ref[k]
            + mm(one_hot(ids, (rows, halo), 1), below_ref[...])
            + mm(one_hot(ids - halo, (rows, halo), 1), above_ref[...])
        )
        sigma = 0.5 + 0.5 * jnp.tanh(0.5 * pre)
        act = pre * sigma
        total = total + act
        sg_ref[k] = (sigma + act - act * sigma).astype(BF16)
    z = grid_ref[...].astype(F32) + mm(total.astype(BF16), w_msg_ref[...])
    centre = z - jnp.mean(z, axis=1, keepdims=True)
    rstd = lax.rsqrt(jnp.mean(centre * centre, axis=1, keepdims=True) + LN_EPS)
    zhat = centre * rstd
    pred = mm((zhat * gain_ref[...]).astype(BF16), w_out_ref[...])
    pred_ref[...] = pred
    pred_bf_ref[...] = pred.astype(BF16)
    zhat_ref[...] = zhat.astype(BF16)
    rstd_ref[...] = jnp.broadcast_to(rstd, rstd_ref.shape)


def backward_kernel(
    edges,
    owned,
    coeff,
    nbt_ref,
    pred_ref,
    others_ref,
    target_ref,
    weight_ref,
    w_out_ref,
    gain_ref,
    zhat_ref,
    rstd_ref,
    w_msg_ref,
    sg_ref,
    dz_ref,
    dsum_ref,
    dpre_ref,
    below_ref,
    above_ref,
    below_acc,
    above_acc,
):
    step = pl.program_id(0)

    @pl.when(step == 0)
    def _():
        below_acc[...] = jnp.zeros_like(below_acc)
        above_acc[...] = jnp.zeros_like(above_acc)

    rows = pred_ref.shape[0]
    halo = below_ref.shape[0]
    pred = pred_ref[...]
    spread = jnp.zeros_like(pred)
    for other in range(others_ref.shape[0]):
        spread = spread + slope(pred - others_ref[other].astype(F32))
    d_pred = (weight_ref[...] * (slope(pred - target_ref[...]) - coeff * spread)).astype(BF16)
    scaled = mm_t(d_pred, w_out_ref[...]) * gain_ref[...]
    zhat = zhat_ref[...].astype(F32)
    d_z = rstd_ref[:, :1] * (
        scaled
        - jnp.mean(scaled, axis=1, keepdims=True)
        - zhat * jnp.mean(scaled * zhat, axis=1, keepdims=True)
    )
    d_zb = d_z.astype(BF16)
    dz_ref[...] = d_zb
    d_act = mm_t(d_zb, w_msg_ref[...])
    total = jnp.zeros(d_act.shape, F32)
    for k in range(edges):
        d_pre = d_act * sg_ref[k].astype(F32)
        total = total + d_pre
        d_pre = d_pre.astype(BF16)
        dpre_ref[k] = d_pre
        ids = nbt_ref[k : k + 1, :] - owned
        below_acc[...] += mm(one_hot(ids, (halo, rows), 0), d_pre)
        above_acc[...] += mm(one_hot(ids - halo, (halo, rows), 0), d_pre)
    dsum_ref[...] = total.astype(BF16)

    @pl.when(step == pl.num_programs(0) - 1)
    def _():
        below_ref[...] = below_acc[...].astype(BF16)
        above_ref[...] = above_acc[...].astype(BF16)


def own_grad_kernel(edges, nbt_ref, dpre_ref, dz_ref, dsum_ref, w_dst_ref, grid_out_ref, slot_ref):
    step = pl.program_id(0)

    @pl.when(step == 0)
    def _():
        slot_ref[...] = jnp.zeros_like(slot_ref)

    rows = dz_ref.shape[0]
    owned = slot_ref.shape[0]
    grid_out_ref[...] = (dz_ref[...].astype(F32) + mm_t(dsum_ref[...], w_dst_ref[...])).astype(BF16)
    for k in range(edges):
        slot_ref[...] += mm(one_hot(nbt_ref[k : k + 1, :], (owned, rows), 0), dpre_ref[k])


def mesh_kernel(send_ref, from_low_ref, from_high_ref, slot_ref, w_src_ref, out_ref):
    owned = slot_ref.shape[0]
    half = from_low_ref.shape[0]
    total = slot_ref[...]
    for part, back in ((0, from_low_ref), (1, from_high_ref)):
        hot = one_hot(send_ref[part : part + 1, :], (owned, half), 0)
        total = total + mm(hot, back[...])
    out_ref[...] = mm_t(total.astype(BF16), w_src_ref[...]).astype(BF16)


def per_device(
    grid_latent,
    mesh_latent,
    edge_attr,
    neighbours,
    send_rows,
    target,
    field_weight,
    w_src,
    w_dst,
    w_edge,
    w_msg,
    ln_gain,
    w_out,
):
    grid_rows = grid_latent[0]
    mesh_rows = mesh_latent[0]
    points, channels = grid_rows.shape
    owned = mesh_rows.shape[0]
    halo = send_rows.shape[1]
    edges = neighbours.shape[1]
    feats = w_edge.shape[0]
    lanes = 128
    fields = -(-w_out.shape[1] // lanes) * lanes
    block = min(points, 256)
    steps = points // block
    sds = jax.ShapeDtypeStruct
    bands = lax.axis_size("band")
    up = [(i, i + 1) for i in range(bands - 1)]
    down = [(i + 1, i) for i in range(bands - 1)]
    members = lax.axis_size("member")

    src, low, high = call(
        send_kernel,
        (1,),
        [whole(owned, channels), whole(channels, channels), whole(2 * halo, 1)],
        [whole(owned, channels), whole(halo, channels), whole(halo, channels)],
        [sds((owned, channels), BF16), sds((halo, channels), BF16), sds((halo, channels), BF16)],
        2 * owned * channels * (channels + 2 * halo),
        4 * owned * channels * 2,
    )(mesh_rows, w_src, send_rows.reshape(2 * halo, 1))
    from_above = lax.ppermute(low, "band", down)
    from_below = lax.ppermute(high, "band", up)

    nb_spec = pl.BlockSpec((block, edges), lambda i: (i, 0))
    nbt_spec = pl.BlockSpec((edges, block), lambda i: (0, i))
    row_spec = pl.BlockSpec((block, channels), lambda i: (i, 0))
    edge_spec = pl.BlockSpec((edges, block, channels), lambda i: (0, i, 0))
    field_spec = pl.BlockSpec((block, fields), lambda i: (i, 0))
    rstd_spec = pl.BlockSpec((block, 128), lambda i: (i, 0))
    gain = ln_gain[None, :]
    attr = padded(edge_attr.reshape(feats * edges, points), 0, lanes).T
    same = jnp.eye(edges, dtype=BF16)[:, None, :, None]
    w_edge = (same * w_edge[None, :, None, :]).reshape(edges, feats * edges, channels)
    w_edge = padded(w_edge, 1, lanes)
    nbt = neighbours.T
    w_out = padded(w_out, 1, fields)
    target = padded(target, 0, fields).T
    weight = padded(field_weight[None, :], 1, fields)

    pre = call(
        functools.partial(own_kernel, edges),
        (steps,),
        [
            nb_spec,
            whole(owned, channels),
            row_spec,
            whole(channels, channels),
            pl.BlockSpec((block, lanes), lambda i: (i, 0)),
            whole(edges, lanes, channels),
        ],
        edge_spec,
        sds((edges, points, channels), F32),
        2 * points * channels * (edges * owned + channels),
        points * channels * edges * 4,
        [pltpu.VMEM((block, channels), F32)],
    )(neighbours, src, grid_rows, w_dst, attr, w_edge)

    pred, pred_bf, sg, zhat, rstd = call(
        functools.partial(forward_kernel, edges, owned),
        (steps,),
        [
            nb_spec,
            edge_spec,
            whole(halo, channels),
            whole(halo, channels),
            row_spec,
            whole(channels, channels),
            whole(1, channels),
            whole(channels, fields),
        ],
        [field_spec, field_spec, edge_spec, row_spec, rstd_spec],
        [
            sds((points, fields), F32),
            sds((points, fields), BF16),
            sds((edges, points, channels), BF16),
            sds((points, channels), BF16),
            sds((points, 128), F32),
        ],
        2 * points * channels * (edges * 2 * halo + channels),
        points * channels * edges * 6,
    )(neighbours, pre, from_below, from_above, grid_rows, w_msg, gain, w_out)

    if members == 2:
        others = lax.ppermute(pred_bf, "member", [(0, 1), (1, 0)])[None]
    else:
        others = lax.all_gather(pred_bf[None], "member", axis=0, tiled=True)
    coeff = ALPHA / (members - 1) + (1.0 - ALPHA) / members

    d_z, d_sum, d_pre, rim_below, rim_above = call(
        functools.partial(backward_kernel, edges, owned, coeff),
        (steps,),
        [
            nbt_spec,
            field_spec,
            pl.BlockSpec((others.shape[0], block, fields), lambda i: (0, i, 0)),
            field_spec,
            whole(1, fields),
            whole(channels, fields),
            whole(1, channels),
            row_spec,
            rstd_spec,
            whole(channels, channels),
            edge_spec,
        ],
        [row_spec, row_spec, edge_spec, whole(halo, channels), whole(halo, channels)],
        [
            sds((points, channels), BF16),
            sds((points, channels), BF16),
            sds((edges, points, channels), BF16),
            sds((halo, channels), BF16),
            sds((halo, channels), BF16),
        ],
        2 * points * channels * (edges * 2 * halo + channels),
        points * channels * edges * 4,
        [pltpu.VMEM((halo, channels), F32), pltpu.VMEM((halo, channels), F32)],
    )(
        nbt, pred, others, target, weight, w_out, gain, zhat, rstd, w_msg, sg
    )
    back_high = lax.ppermute(rim_below, "band", down)
    back_low = lax.ppermute(rim_above, "band", up)

    d_grid, slot_own = call(
        functools.partial(own_grad_kernel, edges),
        (steps,),
        [nbt_spec, edge_spec, row_spec, row_spec, whole(channels, channels)],
        [row_spec, whole(owned, channels)],
        [sds((points, channels), BF16), sds((owned, channels), F32)],
        2 * points * channels * (edges * owned + channels),
        points * channels * edges * 4,
    )(nbt, d_pre, d_z, d_sum, w_dst)

    d_mesh = call(
        mesh_kernel,
        (1,),
        [
            whole(2, halo),
            whole(halo, channels),
            whole(halo, channels),
            whole(owned, channels),
            whole(channels, channels),
        ],
        whole(owned, channels),
        sds((owned, channels), BF16),
        2 * owned * channels * (channels + 2 * halo),
        owned * channels * 8,
    )(send_rows, back_low, back_high, slot_own, w_src)
    return (d_grid[None], d_mesh[None])


def solution(mesh):
    placed = (
        P("member", "band", None),
        P("member", "band", None),
        P(None, None, "band"),
        P("band", None),
        P("band", None),
        P(None, "band"),
        P(),
        P(),
        P(),
        P(),
        P(),
        P(),
        P(),
    )
    return jax.shard_map(
        per_device,
        mesh=mesh,
        in_specs=placed,
        out_specs=(P("member", "band", None), P("member", "band", None)),
        check_vma=False,
    )
```

```python
import functools

import jax
import jax.numpy as jnp
from jax import lax
from jax.experimental import pallas as pl
from jax.experimental.pallas import tpu as pltpu
from jax.sharding import PartitionSpec as P

DELTA_SQ = 0.0625
ALPHA = 0.95
LN_EPS = 1e-05
F32 = jnp.float32
BF16 = jnp.bfloat16
VMEM_LIMIT = 28 * 1024 * 1024


def slope(diff):
    return diff * lax.rsqrt(diff * diff + DELTA_SQ)


def mm(left, right):
    return jnp.dot(left, right, preferred_element_type=F32)


def mm_t(left, right):
    return lax.dot_general(left, right, (((1,), (1,)), ((), ())), preferred_element_type=F32)


def column_hot(ids, base, slots):
    lanes = 128
    rows = ids.shape[1]
    column = jnp.broadcast_to((ids - base).astype(F32), (lanes, rows)).T.astype(jnp.int16)
    lane = lax.broadcasted_iota(jnp.int16, (rows, lanes), 1)
    parts = [
        jnp.where(column == lane + jnp.int16(first), BF16(1), BF16(0))
        for first in range(0, slots, lanes)
    ]
    return jnp.concatenate(parts, axis=1)


def row_hot(ids, base, slots):
    row = (ids - base).astype(jnp.int16)
    return jnp.where(
        row == lax.broadcasted_iota(jnp.int16, (slots, ids.shape[1]), 0), BF16(1), BF16(0)
    )


def row_hots(ids_ref, base, slots):
    return jnp.concatenate(
        [row_hot(ids_ref[k : k + 1, :], base, slots) for k in range(ids_ref.shape[0])], axis=1
    )


def whole(*shape):
    return pl.BlockSpec(shape, lambda *_: (0,) * len(shape))


def padded(array, dim, size):
    widths = [(0, 0)] * array.ndim
    widths[dim] = (0, size - array.shape[dim])
    return jnp.pad(array, widths)


def swap(firsts):
    return [pair for i in firsts for pair in ((i, i + 1), (i + 1, i))]


def call(body, grid, in_specs, out_specs, out_shape, flops, nbytes, scratch=()):
    return pl.pallas_call(
        body,
        grid=grid,
        in_specs=in_specs,
        out_specs=out_specs,
        out_shape=out_shape,
        scratch_shapes=scratch,
        compiler_params=pltpu.CompilerParams(vmem_limit_bytes=VMEM_LIMIT),
        cost_estimate=pl.CostEstimate(flops=flops, bytes_accessed=nbytes, transcendentals=0),
    )


def send_kernel(mesh_ref, w_src_ref, send_ref, src_ref, near_ref, far_ref):
    src = mm(mesh_ref[...], w_src_ref[...]).astype(BF16)
    src_ref[...] = src
    owned = src.shape[0]
    far_ref[...] = mm(column_hot(send_ref[1:2, :], 0, owned), src).astype(BF16)
    near_ref[...] = mm(column_hot(send_ref[0:1, :], 0, owned), src).astype(BF16)


def own_kernel(
    slots_ref, src_ref, near_ref, grid_ref, w_dst_ref, attr_ref, w_edge_ref, pre_ref, dst_ref
):
    owned = src_ref.shape[0]
    near = near_ref.shape[0]
    dst_ref[...] = mm(grid_ref[...], w_dst_ref[...])
    for k in range(slots_ref.shape[0]):
        ids = slots_ref[k : k + 1, :]
        picked = mm(column_hot(ids, 0, owned), src_ref[...])
        picked = picked + mm(column_hot(ids, owned, near), near_ref[...])
        embed = mm(attr_ref[...], w_edge_ref[k])
        pre_ref[k] = (picked + embed + dst_ref[...]).astype(BF16)


def forward_kernel(
    base,
    slots_ref,
    pre_ref,
    far_ref,
    grid_ref,
    w_msg_ref,
    gain_ref,
    w_out_ref,
    pred_ref,
    pred_bf_ref,
    sg_ref,
    zhat_ref,
    rstd_ref,
):
    half = BF16(0.5)
    acts = []
    for k in range(slots_ref.shape[0]):
        hot = column_hot(slots_ref[k : k + 1, :], base, far_ref.shape[0])
        pre = pre_ref[k] + mm(hot, far_ref[...]).astype(BF16)
        sigma = half + half * jnp.tanh(half * pre)
        act = pre * sigma
        acts.append(act)
        sg_ref[k] = sigma + (act - act * sigma)
    while len(acts) > 1:
        acts = [sum(acts[i : i + 2][1:], acts[i]) for i in range(0, len(acts), 2)]
    z = grid_ref[...].astype(F32) + mm(acts[0], w_msg_ref[...])
    centre = z - jnp.mean(z, axis=1, keepdims=True)
    rstd = lax.rsqrt(jnp.mean(centre * centre, axis=1, keepdims=True) + LN_EPS)
    zhat = centre * rstd
    pred = mm_t((zhat * gain_ref[...]).astype(BF16), w_out_ref[...])
    pred_ref[...] = pred
    pred_bf_ref[...] = pred.astype(BF16)
    zhat_ref[...] = zhat.astype(BF16)
    rstd_ref[...] = jnp.broadcast_to(rstd, rstd_ref.shape)


def backward_kernel(
    base,
    coeff,
    slots_ref,
    pred_ref,
    others_ref,
    target_ref,
    weight_ref,
    w_out_ref,
    gain_ref,
    zhat_ref,
    rstd_ref,
    w_msg_ref,
    sg_ref,
    dz_ref,
    dsum_ref,
    dpre_ref,
    far_ref,
    far_acc,
):
    step = pl.program_id(0)

    @pl.when(step == 0)
    def _():
        far_acc[...] = jnp.zeros_like(far_acc)

    pred = pred_ref[...]
    spread = jnp.zeros_like(pred)
    for other in range(others_ref.shape[0]):
        spread = spread + slope(pred - others_ref[other].astype(F32))
    d_pred = (weight_ref[...] * (slope(pred - target_ref[...]) - coeff * spread)).astype(BF16)
    scaled = mm(d_pred, w_out_ref[...]) * gain_ref[...]
    zhat = zhat_ref[...].astype(F32)
    d_z = rstd_ref[:, :1] * (
        scaled
        - jnp.mean(scaled, axis=1, keepdims=True)
        - zhat * jnp.mean(scaled * zhat, axis=1, keepdims=True)
    )
    d_zb = d_z.astype(BF16)
    dz_ref[...] = d_zb
    d_act = mm_t(d_zb, w_msg_ref[...])
    d_act_b = d_act.astype(BF16)
    total = jnp.zeros(d_act.shape, F32)
    parts = []
    for k in range(slots_ref.shape[0]):
        d_pre = d_act_b * sg_ref[k]
        total = total + d_pre.astype(F32)
        dpre_ref[k] = d_pre
        parts.append(d_pre)
    dsum_ref[...] = total.astype(BF16)
    hot = row_hots(slots_ref, base, far_ref.shape[0])
    far_acc[...] += mm(hot, jnp.concatenate(parts, axis=0))

    @pl.when(step == pl.num_programs(0) - 1)
    def _():
        far_ref[...] = far_acc[...].astype(BF16)


def rim_kernel(base, slots_ref, dpre_ref, rim_ref, acc):
    step = pl.program_id(0)

    @pl.when(step == 0)
    def _():
        acc[...] = jnp.zeros_like(acc)

    edges, rows, channels = dpre_ref.shape
    hot = row_hots(slots_ref, base, rim_ref.shape[0])
    acc[...] += mm(hot, dpre_ref[...].reshape(edges * rows, channels))

    @pl.when(step == pl.num_programs(0) - 1)
    def _():
        rim_ref[...] = acc[...].astype(BF16)


def own_grad_kernel(slots_ref, dpre_ref, dz_ref, dsum_ref, w_dst_ref, grid_out_ref, own_ref):
    step = pl.program_id(0)

    @pl.when(step == 0)
    def _():
        own_ref[...] = jnp.zeros_like(own_ref)

    edges, rows, channels = dpre_ref.shape
    hot = row_hots(slots_ref, 0, own_ref.shape[0])
    own_ref[...] += mm(hot, dpre_ref[...].reshape(edges * rows, channels))
    grid_out_ref[...] = (dz_ref[...].astype(F32) + mm_t(dsum_ref[...], w_dst_ref[...])).astype(BF16)


def mesh_kernel(send_ref, near_ref, far_ref, own_ref, w_src_ref, out_ref):
    owned = own_ref.shape[0]
    total = own_ref[...] + mm(row_hot(send_ref[0:1, :], 0, owned), near_ref[...])
    total = total + mm(row_hot(send_ref[1:2, :], 0, owned), far_ref[...])
    out_ref[...] = mm_t(total.astype(BF16), w_src_ref[...]).astype(BF16)


def per_device(
    grid_latent,
    mesh_latent,
    edge_attr,
    neighbours,
    send_rows,
    target,
    field_weight,
    w_src,
    w_dst,
    w_edge,
    w_msg,
    ln_gain,
    w_out,
):
    grid_rows = grid_latent[0]
    mesh_rows = mesh_latent[0]
    points, channels = grid_rows.shape
    owned = mesh_rows.shape[0]
    halo = send_rows.shape[1]
    edges = neighbours.shape[1]
    feats = w_edge.shape[0]
    lanes = 128
    fields = -(-w_out.shape[1] // lanes) * lanes
    block = min(points, 256)
    wide = min(points, 512)
    sds = jax.ShapeDtypeStruct
    members = lax.axis_size("member")
    bands = lax.axis_size("band")
    near_swap = swap(range(0, bands - 1, 2))
    far_swap = swap(range(1, bands - 1, 2))
    even = lax.axis_index("band") % 2 == 0
    send_near_far = jnp.where(even, send_rows[::-1], send_rows)
    slots = neighbours.T
    swapped = jnp.where(slots < owned, slots, jnp.where(slots < owned + halo, slots + halo, slots - halo))
    slots = jnp.where(even, swapped, slots)

    src, near, far = call(
        send_kernel,
        (1,),
        [whole(owned, channels), whole(channels, channels), whole(2, halo)],
        [whole(owned, channels), whole(halo, channels), whole(halo, channels)],
        [sds((owned, channels), BF16), sds((halo, channels), BF16), sds((halo, channels), BF16)],
        2 * owned * channels * (channels + 2 * halo),
        4 * owned * channels * 2,
    )(mesh_rows, w_src, send_near_far)
    far = lax.ppermute(far, "band", far_swap)
    near = lax.ppermute(near, "band", near_swap)

    def slots_spec(rows):
        return pl.BlockSpec((edges, rows), lambda i: (0, i))

    def row_spec(rows, width=channels):
        return pl.BlockSpec((rows, width), lambda i: (i, 0))

    def edge_spec(rows):
        return pl.BlockSpec((edges, rows, channels), lambda i: (0, i, 0))

    gain = ln_gain[None, :]
    attr = padded(edge_attr.reshape(feats * edges, points), 0, lanes).T
    same = jnp.eye(edges, dtype=BF16)[:, None, :, None]
    w_edge = (same * w_edge[None, :, None, :]).reshape(edges, feats * edges, channels)
    w_edge = padded(w_edge, 1, lanes)
    w_out = padded(w_out.T, 0, fields)
    target = padded(target, 0, fields).T
    weight = padded(field_weight[None, :], 1, fields)

    pre = call(
        own_kernel,
        (points // block,),
        [
            slots_spec(block),
            whole(owned, channels),
            whole(halo, channels),
            row_spec(block),
            whole(channels, channels),
            row_spec(block, lanes),
            whole(edges, lanes, channels),
        ],
        edge_spec(block),
        sds((edges, points, channels), BF16),
        2 * points * channels * (edges * (owned + halo) + channels),
        points * channels * edges * 2,
        [pltpu.VMEM((block, channels), F32)],
    )(slots, src, near, grid_rows, w_dst, attr, w_edge)

    pred, pred_bf, sg, zhat, rstd = call(
        functools.partial(forward_kernel, owned + halo),
        (points // block,),
        [
            slots_spec(block),
            edge_spec(block),
            whole(halo, channels),
            row_spec(block),
            whole(channels, channels),
            whole(1, channels),
            whole(fields, channels),
        ],
        [
            row_spec(block, fields),
            row_spec(block, fields),
            edge_spec(block),
            row_spec(block),
            row_spec(block, lanes),
        ],
        [
            sds((points, fields), F32),
            sds((points, fields), BF16),
            sds((edges, points, channels), BF16),
            sds((points, channels), BF16),
            sds((points, lanes), F32),
        ],
        2 * points * channels * (edges * halo + channels),
        points * channels * edges * 4,
    )(slots, pre, far, grid_rows, w_msg, gain, w_out)

    if members == 2:
        others = lax.ppermute(pred_bf, "member", [(0, 1), (1, 0)])[None]
    else:
        others = lax.all_gather(pred_bf[None], "member", axis=0, tiled=True)
    coeff = ALPHA / (members - 1) + (1.0 - ALPHA) / members

    d_z, d_sum, d_pre, far = call(
        functools.partial(backward_kernel, owned + halo, coeff),
        (points // block,),
        [
            slots_spec(block),
            row_spec(block, fields),
            pl.BlockSpec((others.shape[0], block, fields), lambda i: (0, i, 0)),
            row_spec(block, fields),
            whole(1, fields),
            whole(fields, channels),
            whole(1, channels),
            row_spec(block),
            row_spec(block, lanes),
            whole(channels, channels),
            edge_spec(block),
        ],
        [row_spec(block), row_spec(block), edge_spec(block), whole(halo, channels)],
        [
            sds((points, channels), BF16),
            sds((points, channels), BF16),
            sds((edges, points, channels), BF16),
            sds((halo, channels), BF16),
        ],
        2 * points * channels * (edges * halo + channels),
        points * channels * edges * 4,
        [pltpu.VMEM((halo, channels), F32)],
    )(slots, pred, others, target, weight, w_out, gain, zhat, rstd, w_msg, sg)
    far = lax.ppermute(far, "band", far_swap)

    near = call(
        functools.partial(rim_kernel, owned),
        (points // wide,),
        [slots_spec(wide), edge_spec(wide)],
        whole(halo, channels),
        sds((halo, channels), BF16),
        2 * points * channels * edges * halo,
        points * channels * edges * 2,
        [pltpu.VMEM((halo, channels), F32)],
    )(slots, d_pre)
    near = lax.ppermute(near, "band", near_swap)

    d_grid, own = call(
        own_grad_kernel,
        (points // wide,),
        [
            slots_spec(wide),
            edge_spec(wide),
            row_spec(wide),
            row_spec(wide),
            whole(channels, channels),
        ],
        [row_spec(wide), whole(owned, channels)],
        [sds((points, channels), BF16), sds((owned, channels), F32)],
        2 * points * channels * (edges * owned + channels),
        points * channels * edges * 2,
    )(slots, d_pre, d_z, d_sum, w_dst)

    d_mesh = call(
        mesh_kernel,
        (1,),
        [
            whole(2, halo),
            whole(halo, channels),
            whole(halo, channels),
            whole(owned, channels),
            whole(channels, channels),
        ],
        whole(owned, channels),
        sds((owned, channels), BF16),
        2 * owned * channels * (channels + 2 * halo),
        owned * channels * 8,
    )(send_near_far, near, far, own, w_src)
    return (d_grid[None], d_mesh[None])


def solution(mesh):
    placed = (
        P("member", "band", None),
        P("member", "band", None),
        P(None, None, "band"),
        P("band", None),
        P("band", None),
        P(None, "band"),
        P(),
        P(),
        P(),
        P(),
        P(),
        P(),
        P(),
    )
    return jax.shard_map(
        per_device,
        mesh=mesh,
        in_specs=placed,
        out_specs=(P("member", "band", None), P("member", "band", None)),
        check_vma=False,
    )
```

```python
import functools

import jax
import jax.numpy as jnp
from jax import lax
from jax.experimental import pallas as pl
from jax.experimental.pallas import tpu as pltpu
from jax.sharding import PartitionSpec as P

DELTA_SQ = 0.0625
ALPHA = 0.95
LN_EPS = 1e-05
F32 = jnp.float32
BF16 = jnp.bfloat16
VMEM_LIMIT = 28 * 1024 * 1024


def slope(diff):
    return diff * lax.rsqrt(diff * diff + DELTA_SQ)


def mm(left, right):
    return jnp.dot(left, right, preferred_element_type=F32)


def mm_t(left, right):
    return lax.dot_general(left, right, (((1,), (1,)), ((), ())), preferred_element_type=F32)


def column_hot(ids, base, slots):
    lanes = 128
    rows = ids.shape[1]
    column = jnp.broadcast_to((ids - base).astype(F32), (lanes, rows)).T.astype(jnp.int16)
    lane = lax.broadcasted_iota(jnp.int16, (rows, lanes), 1)
    parts = [
        jnp.where(column == lane + jnp.int16(first), BF16(1), BF16(0))
        for first in range(0, slots, lanes)
    ]
    return jnp.concatenate(parts, axis=1)


def row_hot(ids, base, slots):
    row = (ids - base).astype(jnp.int16)
    return jnp.where(
        row == lax.broadcasted_iota(jnp.int16, (slots, ids.shape[1]), 0), BF16(1), BF16(0)
    )


def row_hots(ids_ref, base, slots):
    return jnp.concatenate(
        [row_hot(ids_ref[k : k + 1, :], base, slots) for k in range(ids_ref.shape[0])], axis=1
    )


def whole(*shape):
    return pl.BlockSpec(shape, lambda *_: (0,) * len(shape))


def padded(array, dim, size):
    widths = [(0, 0)] * array.ndim
    widths[dim] = (0, size - array.shape[dim])
    return jnp.pad(array, widths)


def swap(firsts):
    return [pair for i in firsts for pair in ((i, i + 1), (i + 1, i))]


def hbm(array):
    return pltpu.with_memory_space_constraint(array, pltpu.HBM)


def in_hbm(shape, dtype=BF16):
    return pltpu.HBM(shape, dtype)


def call(body, grid, in_specs, out_specs, out_shape, flops, nbytes, scratch=(), aliases=None):
    return pl.pallas_call(
        body,
        grid=grid,
        in_specs=in_specs,
        out_specs=out_specs,
        out_shape=out_shape,
        scratch_shapes=scratch,
        input_output_aliases=aliases or {},
        compiler_params=pltpu.CompilerParams(vmem_limit_bytes=VMEM_LIMIT),
        cost_estimate=pl.CostEstimate(flops=flops, bytes_accessed=nbytes, transcendentals=0),
    )


def near_far(send_ref):
    odd = lax.axis_index("band") % 2
    low, high = send_ref[0:1, :], send_ref[1:2, :]
    return jnp.where(odd == 1, low, high), jnp.where(odd == 1, high, low)


def send_kernel(mesh_ref, w_src_ref, send_ref, src_ref, near_ref, far_ref):
    src = mm(mesh_ref[...], w_src_ref[...]).astype(BF16)
    src_ref[...] = src
    owned = src.shape[0]
    near, far = near_far(send_ref)
    far_ref[...] = mm(column_hot(far, 0, owned), src).astype(BF16)
    near_ref[...] = mm(column_hot(near, 0, owned), src).astype(BF16)


def own_kernel(
    slots_ref, src_ref, near_ref, grid_ref, w_dst_ref, attr_ref, w_edge_ref, pre_ref, dst_ref, embed_ref
):
    edges, lanes, channels = embed_ref.shape
    feats = w_edge_ref.shape[0]
    rows = grid_ref.shape[0]

    @pl.when(pl.program_id(0) == 0)
    def _():
        row = lax.broadcasted_iota(jnp.int32, (lanes, channels), 0)
        w_edge = w_edge_ref[...].astype(F32)
        for k in range(edges):
            spread = jnp.zeros((lanes, channels), F32)
            for e in range(feats):
                spread = jnp.where(row == e * edges + k, w_edge[e : e + 1, :], spread)
            embed_ref[k] = spread.astype(BF16)

    owned = src_ref.shape[0]
    near = near_ref.shape[0]
    dst_ref[...] = mm(grid_ref[...], w_dst_ref[...])
    attr = attr_ref[...].astype(F32)
    attr = jnp.concatenate([attr, jnp.zeros((lanes - attr.shape[0], rows), F32)], axis=0)
    attr = attr.T.astype(BF16)
    for k in range(edges):
        ids = slots_ref[k : k + 1, :]
        picked = mm(column_hot(ids, 0, owned), src_ref[...])
        picked = picked + mm(column_hot(ids, owned, near), near_ref[...])
        embed = mm(attr, embed_ref[k])
        pre_ref[k] = (picked + embed + dst_ref[...]).astype(BF16)


def forward_kernel(
    base,
    slots_ref,
    pre_ref,
    far_ref,
    grid_ref,
    w_msg_ref,
    gain_ref,
    w_out_ref,
    pred_ref,
    pred_bf_ref,
    sg_ref,
    zhat_ref,
    rstd_ref,
):
    half = BF16(0.5)
    acts = []
    for k in range(slots_ref.shape[0]):
        hot = column_hot(slots_ref[k : k + 1, :], base, far_ref.shape[0])
        pre = pre_ref[k] + mm(hot, far_ref[...]).astype(BF16)
        sigma = half + half * jnp.tanh(half * pre)
        act = pre * sigma
        acts.append(act)
        sg_ref[k] = sigma + (act - act * sigma)
    while len(acts) > 1:
        acts = [sum(acts[i : i + 2][1:], acts[i]) for i in range(0, len(acts), 2)]
    z = grid_ref[...].astype(F32) + mm(acts[0], w_msg_ref[...])
    centre = z - jnp.mean(z, axis=1, keepdims=True)
    rstd = lax.rsqrt(jnp.mean(centre * centre, axis=1, keepdims=True) + LN_EPS)
    zhat = centre * rstd
    pred = mm_t(w_out_ref[...], (zhat * gain_ref[...]).astype(BF16))
    pred_ref[...] = pred
    pred_bf_ref[...] = pred.astype(BF16)
    zhat_ref[...] = zhat.astype(BF16)
    rstd_ref[...] = jnp.broadcast_to(rstd, rstd_ref.shape)


def backward_kernel(
    base,
    coeff,
    slots_ref,
    pred_ref,
    others_ref,
    target_ref,
    weight_ref,
    w_out_ref,
    gain_ref,
    zhat_ref,
    rstd_ref,
    w_msg_ref,
    sg_ref,
    *refs,
):
    dz_ref, dsum_ref, dpre_ref, far_ref, far_acc = refs[-5:]
    step = pl.program_id(0)

    @pl.when(step == 0)
    def _():
        far_acc[...] = refs[0][...] if len(refs) > 5 else jnp.zeros_like(far_acc)

    pred = pred_ref[...]
    spread = jnp.zeros_like(pred)
    for other in range(others_ref.shape[0]):
        spread = spread + slope(pred - others_ref[other].astype(F32))
    d_pred = slope(pred - target_ref[...]) - coeff * spread
    d_pred = (weight_ref[...] * d_pred.T).astype(BF16)
    scaled = mm(d_pred, w_out_ref[...]) * gain_ref[...]
    zhat = zhat_ref[...].astype(F32)
    d_z = rstd_ref[:, :1] * (
        scaled
        - jnp.mean(scaled, axis=1, keepdims=True)
        - zhat * jnp.mean(scaled * zhat, axis=1, keepdims=True)
    )
    d_zb = d_z.astype(BF16)
    dz_ref[...] = d_zb
    d_act = mm_t(d_zb, w_msg_ref[...])
    d_act_b = d_act.astype(BF16)
    total = jnp.zeros(d_act.shape, F32)
    parts = []
    for k in range(slots_ref.shape[0]):
        d_pre = d_act_b * sg_ref[k]
        total = total + d_pre.astype(F32)
        dpre_ref[k] = d_pre
        parts.append(d_pre)
    dsum_ref[...] = total.astype(BF16)
    hot = row_hots(slots_ref, base, far_ref.shape[0])
    far_acc[...] += mm(hot, jnp.concatenate(parts, axis=0))

    @pl.when(step == pl.num_programs(0) - 1)
    def _():
        far_ref[...] = far_acc[...].astype(far_ref.dtype)


def own_grad_kernel(
    slots_ref, dpre_ref, dz_ref, dsum_ref, w_dst_ref, grid_out_ref, own_ref, near_ref, near_acc
):
    step = pl.program_id(0)

    @pl.when(step == 0)
    def _():
        own_ref[...] = jnp.zeros_like(own_ref)
        near_acc[...] = jnp.zeros_like(near_acc)

    edges, rows, channels = dpre_ref.shape
    owned = own_ref.shape[0]
    d_pre = dpre_ref[...].reshape(edges * rows, channels)
    near_acc[...] += mm(row_hots(slots_ref, owned, near_acc.shape[0]), d_pre)
    own_ref[...] += mm(row_hots(slots_ref, 0, owned), d_pre)
    grid_out_ref[...] = (dz_ref[...].astype(F32) + mm_t(dsum_ref[...], w_dst_ref[...])).astype(BF16)

    @pl.when(step == pl.num_programs(0) - 1)
    def _():
        near_ref[...] = near_acc[...].astype(BF16)


def mesh_kernel(send_ref, near_ref, far_ref, own_ref, w_src_ref, out_ref):
    owned = own_ref.shape[0]
    near, far = near_far(send_ref)
    total = own_ref[...] + mm(row_hot(near, 0, owned), near_ref[...])
    total = total + mm(row_hot(far, 0, owned), far_ref[...])
    out_ref[...] = mm_t(total.astype(BF16), w_src_ref[...]).astype(BF16)


def per_device(
    grid_latent,
    mesh_latent,
    edge_attr,
    neighbours,
    send_rows,
    target,
    field_weight,
    w_src,
    w_dst,
    w_edge,
    w_msg,
    ln_gain,
    w_out,
):
    grid_rows = grid_latent[0]
    mesh_rows = mesh_latent[0]
    points, channels = grid_rows.shape
    owned = mesh_rows.shape[0]
    halo = send_rows.shape[1]
    edges = neighbours.shape[1]
    feats = w_edge.shape[0]
    lanes = 128
    fields = -(-w_out.shape[1] // lanes) * lanes
    block = min(points, 256)
    wide = min(points, 512)
    sds = jax.ShapeDtypeStruct
    members = lax.axis_size("member")
    bands = lax.axis_size("band")
    near_swap = swap(range(0, bands - 1, 2))
    far_swap = swap(range(1, bands - 1, 2))
    even = lax.axis_index("band") % 2 == 0
    slots = neighbours.T
    swapped = jnp.where(slots < owned, slots, jnp.where(slots < owned + halo, slots + halo, slots - halo))
    slots = jnp.where(even, swapped, slots)

    src, near, far = call(
        send_kernel,
        (1,),
        [whole(owned, channels), whole(channels, channels), whole(2, halo)],
        [whole(owned, channels), whole(halo, channels), whole(halo, channels)],
        [in_hbm((owned, channels)), sds((halo, channels), BF16), sds((halo, channels), BF16)],
        2 * owned * channels * (channels + 2 * halo),
        4 * owned * channels * 2,
    )(hbm(mesh_rows), hbm(w_src), hbm(send_rows))
    far = lax.ppermute(far, "band", far_swap)
    near = lax.ppermute(near, "band", near_swap)

    def slots_spec(rows, first=0):
        return pl.BlockSpec((edges, rows), lambda i: (0, i + first))

    def row_spec(rows, width=channels, first=0):
        return pl.BlockSpec((rows, width), lambda i: (i + first, 0))

    def edge_spec(rows, first=0):
        return pl.BlockSpec((edges, rows, channels), lambda i: (0, i + first, 0))

    def field_spec(rows, first=0):
        return pl.BlockSpec((fields, rows), lambda i: (0, i + first))

    gain = hbm(ln_gain[None, :])
    attr = edge_attr.reshape(feats * edges, points)
    w_out = padded(w_out.T, 0, fields)
    target = padded(target, 0, fields)
    weight = padded(field_weight[None, :], 1, fields)
    slots = hbm(slots)

    pre = call(
        own_kernel,
        (points // block,),
        [
            slots_spec(block),
            whole(owned, channels),
            whole(halo, channels),
            row_spec(block),
            whole(channels, channels),
            pl.BlockSpec((feats * edges, block), lambda i: (0, i)),
            whole(feats, channels),
        ],
        edge_spec(block),
        in_hbm((edges, points, channels)),
        2 * points * channels * (edges * (owned + halo) + channels),
        points * channels * edges * 2,
        [pltpu.VMEM((block, channels), F32), pltpu.VMEM((edges, lanes, channels), BF16)],
    )(slots, hbm(src), near, hbm(grid_rows), hbm(w_dst), hbm(attr), hbm(w_edge))

    chunks = 2
    part = points // chunks
    steps = part // block
    ahead = []
    for c in range(chunks):
        pred, pred_bf, sg, zhat, rstd = call(
            functools.partial(forward_kernel, owned + halo),
            (steps,),
            [
                slots_spec(block, c * steps),
                edge_spec(block, c * steps),
                whole(halo, channels),
                row_spec(block, channels, c * steps),
                whole(channels, channels),
                whole(1, channels),
                whole(fields, channels),
            ],
            [
                field_spec(block),
                field_spec(block),
                edge_spec(block),
                row_spec(block),
                row_spec(block, lanes),
            ],
            [
                in_hbm((fields, part), F32),
                sds((fields, part), BF16),
                in_hbm((edges, part, channels)),
                in_hbm((part, channels)),
                in_hbm((part, lanes), F32),
            ],
            2 * part * channels * (edges * halo + channels),
            part * channels * edges * 4,
        )(slots, hbm(pre), far, hbm(grid_rows), hbm(w_msg), gain, hbm(w_out))
        if members == 2:
            others = lax.ppermute(pred_bf, "member", [(0, 1), (1, 0)])[None]
        else:
            others = lax.all_gather(pred_bf[None], "member", axis=0, tiled=True)
        ahead.append((hbm(pred), others, hbm(sg), hbm(zhat), hbm(rstd)))

    coeff = ALPHA / (members - 1) + (1.0 - ALPHA) / members
    done = ()
    for c, (pred, others, sg, zhat, rstd) in enumerate(ahead):
        last = c == chunks - 1
        anywhere = [pl.BlockSpec(memory_space=pltpu.HBM)] * 3 if done else []
        done = call(
            functools.partial(backward_kernel, owned + halo, coeff),
            (steps,),
            [
                slots_spec(block, c * steps),
                field_spec(block),
                pl.BlockSpec((others.shape[0], fields, block), lambda i: (0, 0, i)),
                field_spec(block, c * steps),
                whole(1, fields),
                whole(fields, channels),
                whole(1, channels),
                row_spec(block),
                row_spec(block, lanes),
                whole(channels, channels),
                edge_spec(block),
            ]
            + ([whole(halo, channels)] if done else [])
            + anywhere,
            [
                row_spec(block, channels, c * steps),
                row_spec(block, channels, c * steps),
                edge_spec(block, c * steps),
                whole(halo, channels),
            ],
            [
                in_hbm((points, channels)),
                in_hbm((points, channels)),
                in_hbm((edges, points, channels)),
                sds((halo, channels), BF16 if last else F32),
            ],
            2 * part * channels * (edges * halo + channels),
            part * channels * edges * 4,
            [pltpu.VMEM((halo, channels), F32)],
            {12: 0, 13: 1, 14: 2} if done else None,
        )(
            slots, pred, others, hbm(target), hbm(weight), hbm(w_out), gain, zhat, rstd,
            hbm(w_msg), sg, *(done[3:] + done[:3] if done else ()),
        )
        done = tuple(done)
    d_z, d_sum, d_pre, far = done
    far = lax.ppermute(far, "band", far_swap)

    d_grid, own, near = call(
        own_grad_kernel,
        (points // wide,),
        [
            slots_spec(wide),
            edge_spec(wide),
            row_spec(wide),
            row_spec(wide),
            whole(channels, channels),
        ],
        [row_spec(wide), whole(owned, channels), whole(halo, channels)],
        [
            in_hbm((points, channels)),
            in_hbm((owned, channels), F32),
            sds((halo, channels), BF16),
        ],
        2 * points * channels * (edges * (owned + halo) + channels),
        points * channels * edges * 2,
        [pltpu.VMEM((halo, channels), F32)],
    )(slots, hbm(d_pre), hbm(d_z), hbm(d_sum), hbm(w_dst))
    near = lax.ppermute(near, "band", near_swap)

    d_mesh = call(
        mesh_kernel,
        (1,),
        [
            whole(2, halo),
            whole(halo, channels),
            whole(halo, channels),
            whole(owned, channels),
            whole(channels, channels),
        ],
        whole(owned, channels),
        in_hbm((owned, channels)),
        2 * owned * channels * (channels + 2 * halo),
        owned * channels * 8,
    )(hbm(send_rows), near, far, hbm(own), hbm(w_src))
    return (d_grid[None], d_mesh[None])


def solution(mesh):
    placed = (
        P("member", "band", None),
        P("member", "band", None),
        P(None, None, "band"),
        P("band", None),
        P("band", None),
        P(None, "band"),
        P(),
        P(),
        P(),
        P(),
        P(),
        P(),
        P(),
    )
    return jax.shard_map(
        per_device,
        mesh=mesh,
        in_specs=placed,
        out_specs=(P("member", "band", None), P("member", "band", None)),
        check_vma=False,
    )
```

```python
import functools

import jax
import jax.numpy as jnp
from jax import lax
from jax.experimental import pallas as pl
from jax.experimental.pallas import tpu as pltpu
from jax.sharding import PartitionSpec as P

DELTA_SQ = 0.0625
ALPHA = 0.95
LN_EPS = 1e-05
F32 = jnp.float32
BF16 = jnp.bfloat16
VMEM_LIMIT = 28 * 1024 * 1024


def slope(diff):
    return diff * lax.rsqrt(diff * diff + DELTA_SQ)


def mm(left, right):
    return jnp.dot(left, right, preferred_element_type=F32)


def mm_t(left, right):
    return lax.dot_general(left, right, (((1,), (1,)), ((), ())), preferred_element_type=F32)


def column_hot(ids, base, slots):
    lanes = 128
    rows = ids.shape[1]
    column = jnp.broadcast_to((ids - base).astype(F32), (lanes, rows)).T.astype(jnp.int16)
    lane = lax.broadcasted_iota(jnp.int16, (rows, lanes), 1)
    parts = [
        jnp.where(column == lane + jnp.int16(first), BF16(1), BF16(0))
        for first in range(0, slots, lanes)
    ]
    return jnp.concatenate(parts, axis=1)


def row_hot(ids, base, slots):
    row = (ids - base).astype(jnp.int16)
    return jnp.where(
        row == lax.broadcasted_iota(jnp.int16, (slots, ids.shape[1]), 0), BF16(1), BF16(0)
    )


def row_hots(ids_ref, base, slots):
    return jnp.concatenate(
        [row_hot(ids_ref[k : k + 1, :], base, slots) for k in range(ids_ref.shape[0])], axis=1
    )


def whole(*shape):
    return pl.BlockSpec(shape, lambda *_: (0,) * len(shape))


def swap(firsts):
    return [pair for i in firsts for pair in ((i, i + 1), (i + 1, i))]


def hbm(array):
    return pltpu.with_memory_space_constraint(array, pltpu.HBM)


def call(body, grid, in_specs, out_specs, out_shape, flops, nbytes, scratch=()):
    return pl.pallas_call(
        body,
        grid=grid,
        in_specs=in_specs,
        out_specs=out_specs,
        out_shape=out_shape,
        scratch_shapes=scratch,
        compiler_params=pltpu.CompilerParams(vmem_limit_bytes=VMEM_LIMIT),
        cost_estimate=pl.CostEstimate(flops=flops, bytes_accessed=nbytes, transcendentals=0),
    )


def near_far(low, high):
    odd = lax.axis_index("band") % 2 == 1
    return jnp.where(odd, low, high), jnp.where(odd, high, low)


def rim_bases(owned, halo):
    return near_far(owned, owned + halo)


def rows_to(array, rows):
    array = array.astype(F32)
    return jnp.concatenate([array, jnp.zeros((rows - array.shape[0], array.shape[1]), F32)], axis=0)


def send_kernel(mesh_ref, w_src_ref, send_ref, src_ref, near_ref, far_ref):
    src = mm(mesh_ref[...], w_src_ref[...]).astype(BF16)
    src_ref[...] = src
    owned = src.shape[0]
    near, far = near_far(send_ref[0:1, :], send_ref[1:2, :])
    far_ref[...] = mm(column_hot(far, 0, owned), src).astype(BF16)
    near_ref[...] = mm(column_hot(near, 0, owned), src).astype(BF16)


def own_kernel(
    slots_ref, src_ref, near_ref, grid_ref, w_dst_ref, attr_ref, w_edge_ref, pre_ref, dst_ref, embed_ref,
    attr_f32,
):
    edges, lanes, channels = embed_ref.shape
    feats = w_edge_ref.shape[0]
    rows = grid_ref.shape[0]

    @pl.when(pl.program_id(0) == 0)
    def _():
        row = lax.broadcasted_iota(jnp.int32, (lanes, channels), 0)
        w_edge = w_edge_ref[...].astype(F32)
        for k in range(edges):
            spread = jnp.zeros((lanes, channels), F32)
            for e in range(feats):
                spread = jnp.where(row == e * edges + k, w_edge[e : e + 1, :], spread)
            embed_ref[k] = spread.astype(BF16)

    owned = src_ref.shape[0]
    near = near_ref.shape[0]
    base = rim_bases(owned, near)[0]
    dst_ref[...] = mm(grid_ref[...], w_dst_ref[...])
    for e in range(feats):
        attr_f32[e * edges : (e + 1) * edges, :] = attr_ref[e].astype(F32)
    attr = rows_to(attr_f32[...], lanes).T.astype(BF16)
    for k in range(edges):
        ids = slots_ref[k : k + 1, :]
        picked = mm(column_hot(ids, 0, owned), src_ref[...])
        picked = picked + mm(column_hot(ids, base, near), near_ref[...])
        embed = mm(attr, embed_ref[k])
        pre_ref[k] = (picked + embed + dst_ref[...]).astype(BF16)


def forward_kernel(
    owned,
    fields,
    slots_ref,
    pre_ref,
    far_ref,
    grid_ref,
    w_msg_ref,
    gain_ref,
    w_out_ref,
    pred_ref,
    pred_bf_ref,
    sg_ref,
    zhat_ref,
    rstd_ref,
):
    half = BF16(0.5)
    halo = far_ref.shape[0]
    base = rim_bases(owned, halo)[1]
    acts = []
    for k in range(slots_ref.shape[0]):
        hot = column_hot(slots_ref[k : k + 1, :], base, halo)
        pre = pre_ref[k] + mm(hot, far_ref[...]).astype(BF16)
        sigma = half + half * jnp.tanh(half * pre)
        act = pre * sigma
        acts.append(act)
        sg_ref[k] = sigma + (act - act * sigma)
    while len(acts) > 1:
        acts = [sum(acts[i : i + 2][1:], acts[i]) for i in range(0, len(acts), 2)]
    z = grid_ref[...].astype(F32) + mm(acts[0], w_msg_ref[...])
    centre = z - jnp.mean(z, axis=1, keepdims=True)
    rstd = lax.rsqrt(jnp.mean(centre * centre, axis=1, keepdims=True) + LN_EPS)
    zhat = centre * rstd
    w_out = rows_to(w_out_ref[...], fields).astype(BF16)
    pred = mm_t(w_out, (zhat * gain_ref[...]).astype(BF16))
    pred_ref[...] = pred
    pred_bf_ref[...] = pred.astype(BF16)
    zhat_ref[...] = zhat.astype(BF16)
    rstd_ref[...] = jnp.broadcast_to(rstd, rstd_ref.shape)


def backward_kernel(
    owned,
    coeff,
    slots_ref,
    pred_ref,
    others_ref,
    target_ref,
    weight_ref,
    w_out_ref,
    gain_ref,
    zhat_ref,
    rstd_ref,
    w_msg_ref,
    sg_ref,
    *refs,
):
    dz_ref, dsum_ref, dpre_ref, near_ref, far_ref, near_acc, far_acc = refs[-7:]
    step = pl.program_id(0)

    @pl.when(step == 0)
    def _():
        near_acc[...] = refs[0][...] if len(refs) > 7 else jnp.zeros_like(near_acc)
        far_acc[...] = refs[1][...] if len(refs) > 7 else jnp.zeros_like(far_acc)

    halo = far_ref.shape[0]
    fields = pred_ref.shape[0]
    pred = pred_ref[...]
    spread = jnp.zeros_like(pred)
    for other in range(others_ref.shape[0]):
        spread = spread + slope(pred - others_ref[other].astype(F32))
    d_pred = slope(pred - rows_to(target_ref[...], fields)) - coeff * spread
    weight = weight_ref[...]
    weight = jnp.concatenate([weight, jnp.zeros((1, fields - weight.shape[1]), F32)], axis=1)
    d_pred = (weight * d_pred.T).astype(BF16)
    scaled = mm(d_pred, rows_to(w_out_ref[...], fields).astype(BF16)) * gain_ref[...]
    zhat = zhat_ref[...].astype(F32)
    d_z = rstd_ref[:, :1] * (
        scaled
        - jnp.mean(scaled, axis=1, keepdims=True)
        - zhat * jnp.mean(scaled * zhat, axis=1, keepdims=True)
    )
    d_zb = d_z.astype(BF16)
    dz_ref[...] = d_zb
    d_act = mm_t(d_zb, w_msg_ref[...])
    d_act_b = d_act.astype(BF16)
    total = jnp.zeros(d_act.shape, F32)
    parts = []
    for k in range(slots_ref.shape[0]):
        d_pre = d_act_b * sg_ref[k]
        total = total + d_pre.astype(F32)
        dpre_ref[k] = d_pre
        parts.append(d_pre)
    dsum_ref[...] = total.astype(BF16)
    d_pre = jnp.concatenate(parts, axis=0)
    near, far = rim_bases(owned, halo)
    far_acc[...] += mm(row_hots(slots_ref, far, halo), d_pre)
    near_acc[...] += mm(row_hots(slots_ref, near, halo), d_pre)

    @pl.when(step == pl.num_programs(0) - 1)
    def _():
        near_ref[...] = near_acc[...].astype(near_ref.dtype)
        far_ref[...] = far_acc[...].astype(far_ref.dtype)


def own_grad_kernel(chunks, slots_ref, w_dst_ref, *refs):
    grid_out_ref, own_ref = refs[-2:]
    step = pl.program_id(0)
    owned = own_ref.shape[0]

    @pl.when(step == 0)
    def _():
        own_ref[...] = jnp.zeros_like(own_ref)

    for c in range(chunks):
        dz_ref, dsum_ref, dpre_ref = refs[3 * c : 3 * c + 3]

        @pl.when(step == c)
        def _():
            edges, rows, channels = dpre_ref.shape
            d_pre = dpre_ref[...].reshape(edges * rows, channels)
            own_ref[...] += mm(row_hots(slots_ref, 0, owned), d_pre)
            d_grid = dz_ref[...].astype(F32) + mm_t(dsum_ref[...], w_dst_ref[...])
            grid_out_ref[...] = d_grid.astype(BF16)


def mesh_kernel(send_ref, near_ref, far_ref, own_ref, w_src_ref, out_ref):
    owned = own_ref.shape[0]
    near, far = near_far(send_ref[0:1, :], send_ref[1:2, :])
    total = own_ref[...] + mm(row_hot(near, 0, owned), near_ref[...])
    total = total + mm(row_hot(far, 0, owned), far_ref[...])
    out_ref[...] = mm_t(total.astype(BF16), w_src_ref[...]).astype(BF16)


def per_device(
    grid_latent,
    mesh_latent,
    edge_attr,
    neighbours,
    send_rows,
    target,
    field_weight,
    w_src,
    w_dst,
    w_edge,
    w_msg,
    ln_gain,
    w_out,
):
    grid_rows = grid_latent[0]
    mesh_rows = mesh_latent[0]
    points, channels = grid_rows.shape
    owned = mesh_rows.shape[0]
    halo = send_rows.shape[1]
    edges = neighbours.shape[1]
    feats = w_edge.shape[0]
    lanes = 128
    fields = -(-w_out.shape[1] // lanes) * lanes
    block = min(points, 256)
    sds = jax.ShapeDtypeStruct
    members = lax.axis_size("member")
    bands = lax.axis_size("band")
    near_swap = swap(range(0, bands - 1, 2))
    far_swap = swap(range(1, bands - 1, 2))
    slots = neighbours.T
    gain = ln_gain[None, :]
    w_out = w_out.T
    weight = field_weight[None, :]

    src, near, far = call(
        send_kernel,
        (1,),
        [whole(owned, channels), whole(channels, channels), whole(2, halo)],
        [whole(owned, channels), whole(halo, channels), whole(halo, channels)],
        [sds((owned, channels), BF16), sds((halo, channels), BF16), sds((halo, channels), BF16)],
        2 * owned * channels * (channels + 2 * halo),
        4 * owned * channels * 2,
    )(hbm(mesh_rows), hbm(w_src), hbm(send_rows))
    far = lax.ppermute(far, "band", far_swap)
    near = lax.ppermute(near, "band", near_swap)

    def slots_spec(rows, first=0):
        return pl.BlockSpec((edges, rows), lambda i: (0, i + first))

    def row_spec(rows, width=channels, first=0):
        return pl.BlockSpec((rows, width), lambda i: (i + first, 0))

    def edge_spec(rows, first=0):
        return pl.BlockSpec((edges, rows, channels), lambda i: (0, i + first, 0))

    def field_spec(count, rows, first=0):
        return pl.BlockSpec((count, rows), lambda i: (0, i + first))

    pre = call(
        own_kernel,
        (points // block,),
        [
            slots_spec(block),
            whole(owned, channels),
            whole(halo, channels),
            row_spec(block),
            whole(channels, channels),
            pl.BlockSpec((feats, edges, block), lambda i: (0, 0, i)),
            whole(feats, channels),
        ],
        edge_spec(block),
        sds((edges, points, channels), BF16),
        2 * points * channels * (edges * (owned + halo) + channels),
        points * channels * edges * 2,
        [
            pltpu.VMEM((block, channels), F32),
            pltpu.VMEM((edges, lanes, channels), BF16),
            pltpu.VMEM((feats * edges, block), F32),
        ],
    )(slots, src, near, grid_rows, w_dst, edge_attr, w_edge)

    chunks = 2
    part = points // chunks
    steps = part // block
    ahead = []
    for c in range(chunks):
        pred, pred_bf, sg, zhat, rstd = call(
            functools.partial(forward_kernel, owned, fields),
            (steps,),
            [
                slots_spec(block, c * steps),
                edge_spec(block, c * steps),
                whole(halo, channels),
                row_spec(block, channels, c * steps),
                whole(channels, channels),
                whole(1, channels),
                whole(*w_out.shape),
            ],
            [
                field_spec(fields, block),
                field_spec(fields, block),
                edge_spec(block),
                row_spec(block),
                row_spec(block, lanes),
            ],
            [
                sds((fields, part), F32),
                sds((fields, part), BF16),
                sds((edges, part, channels), BF16),
                sds((part, channels), BF16),
                sds((part, lanes), F32),
            ],
            2 * part * channels * (edges * halo + channels),
            part * channels * edges * 4,
        )(slots, pre, far, grid_rows, w_msg, gain, w_out)
        if members == 2:
            others = lax.ppermute(pred_bf, "member", [(0, 1), (1, 0)])[None]
        else:
            others = lax.all_gather(pred_bf[None], "member", axis=0, tiled=True)
        ahead.append((pred, others, sg, zhat, rstd))

    coeff = ALPHA / (members - 1) + (1.0 - ALPHA) / members
    rims = ()
    behind = []
    for c, (pred, others, sg, zhat, rstd) in enumerate(ahead):
        rim_type = BF16 if c == chunks - 1 else F32
        d_z, d_sum, d_pre, *rims = call(
            functools.partial(backward_kernel, owned, coeff),
            (steps,),
            [
                slots_spec(block, c * steps),
                field_spec(fields, block),
                pl.BlockSpec((others.shape[0], fields, block), lambda i: (0, 0, i)),
                field_spec(target.shape[0], block, c * steps),
                whole(*weight.shape),
                whole(*w_out.shape),
                whole(1, channels),
                row_spec(block),
                row_spec(block, lanes),
                whole(channels, channels),
                edge_spec(block),
            ]
            + [whole(halo, channels)] * len(rims),
            [
                row_spec(block),
                row_spec(block),
                edge_spec(block),
                whole(halo, channels),
                whole(halo, channels),
            ],
            [
                sds((part, channels), BF16),
                sds((part, channels), BF16),
                sds((edges, part, channels), BF16),
                sds((halo, channels), rim_type),
                sds((halo, channels), rim_type),
            ],
            2 * part * channels * (edges * 2 * halo + channels),
            part * channels * edges * 4,
            [pltpu.VMEM((halo, channels), F32), pltpu.VMEM((halo, channels), F32)],
        )(slots, pred, others, target, weight, w_out, gain, zhat, rstd, w_msg, sg, *rims)
        behind += [d_z, d_sum, d_pre]
    near, far = rims
    far = lax.ppermute(far, "band", far_swap)
    near = lax.ppermute(near, "band", near_swap)

    d_grid, own = call(
        functools.partial(own_grad_kernel, chunks),
        (chunks,),
        [slots_spec(part), whole(channels, channels)]
        + [whole(part, channels), whole(part, channels), whole(edges, part, channels)] * chunks,
        [row_spec(part), whole(owned, channels)],
        [sds((points, channels), BF16), sds((owned, channels), F32)],
        2 * points * channels * (edges * owned + channels),
        points * channels * edges * 2,
    )(slots, w_dst, *behind)

    d_mesh = call(
        mesh_kernel,
        (1,),
        [
            whole(2, halo),
            whole(halo, channels),
            whole(halo, channels),
            whole(owned, channels),
            whole(channels, channels),
        ],
        whole(owned, channels),
        sds((owned, channels), BF16),
        2 * owned * channels * (channels + 2 * halo),
        owned * channels * 8,
    )(send_rows, near, far, own, w_src)
    return (d_grid[None], d_mesh[None])


def solution(mesh):
    placed = (
        P("member", "band", None),
        P("member", "band", None),
        P(None, None, "band"),
        P("band", None),
        P("band", None),
        P(None, "band"),
        P(),
        P(),
        P(),
        P(),
        P(),
        P(),
        P(),
    )
    return jax.shard_map(
        per_device,
        mesh=mesh,
        in_specs=placed,
        out_specs=(P("member", "band", None), P("member", "band", None)),
        check_vma=False,
    )
```

```python
import functools

import jax
import jax.numpy as jnp
from jax import lax
from jax.experimental import pallas as pl
from jax.experimental.pallas import tpu as pltpu
from jax.sharding import PartitionSpec as P

DELTA_SQ = 0.0625
ALPHA = 0.95
LN_EPS = 1e-05
F32 = jnp.float32
BF16 = jnp.bfloat16
VMEM_LIMIT = 28 * 1024 * 1024


def slope(diff):
    return diff * lax.rsqrt(diff * diff + DELTA_SQ)


def mm(left, right):
    return jnp.dot(left, right, preferred_element_type=F32)


def mm_t(left, right):
    return lax.dot_general(left, right, (((1,), (1,)), ((), ())), preferred_element_type=F32)


def column_hot(ids, base, slots):
    lanes = 128
    rows = ids.shape[1]
    column = jnp.broadcast_to((ids - base).astype(F32), (lanes, rows)).T.astype(jnp.int16)
    lane = lax.broadcasted_iota(jnp.int16, (rows, lanes), 1)
    parts = [
        jnp.where(column == lane + jnp.int16(first), BF16(1), BF16(0))
        for first in range(0, slots, lanes)
    ]
    return jnp.concatenate(parts, axis=1)


def row_hot(ids, base, slots):
    row = (ids - base).astype(jnp.int16)
    return jnp.where(
        row == lax.broadcasted_iota(jnp.int16, (slots, ids.shape[1]), 0), BF16(1), BF16(0)
    )


def row_hots(ids, base, slots):
    return jnp.concatenate(
        [row_hot(ids[k : k + 1, :], base, slots) for k in range(ids.shape[0])], axis=1
    )


def swap(firsts):
    return [pair for i in firsts for pair in ((i, i + 1), (i + 1, i))]


def hbm(array):
    return pltpu.with_memory_space_constraint(array, pltpu.HBM)


def call(body, places, out_places, out_shape, flops, nbytes, scratch=()):
    def specs(memories):
        return [pl.BlockSpec(memory_space=memory) for memory in memories]

    return pl.pallas_call(
        body,
        in_specs=specs(places),
        out_specs=specs(out_places),
        out_shape=out_shape,
        scratch_shapes=scratch,
        compiler_params=pltpu.CompilerParams(vmem_limit_bytes=VMEM_LIMIT),
        cost_estimate=pl.CostEstimate(flops=flops, bytes_accessed=nbytes, transcendentals=0),
    )


def near_far(low, high):
    odd = lax.axis_index("band") % 2 == 1
    return jnp.where(odd, low, high), jnp.where(odd, high, low)


def rim_bases(owned, halo):
    return near_far(owned, owned + halo)


def rows_to(array, rows):
    array = array.astype(F32)
    return jnp.concatenate([array, jnp.zeros((rows - array.shape[0], array.shape[1]), F32)], axis=0)


def pieces(rows, size):
    return [slice(first, first + size) for first in range(0, rows, size)]


def send_kernel(
    mesh_hbm, w_src_hbm, send_hbm, src_ref, near_ref, far_ref, mesh_ref, w_src_ref, send_ref, sems
):
    owned = src_ref.shape[0]
    parts = pieces(owned, owned // 4)
    weights = pltpu.make_async_copy(w_src_hbm, w_src_ref, sems.at[0])
    lists = pltpu.make_async_copy(send_hbm, send_ref, sems.at[1])
    lists.start()
    weights.start()
    loads = []
    for i, part in enumerate(parts):
        loads.append(pltpu.make_async_copy(mesh_hbm.at[part], mesh_ref.at[part], sems.at[2 + i]))
        loads[-1].start()
    lists.wait()
    near, far = near_far(send_ref[0:1, :], send_ref[1:2, :])
    far_hot = column_hot(far, 0, owned)
    near_hot = column_hot(near, 0, owned)
    weights.wait()
    for load, part in zip(loads, parts):
        load.wait()
        src_ref[part] = mm(mesh_ref[part], w_src_ref[...]).astype(BF16)
    far_ref[...] = mm(far_hot, src_ref[...]).astype(BF16)
    near_ref[...] = mm(near_hot, src_ref[...]).astype(BF16)


def own_kernel(
    block,
    slots_ref,
    src_ref,
    near_ref,
    grid_ref,
    w_dst_ref,
    attr_ref,
    w_edge_ref,
    pre_ref,
    dst_ref,
    embed_ref,
    attr_f32,
):
    edges, lanes, channels = embed_ref.shape
    feats = w_edge_ref.shape[0]
    row = lax.broadcasted_iota(jnp.int32, (lanes, channels), 0)
    w_edge = w_edge_ref[...].astype(F32)
    for k in range(edges):
        spread = jnp.zeros((lanes, channels), F32)
        for e in range(feats):
            spread = jnp.where(row == e * edges + k, w_edge[e : e + 1, :], spread)
        embed_ref[k] = spread.astype(BF16)
    for e in range(feats):
        attr_f32[e * edges : (e + 1) * edges, :] = attr_ref[e].astype(F32)
    owned = src_ref.shape[0]
    halo = near_ref.shape[0]
    base = rim_bases(owned, halo)[0]
    for at, rows in enumerate(pieces(grid_ref.shape[0], block)):
        dst_ref[at] = mm(grid_ref[rows, :], w_dst_ref[...])
        attr = rows_to(attr_f32[:, rows], lanes).T.astype(BF16)
        for k in range(edges):
            ids = slots_ref[k : k + 1, rows]
            picked = mm(column_hot(ids, 0, owned), src_ref[...])
            picked = picked + mm(column_hot(ids, base, halo), near_ref[...])
            embed = mm(attr, embed_ref[k])
            pre_ref[k, rows, :] = (picked + embed + dst_ref[at]).astype(BF16)


def forward_kernel(
    first,
    block,
    owned,
    fields,
    slots_ref,
    pre_ref,
    far_ref,
    grid_ref,
    w_msg_ref,
    gain_ref,
    w_out_ref,
    pred_ref,
    pred_bf_ref,
    sg_ref,
    zhat_ref,
    rstd_ref,
):
    half = BF16(0.5)
    halo = far_ref.shape[0]
    base = rim_bases(owned, halo)[1]
    w_out = rows_to(w_out_ref[...], fields).astype(BF16)
    for rows in pieces(zhat_ref.shape[0], block):
        source = slice(first + rows.start, first + rows.stop)
        acts = []
        for k in range(slots_ref.shape[0]):
            hot = column_hot(slots_ref[k : k + 1, source], base, halo)
            pre = pre_ref[k, source, :] + mm(hot, far_ref[...]).astype(BF16)
            sigma = half + half * jnp.tanh(half * pre)
            act = pre * sigma
            acts.append(act)
            sg_ref[k, rows, :] = sigma + (act - act * sigma)
        while len(acts) > 1:
            acts = [sum(acts[i : i + 2][1:], acts[i]) for i in range(0, len(acts), 2)]
        z = grid_ref[source, :].astype(F32) + mm(acts[0], w_msg_ref[...])
        centre = z - jnp.mean(z, axis=1, keepdims=True)
        rstd = lax.rsqrt(jnp.mean(centre * centre, axis=1, keepdims=True) + LN_EPS)
        zhat = centre * rstd
        pred = mm_t(w_out, (zhat * gain_ref[...]).astype(BF16))
        pred_ref[:, rows] = pred
        pred_bf_ref[:, rows] = pred.astype(BF16)
        zhat_ref[rows, :] = zhat.astype(BF16)
        rstd_ref[rows, :] = jnp.broadcast_to(rstd, (block, rstd_ref.shape[1]))


def backward_kernel(
    first,
    block,
    owned,
    coeff,
    slots_ref,
    pred_ref,
    others_ref,
    target_ref,
    weight_ref,
    w_out_ref,
    gain_ref,
    zhat_ref,
    rstd_ref,
    w_msg_ref,
    sg_ref,
    *refs,
):
    dz_ref, dsum_ref, dpre_ref = refs[-6:-3] if len(refs) > 4 else refs[:3]
    fields = pred_ref.shape[0]
    weight = weight_ref[...]
    weight = jnp.concatenate([weight, jnp.zeros((1, fields - weight.shape[1]), F32)], axis=1)
    w_out = rows_to(w_out_ref[...], fields).astype(BF16)
    edges, points, channels = dpre_ref.shape
    for rows in pieces(points, block):
        source = slice(first + rows.start, first + rows.stop)
        pred = pred_ref[:, rows]
        spread = jnp.zeros_like(pred)
        for other in range(others_ref.shape[0]):
            spread = spread + slope(pred - others_ref[other, :, rows].astype(F32))
        d_pred = slope(pred - rows_to(target_ref[:, source], fields)) - coeff * spread
        d_pred = (weight * d_pred.T).astype(BF16)
        scaled = mm(d_pred, w_out) * gain_ref[...]
        zhat = zhat_ref[rows, :].astype(F32)
        d_z = rstd_ref[rows, :1] * (
            scaled
            - jnp.mean(scaled, axis=1, keepdims=True)
            - zhat * jnp.mean(scaled * zhat, axis=1, keepdims=True)
        )
        d_zb = d_z.astype(BF16)
        dz_ref[rows, :] = d_zb
        d_act = mm_t(d_zb, w_msg_ref[...]).astype(BF16)
        total = jnp.zeros((block, channels), F32)
        for k in range(edges):
            d_pre = d_act * sg_ref[k, rows, :]
            total = total + d_pre.astype(F32)
            dpre_ref[k, rows, :] = d_pre
        dsum_ref[rows, :] = total.astype(BF16)
    slots = slots_ref[:, first : first + points]
    d_pre = dpre_ref[...].reshape(edges * points, channels)
    if len(refs) == 4:
        rims_ref = refs[3]
        rims_ref[...] = mm(row_hots(slots, owned, rims_ref.shape[0]), d_pre)
    else:
        rims_ref, near_ref, far_ref, acc = refs[0], *refs[-3:]
        acc[...] = rims_ref[...] + mm(row_hots(slots, owned, acc.shape[0]), d_pre)
        halo = far_ref.shape[0]
        near, far = rim_bases(0, halo)
        near_ref[...] = acc[pl.ds(pl.multiple_of(near, halo), halo), :].astype(BF16)
        far_ref[...] = acc[pl.ds(pl.multiple_of(far, halo), halo), :].astype(BF16)


def own_grad_kernel(chunks, slots_ref, w_dst_ref, *refs):
    grid_hbm, own_ref, grid_ref, sems = refs[-4:]
    owned = own_ref.shape[0]
    stores = []
    for c in range(chunks):
        dz_ref, dsum_ref, dpre_ref = refs[3 * c : 3 * c + 3]
        points = dz_ref.shape[0]
        rows = slice(c * points, (c + 1) * points)
        d_grid = dz_ref[...].astype(F32) + mm_t(dsum_ref[...], w_dst_ref[...])
        grid_ref[rows, :] = d_grid.astype(BF16)
        stores.append(pltpu.make_async_copy(grid_ref.at[rows], grid_hbm.at[rows], sems.at[c]))
        stores[-1].start()
    for c in range(chunks):
        dpre_ref = refs[3 * c + 2]
        edges, points, channels = dpre_ref.shape
        slots = slots_ref[:, c * points : (c + 1) * points]
        d_pre = dpre_ref[...].reshape(edges * points, channels)
        added = mm(row_hots(slots, 0, owned), d_pre)
        own_ref[...] = added if c == 0 else own_ref[...] + added
    for store in stores:
        store.wait()


def mesh_kernel(send_ref, near_ref, far_ref, own_ref, w_src_ref, mesh_hbm, out_ref, sems):
    owned = own_ref.shape[0]
    near, far = near_far(send_ref[0:1, :], send_ref[1:2, :])
    stores = []
    for i, part in enumerate(pieces(owned, owned // 4)):
        size = part.stop - part.start
        total = own_ref[part, :] + mm(row_hot(near - part.start, 0, size), near_ref[...])
        total = total + mm(row_hot(far - part.start, 0, size), far_ref[...])
        out_ref[part, :] = mm_t(total.astype(BF16), w_src_ref[...]).astype(BF16)
        stores.append(pltpu.make_async_copy(out_ref.at[part], mesh_hbm.at[part], sems.at[i]))
        stores[-1].start()
    for store in stores:
        store.wait()


def per_device(
    grid_latent,
    mesh_latent,
    edge_attr,
    neighbours,
    send_rows,
    target,
    field_weight,
    w_src,
    w_dst,
    w_edge,
    w_msg,
    ln_gain,
    w_out,
):
    grid_rows = grid_latent[0]
    mesh_rows = mesh_latent[0]
    points, channels = grid_rows.shape
    owned = mesh_rows.shape[0]
    halo = send_rows.shape[1]
    edges = neighbours.shape[1]
    feats = w_edge.shape[0]
    lanes = 128
    fields = -(-w_out.shape[1] // lanes) * lanes
    block = min(points, 256)
    sds = jax.ShapeDtypeStruct
    members = lax.axis_size("member")
    bands = lax.axis_size("band")
    near_swap = swap(range(0, bands - 1, 2))
    far_swap = swap(range(1, bands - 1, 2))
    slots = neighbours.T
    gain = ln_gain[None, :]
    w_out = w_out.T
    weight = field_weight[None, :]

    vmem, far_memory = pltpu.VMEM, pltpu.HBM
    src, near, far = call(
        send_kernel,
        [far_memory] * 3,
        [vmem] * 3,
        [sds((owned, channels), BF16), sds((halo, channels), BF16), sds((halo, channels), BF16)],
        2 * owned * channels * (channels + 2 * halo),
        4 * owned * channels * 2,
        [
            vmem((owned, channels), BF16),
            vmem((channels, channels), BF16),
            vmem((2, halo), jnp.int32),
            pltpu.SemaphoreType.DMA((6,)),
        ],
    )(hbm(mesh_rows), hbm(w_src), hbm(send_rows))
    far = lax.ppermute(far, "band", far_swap)
    near = lax.ppermute(near, "band", near_swap)

    [pre] = call(
        functools.partial(own_kernel, block),
        [vmem] * 7,
        [vmem],
        [sds((edges, points, channels), BF16)],
        2 * points * channels * (edges * (owned + halo) + channels),
        points * channels * edges * 2,
        [
            vmem((points // block, block, channels), F32),
            vmem((edges, lanes, channels), BF16),
            vmem((feats * edges, points), F32),
        ],
    )(slots, src, near, grid_rows, w_dst, edge_attr, w_edge)

    chunks = 2
    part = points // chunks
    ahead = []
    for c in range(chunks):
        pred, pred_bf, sg, zhat, rstd = call(
            functools.partial(forward_kernel, c * part, block, owned, fields),
            [vmem] * 7,
            [vmem] * 5,
            [
                sds((fields, part), F32),
                sds((fields, part), BF16),
                sds((edges, part, channels), BF16),
                sds((part, channels), BF16),
                sds((part, lanes), F32),
            ],
            2 * part * channels * (edges * halo + channels),
            part * channels * edges * 4,
        )(slots, pre, far, grid_rows, w_msg, gain, w_out)
        if members == 2:
            others = lax.ppermute(pred_bf, "member", [(0, 1), (1, 0)])[None]
        else:
            others = lax.all_gather(pred_bf[None], "member", axis=0, tiled=True)
        ahead.append((pred, others, sg, zhat, rstd))

    coeff = ALPHA / (members - 1) + (1.0 - ALPHA) / members
    rims = []
    behind = []
    for c, (pred, others, sg, zhat, rstd) in enumerate(ahead):
        last = c == chunks - 1
        rim_shapes = (
            [sds((halo, channels), BF16)] * 2 if last else [sds((2 * halo, channels), F32)]
        )
        d_z, d_sum, d_pre, *rims = call(
            functools.partial(backward_kernel, c * part, block, owned, coeff),
            [vmem] * (11 + len(rims)),
            [vmem] * (3 + len(rim_shapes)),
            [
                sds((part, channels), BF16),
                sds((part, channels), BF16),
                sds((edges, part, channels), BF16),
                *rim_shapes,
            ],
            2 * part * channels * (edges * 2 * halo + channels),
            part * channels * edges * 4,
            [vmem((2 * halo, channels), F32)] * last,
        )(slots, pred, others, target, weight, w_out, gain, zhat, rstd, w_msg, sg, *rims)
        behind += [d_z, d_sum, d_pre]
    near, far = rims
    far = lax.ppermute(far, "band", far_swap)
    near = lax.ppermute(near, "band", near_swap)

    d_grid, own = call(
        functools.partial(own_grad_kernel, chunks),
        [vmem] * (2 + len(behind)),
        [far_memory, vmem],
        [sds((points, channels), BF16), sds((owned, channels), F32)],
        2 * points * channels * (edges * owned + channels),
        points * channels * edges * 2,
        [vmem((points, channels), BF16), pltpu.SemaphoreType.DMA((chunks,))],
    )(slots, w_dst, *behind)

    [d_mesh] = call(
        mesh_kernel,
        [vmem] * 5,
        [far_memory],
        [sds((owned, channels), BF16)],
        2 * owned * channels * (channels + 2 * halo),
        owned * channels * 8,
        [vmem((owned, channels), BF16), pltpu.SemaphoreType.DMA((4,))],
    )(send_rows, near, far, own, w_src)
    return (d_grid[None], d_mesh[None])


def solution(mesh):
    placed = (
        P("member", "band", None),
        P("member", "band", None),
        P(None, None, "band"),
        P("band", None),
        P("band", None),
        P(None, "band"),
        P(),
        P(),
        P(),
        P(),
        P(),
        P(),
        P(),
    )
    return jax.shard_map(
        per_device,
        mesh=mesh,
        in_specs=placed,
        out_specs=(P("member", "band", None), P("member", "band", None)),
        check_vma=False,
    )
```

```python
import functools

import jax
import jax.numpy as jnp
from jax import lax
from jax.experimental import pallas as pl
from jax.experimental.pallas import tpu as pltpu
from jax.sharding import PartitionSpec as P

DELTA_SQ = 0.0625
ALPHA = 0.95
LN_EPS = 1e-05
F32 = jnp.float32
BF16 = jnp.bfloat16
IN_SHADOW = (1, 1)
VMEM_LIMIT = 28 * 1024 * 1024


def slope(diff):
    return diff * lax.rsqrt(diff * diff + DELTA_SQ)


def mm(left, right):
    return jnp.dot(left, right, preferred_element_type=F32)


def mm_t(left, right):
    return lax.dot_general(left, right, (((1,), (1,)), ((), ())), preferred_element_type=F32)


def column_hot(ids, base, slots):
    lanes = 128
    rows = ids.shape[1]
    column = jnp.broadcast_to((ids - base).astype(F32), (lanes, rows)).T.astype(jnp.int16)
    lane = lax.broadcasted_iota(jnp.int16, (rows, lanes), 1)
    parts = [
        jnp.where(column == lane + jnp.int16(first), BF16(1), BF16(0))
        for first in range(0, slots, lanes)
    ]
    return jnp.concatenate(parts, axis=1)


def row_hot(ids, base, slots):
    row = (ids - base).astype(jnp.int16)
    return jnp.where(
        row == lax.broadcasted_iota(jnp.int16, (slots, ids.shape[1]), 0), BF16(1), BF16(0)
    )


def row_hots(ids, base, slots):
    return jnp.concatenate(
        [row_hot(ids[k : k + 1, :], base, slots) for k in range(ids.shape[0])], axis=1
    )


def swap(firsts):
    return [pair for i in firsts for pair in ((i, i + 1), (i + 1, i))]


def hbm(array):
    return pltpu.with_memory_space_constraint(array, pltpu.HBM)


def call(body, places, out_places, out_shape, flops, nbytes, scratch=()):
    def specs(memories):
        return [pl.BlockSpec(memory_space=memory) for memory in memories]

    return pl.pallas_call(
        body,
        in_specs=specs(places),
        out_specs=specs(out_places),
        out_shape=out_shape,
        scratch_shapes=scratch,
        compiler_params=pltpu.CompilerParams(vmem_limit_bytes=VMEM_LIMIT),
        cost_estimate=pl.CostEstimate(flops=flops, bytes_accessed=nbytes, transcendentals=0),
    )


def near_far(low, high):
    odd = lax.axis_index("band") % 2 == 1
    return jnp.where(odd, low, high), jnp.where(odd, high, low)


def rim_bases(owned, halo):
    return near_far(owned, owned + halo)


def rows_to(array, rows):
    array = array.astype(F32)
    return jnp.concatenate([array, jnp.zeros((rows - array.shape[0], array.shape[1]), F32)], axis=0)


def pieces(rows, size):
    return [slice(first, first + size) for first in range(0, rows, size)]


def far_kernel(mesh_hbm, w_src_hbm, send_hbm, far_ref, mesh_ref, w_src_ref, send_ref, sems):
    owned = mesh_ref.shape[0]
    parts = pieces(owned, owned // 2)
    lists = pltpu.make_async_copy(send_hbm, send_ref, sems.at[0])
    lists.start()
    loads = []
    for i, part in enumerate(parts):
        loads.append(pltpu.make_async_copy(mesh_hbm.at[part], mesh_ref.at[part], sems.at[2 + i]))
        loads[-1].start()
    weights = pltpu.make_async_copy(w_src_hbm, w_src_ref, sems.at[1])
    weights.start()
    lists.wait()
    far = near_far(send_ref[0:1, :], send_ref[1:2, :])[1]
    hots = [column_hot(far, part.start, part.stop - part.start) for part in parts]
    rows = None
    for load, part, hot in zip(loads, parts, hots):
        load.wait()
        picked = mm(hot, mesh_ref[part])
        rows = picked if rows is None else rows + picked
    weights.wait()
    far_ref[...] = mm(rows.astype(BF16), w_src_ref[...]).astype(BF16)


def near_kernel(mesh_ref, w_src_ref, send_ref, src_ref, *near_refs):
    src = mm(mesh_ref[...], w_src_ref[...]).astype(BF16)
    src_ref[...] = src
    near = near_far(send_ref[0:1, :], send_ref[1:2, :])[0]
    size = near_refs[0].shape[0]
    for i, near_ref in enumerate(near_refs):
        ids = near[:, i * size : (i + 1) * size]
        near_ref[...] = mm(column_hot(ids, 0, src.shape[0]), src_ref[...]).astype(BF16)


def own_kernel(
    block,
    slots_ref,
    src_ref,
    grid_ref,
    w_dst_ref,
    attr_ref,
    w_edge_ref,
    *refs,
):
    *near_refs, pre_ref, dst_ref, embed_ref, attr_f32 = refs
    edges, lanes, channels = embed_ref.shape
    feats = w_edge_ref.shape[0]
    row = lax.broadcasted_iota(jnp.int32, (lanes, channels), 0)
    w_edge = w_edge_ref[...].astype(F32)
    for k in range(edges):
        spread = jnp.zeros((lanes, channels), F32)
        for e in range(feats):
            spread = jnp.where(row == e * edges + k, w_edge[e : e + 1, :], spread)
        embed_ref[k] = spread.astype(BF16)
    for e in range(feats):
        attr_f32[e * edges : (e + 1) * edges, :] = attr_ref[e].astype(F32)
    owned = src_ref.shape[0]
    size = near_refs[0].shape[0]
    base = rim_bases(owned, size * len(near_refs))[0]
    for at, rows in enumerate(pieces(grid_ref.shape[0], block)):
        dst_ref[at] = mm(grid_ref[rows, :], w_dst_ref[...])
        attr = rows_to(attr_f32[:, rows], lanes).T.astype(BF16)
        for k in range(edges):
            ids = slots_ref[k : k + 1, rows]
            picked = mm(column_hot(ids, 0, owned), src_ref[...])
            for i, near_ref in enumerate(near_refs):
                picked = picked + mm(column_hot(ids, base + i * size, size), near_ref[...])
            embed = mm(attr, embed_ref[k])
            pre_ref[k, rows, :] = (picked + embed + dst_ref[at]).astype(BF16)


def forward_kernel(
    first,
    block,
    owned,
    fields,
    slots_ref,
    pre_ref,
    far_ref,
    grid_ref,
    w_msg_ref,
    gain_ref,
    w_out_ref,
    pred_ref,
    pred_bf_ref,
    sg_ref,
    zhat_ref,
    rstd_ref,
):
    half = BF16(0.5)
    halo = far_ref.shape[0]
    base = rim_bases(owned, halo)[1]
    w_out = rows_to(w_out_ref[...], fields).astype(BF16)
    for rows in pieces(zhat_ref.shape[0], block):
        source = slice(first + rows.start, first + rows.stop)
        acts = []
        for k in range(slots_ref.shape[0]):
            hot = column_hot(slots_ref[k : k + 1, source], base, halo)
            pre = pre_ref[k, source, :] + mm(hot, far_ref[...]).astype(BF16)
            sigma = half + half * jnp.tanh(half * pre)
            act = pre * sigma
            acts.append(act)
            sg_ref[k, rows, :] = sigma + (act - act * sigma)
        while len(acts) > 1:
            acts = [sum(acts[i : i + 2][1:], acts[i]) for i in range(0, len(acts), 2)]
        z = grid_ref[source, :].astype(F32) + mm(acts[0], w_msg_ref[...])
        centre = z - jnp.mean(z, axis=1, keepdims=True)
        rstd = lax.rsqrt(jnp.mean(centre * centre, axis=1, keepdims=True) + LN_EPS)
        zhat = centre * rstd
        pred = mm_t(w_out, (zhat * gain_ref[...]).astype(BF16))
        pred_ref[:, rows] = pred
        pred_bf_ref[:, rows] = pred.astype(BF16)
        zhat_ref[rows, :] = zhat.astype(BF16)
        rstd_ref[rows, :] = jnp.broadcast_to(rstd, (block, rstd_ref.shape[1]))


def backward_kernel(
    first,
    block,
    owned,
    coeff,
    slots_ref,
    pred_ref,
    others_ref,
    target_ref,
    weight_ref,
    w_out_ref,
    gain_ref,
    zhat_ref,
    rstd_ref,
    w_msg_ref,
    sg_ref,
    *refs,
):
    dz_ref, dsum_ref, dpre_ref = refs[-4:-1]
    fields = pred_ref.shape[0]
    weight = weight_ref[...]
    weight = jnp.concatenate([weight, jnp.zeros((1, fields - weight.shape[1]), F32)], axis=1)
    w_out = rows_to(w_out_ref[...], fields).astype(BF16)
    edges, points, channels = dpre_ref.shape
    for rows in pieces(points, block):
        source = slice(first + rows.start, first + rows.stop)
        pred = pred_ref[:, rows]
        spread = jnp.zeros_like(pred)
        for other in range(others_ref.shape[0]):
            spread = spread + slope(pred - others_ref[other, :, rows].astype(F32))
        d_pred = slope(pred - rows_to(target_ref[:, source], fields)) - coeff * spread
        d_pred = (weight * d_pred.T).astype(BF16)
        scaled = mm(d_pred, w_out) * gain_ref[...]
        zhat = zhat_ref[rows, :].astype(F32)
        d_z = rstd_ref[rows, :1] * (
            scaled
            - jnp.mean(scaled, axis=1, keepdims=True)
            - zhat * jnp.mean(scaled * zhat, axis=1, keepdims=True)
        )
        d_zb = d_z.astype(BF16)
        dz_ref[rows, :] = d_zb
        d_act = mm_t(d_zb, w_msg_ref[...]).astype(BF16)
        total = jnp.zeros((block, channels), F32)
        for k in range(edges):
            d_pre = d_act * sg_ref[k, rows, :]
            total = total + d_pre.astype(F32)
            dpre_ref[k, rows, :] = d_pre
        dsum_ref[rows, :] = total.astype(BF16)
    slots = slots_ref[:, first : first + points]
    d_pre = dpre_ref[...].reshape(edges * points, channels)
    far_ref = refs[-1]
    halo = far_ref.shape[0]
    far = mm(row_hots(slots, rim_bases(owned, halo)[1], halo), d_pre)
    if len(refs) > 4:
        far = far + refs[0][...]
    far_ref[...] = far.astype(far_ref.dtype)


def rim_kernel(owned, chunks, slots_ref, *refs):
    dpre_refs = refs[:chunks]
    *near_refs, acc = refs[chunks:]
    size = near_refs[0].shape[0]
    base = rim_bases(owned, acc.shape[0])[0]
    first = 0
    for c, dpre_ref in enumerate(dpre_refs):
        edges, points, channels = dpre_ref.shape
        slots = slots_ref[:, first : first + points]
        first += points
        added = mm(
            row_hots(slots, base, acc.shape[0]), dpre_ref[...].reshape(edges * points, channels)
        )
        acc[...] = added if c == 0 else acc[...] + added
    for i, near_ref in enumerate(near_refs):
        near_ref[...] = acc[i * size : (i + 1) * size, :].astype(BF16)


def own_grad_kernel(chunks, slots_ref, w_dst_ref, *refs):
    grid_hbm, own_ref, grid_ref, sems = refs[-4:]
    owned = own_ref.shape[0]
    stores = []
    for c in range(chunks):
        dz_ref, dsum_ref, dpre_ref = refs[3 * c : 3 * c + 3]
        points = dz_ref.shape[0]
        rows = slice(c * points, (c + 1) * points)
        d_grid = dz_ref[...].astype(F32) + mm_t(dsum_ref[...], w_dst_ref[...])
        grid_ref[rows, :] = d_grid.astype(BF16)
        stores.append(pltpu.make_async_copy(grid_ref.at[rows], grid_hbm.at[rows], sems.at[c]))
        stores[-1].start()
    for c in range(chunks):
        dpre_ref = refs[3 * c + 2]
        edges, points, channels = dpre_ref.shape
        slots = slots_ref[:, c * points : (c + 1) * points]
        d_pre = dpre_ref[...].reshape(edges * points, channels)
        added = mm(row_hots(slots, 0, owned), d_pre)
        own_ref[...] = added if c == 0 else own_ref[...] + added
    for store in stores:
        store.wait()


def merge_kernel(send_ref, own_ref, *refs):
    *near_refs, sum_ref, hot_ref = refs
    owned = own_ref.shape[0]
    near, far = near_far(send_ref[0:1, :], send_ref[1:2, :])
    size = near_refs[0].shape[0]
    total = own_ref[...]
    for i, near_ref in enumerate(near_refs):
        total = total + mm(row_hot(near[:, i * size : (i + 1) * size], 0, owned), near_ref[...])
    sum_ref[...] = total
    hot_ref[...] = row_hot(far, 0, owned)


def mesh_kernel(far_ref, hot_ref, sum_ref, w_src_ref, mesh_hbm, out_ref, sems):
    owned = sum_ref.shape[0]
    stores = []
    for i, part in enumerate(pieces(owned, owned // 4)):
        total = sum_ref[part, :] + mm(hot_ref[part, :], far_ref[...])
        out_ref[part, :] = mm_t(total.astype(BF16), w_src_ref[...]).astype(BF16)
        stores.append(pltpu.make_async_copy(out_ref.at[part], mesh_hbm.at[part], sems.at[i]))
        stores[-1].start()
    for store in stores:
        store.wait()


def per_device(
    grid_latent,
    mesh_latent,
    edge_attr,
    neighbours,
    send_rows,
    target,
    field_weight,
    w_src,
    w_dst,
    w_edge,
    w_msg,
    ln_gain,
    w_out,
):
    grid_rows = grid_latent[0]
    mesh_rows = mesh_latent[0]
    points, channels = grid_rows.shape
    owned = mesh_rows.shape[0]
    halo = send_rows.shape[1]
    edges = neighbours.shape[1]
    feats = w_edge.shape[0]
    lanes = 128
    fields = -(-w_out.shape[1] // lanes) * lanes
    block = min(points, 256)
    sds = jax.ShapeDtypeStruct
    members = lax.axis_size("member")
    bands = lax.axis_size("band")
    near_swap = swap(range(0, bands - 1, 2))
    far_swap = swap(range(1, bands - 1, 2))
    vmem, far_memory = pltpu.VMEM, pltpu.HBM
    slots = neighbours.T
    gain = ln_gain[None, :]
    w_out = w_out.T
    weight = field_weight[None, :]

    [far] = call(
        far_kernel,
        [far_memory] * 3,
        [vmem],
        [sds((halo, channels), BF16)],
        2 * owned * channels * halo,
        2 * owned * channels,
        [
            vmem((owned, channels), BF16),
            vmem((channels, channels), BF16),
            vmem((2, halo), jnp.int32),
            pltpu.SemaphoreType.DMA((4,)),
        ],
    )(hbm(mesh_rows), hbm(w_src), hbm(send_rows))
    far = lax.ppermute(far, "band", far_swap)

    near_shapes = [sds((halo // 2, channels), BF16)] * 2
    src, *near = call(
        near_kernel,
        [vmem] * 3,
        [vmem] * 3,
        [sds((owned, channels), BF16), *near_shapes],
        *IN_SHADOW,
    )(mesh_rows, w_src, send_rows)
    near = [lax.ppermute(piece, "band", near_swap) for piece in near]

    [pre] = call(
        functools.partial(own_kernel, block),
        [vmem] * (6 + len(near)),
        [vmem],
        [sds((edges, points, channels), BF16)],
        *IN_SHADOW,
        [
            vmem((points // block, block, channels), F32),
            vmem((edges, lanes, channels), BF16),
            vmem((feats * edges, points), F32),
        ],
    )(slots, src, grid_rows, w_dst, edge_attr, w_edge, *near)

    chunks = 2
    part = points // chunks
    ahead = []
    for c in range(chunks):
        pred, pred_bf, sg, zhat, rstd = call(
            functools.partial(forward_kernel, c * part, block, owned, fields),
            [vmem] * 7,
            [vmem] * 5,
            [
                sds((fields, part), F32),
                sds((fields, part), BF16),
                sds((edges, part, channels), BF16),
                sds((part, channels), BF16),
                sds((part, lanes), F32),
            ],
            2 * part * channels * (edges * halo + channels),
            part * channels * edges * 4,
        )(slots, pre, far, grid_rows, w_msg, gain, w_out)
        if members == 2:
            others = lax.ppermute(pred_bf, "member", [(0, 1), (1, 0)])[None]
        else:
            others = lax.all_gather(pred_bf[None], "member", axis=0, tiled=True)
        ahead.append((pred, others, sg, zhat, rstd))

    coeff = ALPHA / (members - 1) + (1.0 - ALPHA) / members
    far = []
    d_zs, d_sums, d_pres = [], [], []
    for c, (pred, others, sg, zhat, rstd) in enumerate(ahead):
        d_z, d_sum, d_pre, *far = call(
            functools.partial(backward_kernel, c * part, block, owned, coeff),
            [vmem] * (11 + len(far)),
            [vmem] * 4,
            [
                sds((part, channels), BF16),
                sds((part, channels), BF16),
                sds((edges, part, channels), BF16),
                sds((halo, channels), BF16 if c == chunks - 1 else F32),
            ],
            2 * part * channels * (edges * halo + channels),
            part * channels * edges * 4,
        )(slots, pred, others, target, weight, w_out, gain, zhat, rstd, w_msg, sg, *far)
        d_zs.append(d_z)
        d_sums.append(d_sum)
        d_pres.append(d_pre)
    far = lax.ppermute(far[0], "band", far_swap)

    near = call(
        functools.partial(rim_kernel, owned, chunks),
        [vmem] * (1 + chunks),
        [vmem] * len(near_shapes),
        near_shapes,
        *IN_SHADOW,
        [vmem((halo, channels), F32)],
    )(slots, *d_pres)
    near = [lax.ppermute(piece, "band", near_swap) for piece in near]

    d_grid, own = call(
        functools.partial(own_grad_kernel, chunks),
        [vmem] * (2 + 3 * chunks),
        [far_memory, vmem],
        [sds((points, channels), BF16), sds((owned, channels), F32)],
        *IN_SHADOW,
        [vmem((points, channels), BF16), pltpu.SemaphoreType.DMA((chunks,))],
    )(slots, w_dst, *[ref for trio in zip(d_zs, d_sums, d_pres) for ref in trio])

    total, far_hot = call(
        merge_kernel,
        [vmem] * (2 + len(near)),
        [vmem] * 2,
        [sds((owned, channels), F32), sds((owned, halo), BF16)],
        *IN_SHADOW,
    )(send_rows, own, *near)

    [d_mesh] = call(
        mesh_kernel,
        [vmem] * 4,
        [far_memory],
        [sds((owned, channels), BF16)],
        2 * owned * channels * (channels + halo),
        owned * channels * 8,
        [vmem((owned, channels), BF16), pltpu.SemaphoreType.DMA((4,))],
    )(far, far_hot, total, w_src)
    return (d_grid[None], d_mesh[None])


def solution(mesh):
    placed = (
        P("member", "band", None),
        P("member", "band", None),
        P(None, None, "band"),
        P("band", None),
        P("band", None),
        P(None, "band"),
        P(),
        P(),
        P(),
        P(),
        P(),
        P(),
        P(),
    )
    return jax.shard_map(
        per_device,
        mesh=mesh,
        in_specs=placed,
        out_specs=(P("member", "band", None), P("member", "band", None)),
        check_vma=False,
    )
```

```python
import functools

import jax
import jax.numpy as jnp
from jax import lax
from jax.experimental import pallas as pl
from jax.experimental.pallas import tpu as pltpu
from jax.sharding import PartitionSpec as P

DELTA_SQ = 0.0625
ALPHA = 0.95
LN_EPS = 1e-05
F32 = jnp.float32
BF16 = jnp.bfloat16
IN_SHADOW = (1, 1)
VMEM_LIMIT = 28 * 1024 * 1024


def slope(diff):
    return diff * lax.rsqrt(diff * diff + DELTA_SQ)


def mm(left, right):
    return jnp.dot(left, right, preferred_element_type=F32)


def mm_t(left, right):
    return lax.dot_general(left, right, (((1,), (1,)), ((), ())), preferred_element_type=F32)


def column_hot(ids, base, slots):
    lanes = 128
    rows = ids.shape[1]
    column = jnp.broadcast_to((ids - base).astype(F32), (lanes, rows)).T.astype(jnp.int16)
    lane = lax.broadcasted_iota(jnp.int16, (rows, lanes), 1)
    parts = [
        jnp.where(column == lane + jnp.int16(first), BF16(1), BF16(0))
        for first in range(0, slots, lanes)
    ]
    return jnp.concatenate(parts, axis=1)


def row_hot(ids, base, slots):
    row = (ids - base).astype(jnp.int16)
    return jnp.where(
        row == lax.broadcasted_iota(jnp.int16, (slots, ids.shape[1]), 0), BF16(1), BF16(0)
    )


def row_hots(ids, base, slots):
    return jnp.concatenate(
        [row_hot(ids[k : k + 1, :], base, slots) for k in range(ids.shape[0])], axis=1
    )


def swap(firsts):
    return [pair for i in firsts for pair in ((i, i + 1), (i + 1, i))]


def hbm(array):
    return pltpu.with_memory_space_constraint(array, pltpu.HBM)


def call(body, places, out_places, out_shape, flops, nbytes, scratch=()):
    def specs(memories):
        return [pl.BlockSpec(memory_space=memory) for memory in memories]

    return pl.pallas_call(
        body,
        in_specs=specs(places),
        out_specs=specs(out_places),
        out_shape=out_shape,
        scratch_shapes=scratch,
        compiler_params=pltpu.CompilerParams(vmem_limit_bytes=VMEM_LIMIT),
        cost_estimate=pl.CostEstimate(flops=flops, bytes_accessed=nbytes, transcendentals=0),
    )


def near_far(low, high):
    odd = lax.axis_index("band") % 2 == 1
    return jnp.where(odd, low, high), jnp.where(odd, high, low)


def rim_bases(owned, halo):
    return near_far(owned, owned + halo)


def rows_to(array, rows):
    array = array.astype(F32)
    return jnp.concatenate([array, jnp.zeros((rows - array.shape[0], array.shape[1]), F32)], axis=0)


def pieces(rows, size):
    return [slice(first, first + size) for first in range(0, rows, size)]


def placed_rows(refs):
    first, out = 0, []
    for ref in refs:
        out.append((slice(first, first + ref.shape[0]), ref))
        first += ref.shape[0]
    return out


def join(refs, whole_ref):
    for rows, ref in placed_rows(refs):
        whole_ref[rows, :] = ref[...]


def far_kernel(mesh_hbm, w_src_hbm, send_hbm, *refs):
    *far_refs, mesh_ref, w_src_ref, send_ref, sems = refs
    owned = mesh_ref.shape[0]
    parts = pieces(owned, owned // 2)
    lists = pltpu.make_async_copy(send_hbm, send_ref, sems.at[0])
    lists.start()
    loads = []
    for i, part in enumerate(parts):
        loads.append(pltpu.make_async_copy(mesh_hbm.at[part], mesh_ref.at[part], sems.at[2 + i]))
        loads[-1].start()
    weights = pltpu.make_async_copy(w_src_hbm, w_src_ref, sems.at[1])
    weights.start()
    lists.wait()
    far = near_far(send_ref[0:1, :], send_ref[1:2, :])[1]
    hots = [column_hot(far, part.start, part.stop - part.start) for part in parts]
    rows = None
    for load, part, hot in zip(loads, parts, hots):
        load.wait()
        picked = mm(hot, mesh_ref[part])
        rows = picked if rows is None else rows + picked
    weights.wait()
    rows = mm(rows.astype(BF16), w_src_ref[...]).astype(BF16)
    size = far_refs[0].shape[0]
    for i, far_ref in enumerate(far_refs):
        far_ref[...] = rows[i * size : (i + 1) * size, :]


def near_kernel(mesh_ref, w_src_ref, send_ref, src_ref, *near_refs):
    src = mm(mesh_ref[...], w_src_ref[...]).astype(BF16)
    src_ref[...] = src
    near = near_far(send_ref[0:1, :], send_ref[1:2, :])[0]
    rows = mm(column_hot(near, 0, src.shape[0]), src_ref[...]).astype(BF16)
    for part, near_ref in placed_rows(near_refs):
        near_ref[...] = rows[part, :]


def own_kernel(
    block,
    slots_ref,
    src_ref,
    grid_ref,
    w_dst_ref,
    attr_ref,
    w_edge_ref,
    *refs,
):
    *near_refs, pre_ref, dst_ref, embed_ref, attr_f32, near_ref = refs
    join(near_refs, near_ref)
    edges, lanes, channels = embed_ref.shape
    feats = w_edge_ref.shape[0]
    row = lax.broadcasted_iota(jnp.int32, (lanes, channels), 0)
    w_edge = w_edge_ref[...].astype(F32)
    for k in range(edges):
        spread = jnp.zeros((lanes, channels), F32)
        for e in range(feats):
            spread = jnp.where(row == e * edges + k, w_edge[e : e + 1, :], spread)
        embed_ref[k] = spread.astype(BF16)
    for e in range(feats):
        attr_f32[e * edges : (e + 1) * edges, :] = attr_ref[e].astype(F32)
    owned = src_ref.shape[0]
    halo = near_ref.shape[0]
    base = rim_bases(owned, halo)[0]
    for at, rows in enumerate(pieces(grid_ref.shape[0], block)):
        dst_ref[at] = mm(grid_ref[rows, :], w_dst_ref[...])
        attr = rows_to(attr_f32[:, rows], lanes).T.astype(BF16)
        for k in range(edges):
            ids = slots_ref[k : k + 1, rows]
            picked = mm(column_hot(ids, 0, owned), src_ref[...])
            picked = picked + mm(column_hot(ids, base, halo), near_ref[...])
            embed = mm(attr, embed_ref[k])
            pre_ref[k, rows, :] = (picked + embed + dst_ref[at]).astype(BF16)


def forward_kernel(
    first,
    block,
    owned,
    fields,
    slots_ref,
    pre_ref,
    grid_ref,
    w_msg_ref,
    gain_ref,
    w_out_ref,
    *refs,
):
    *far_refs, pred_ref, pred_bf_ref, sg_ref, zhat_ref, rstd_ref = refs
    half = BF16(0.5)
    size = far_refs[0].shape[0]
    base = rim_bases(owned, size * len(far_refs))[1]
    w_out = rows_to(w_out_ref[...], fields).astype(BF16)
    for rows in pieces(zhat_ref.shape[0], block):
        source = slice(first + rows.start, first + rows.stop)
        acts = []
        for k in range(slots_ref.shape[0]):
            ids = slots_ref[k : k + 1, source]
            picked = None
            for i, far_ref in enumerate(far_refs):
                rows_i = mm(column_hot(ids, base + i * size, size), far_ref[...])
                picked = rows_i if picked is None else picked + rows_i
            pre = pre_ref[k, source, :] + picked.astype(BF16)
            sigma = half + half * jnp.tanh(half * pre)
            act = pre * sigma
            acts.append(act)
            sg_ref[k, rows, :] = sigma + (act - act * sigma)
        while len(acts) > 1:
            acts = [sum(acts[i : i + 2][1:], acts[i]) for i in range(0, len(acts), 2)]
        z = grid_ref[source, :].astype(F32) + mm(acts[0], w_msg_ref[...])
        centre = z - jnp.mean(z, axis=1, keepdims=True)
        rstd = lax.rsqrt(jnp.mean(centre * centre, axis=1, keepdims=True) + LN_EPS)
        zhat = centre * rstd
        pred = mm_t(w_out, (zhat * gain_ref[...]).astype(BF16))
        pred_ref[:, rows] = pred
        pred_bf_ref[:, rows] = pred.astype(BF16)
        zhat_ref[rows, :] = zhat.astype(BF16)
        rstd_ref[rows, :] = jnp.broadcast_to(rstd, (block, rstd_ref.shape[1]))


def backward_kernel(
    first,
    block,
    owned,
    coeff,
    given,
    slots_ref,
    pred_ref,
    others_ref,
    target_ref,
    weight_ref,
    w_out_ref,
    gain_ref,
    zhat_ref,
    rstd_ref,
    w_msg_ref,
    sg_ref,
    *refs,
):
    prior, (dz_ref, dpre_ref, *far_refs) = refs[:given], refs[given:]
    fields = pred_ref.shape[0]
    weight = weight_ref[...]
    weight = jnp.concatenate([weight, jnp.zeros((1, fields - weight.shape[1]), F32)], axis=1)
    w_out = rows_to(w_out_ref[...], fields).astype(BF16)
    edges, points, channels = dpre_ref.shape
    for rows in pieces(points, block):
        source = slice(first + rows.start, first + rows.stop)
        pred = pred_ref[:, rows]
        spread = jnp.zeros_like(pred)
        for other in range(others_ref.shape[0]):
            spread = spread + slope(pred - others_ref[other, :, rows].astype(F32))
        d_pred = slope(pred - rows_to(target_ref[:, source], fields)) - coeff * spread
        d_pred = (weight * d_pred.T).astype(BF16)
        scaled = mm(d_pred, w_out) * gain_ref[...]
        zhat = zhat_ref[rows, :].astype(F32)
        d_z = rstd_ref[rows, :1] * (
            scaled
            - jnp.mean(scaled, axis=1, keepdims=True)
            - zhat * jnp.mean(scaled * zhat, axis=1, keepdims=True)
        )
        d_zb = d_z.astype(BF16)
        dz_ref[rows, :] = d_zb
        d_act = mm_t(d_zb, w_msg_ref[...]).astype(BF16)
        for k in range(edges):
            dpre_ref[k, rows, :] = d_act * sg_ref[k, rows, :]
    slots = slots_ref[:, first : first + points]
    d_pre = dpre_ref[...].reshape(edges * points, channels)
    size = far_refs[0].shape[0]
    halo = size * len(far_refs)
    far = mm(row_hots(slots, rim_bases(owned, halo)[1], halo), d_pre)
    if prior:
        far = far + prior[0][...]
    for i, far_ref in enumerate(far_refs):
        far_ref[...] = far[i * size : (i + 1) * size, :].astype(far_ref.dtype)


def rim_kernel(owned, chunks, slots_ref, *refs):
    dpre_refs = refs[:chunks]
    *near_refs, acc = refs[chunks:]
    base = rim_bases(owned, acc.shape[0])[0]
    first = 0
    for c, dpre_ref in enumerate(dpre_refs):
        edges, points, channels = dpre_ref.shape
        slots = slots_ref[:, first : first + points]
        first += points
        added = mm(
            row_hots(slots, base, acc.shape[0]), dpre_ref[...].reshape(edges * points, channels)
        )
        acc[...] = added if c == 0 else acc[...] + added
    for rows, near_ref in placed_rows(near_refs):
        near_ref[...] = acc[rows, :].astype(BF16)


def own_grad_kernel(chunks, slots_ref, w_dst_ref, *refs):
    grid_hbm, own_ref, grid_ref, sems = refs[-4:]
    owned = own_ref.shape[0]
    stores = []
    for c in range(chunks):
        dz_ref, dpre_ref = refs[2 * c : 2 * c + 2]
        points = dz_ref.shape[0]
        rows = slice(c * points, (c + 1) * points)
        d_sum = sum(dpre_ref[k].astype(F32) for k in range(dpre_ref.shape[0]))
        d_grid = dz_ref[...].astype(F32) + mm_t(d_sum.astype(BF16), w_dst_ref[...])
        grid_ref[rows, :] = d_grid.astype(BF16)
        stores.append(pltpu.make_async_copy(grid_ref.at[rows], grid_hbm.at[rows], sems.at[c]))
        stores[-1].start()
    for c in range(chunks):
        dpre_ref = refs[2 * c + 1]
        edges, points, channels = dpre_ref.shape
        slots = slots_ref[:, c * points : (c + 1) * points]
        d_pre = dpre_ref[...].reshape(edges * points, channels)
        added = mm(row_hots(slots, 0, owned), d_pre)
        own_ref[...] = added if c == 0 else own_ref[...] + added
    for store in stores:
        store.wait()


def merge_kernel(send_ref, own_ref, w_src_ref, *refs):
    *near_refs, base_ref, hot_ref, near_ref = refs
    join(near_refs, near_ref)
    owned = own_ref.shape[0]
    near, far = near_far(send_ref[0:1, :], send_ref[1:2, :])
    total = own_ref[...] + mm(row_hot(near, 0, owned), near_ref[...])
    base_ref[...] = mm_t(total.astype(BF16), w_src_ref[...])
    hot_ref[...] = row_hot(far, 0, owned)


def mesh_kernel(hot_ref, base_ref, w_src_ref, *refs):
    *far_refs, mesh_hbm, rows_ref, out_ref, sems = refs
    owned = base_ref.shape[0]
    size = far_refs[0].shape[0]
    for i, far_ref in enumerate(far_refs):
        rows_ref[i * size : (i + 1) * size, :] = mm_t(far_ref[...], w_src_ref[...]).astype(BF16)
    stores = []
    for i, part in enumerate(pieces(owned, owned // 4)):
        out = base_ref[part, :] + mm(hot_ref[part, :], rows_ref[...])
        out_ref[part, :] = out.astype(BF16)
        stores.append(pltpu.make_async_copy(out_ref.at[part], mesh_hbm.at[part], sems.at[i]))
        stores[-1].start()
    for store in stores:
        store.wait()


def per_device(
    grid_latent,
    mesh_latent,
    edge_attr,
    neighbours,
    send_rows,
    target,
    field_weight,
    w_src,
    w_dst,
    w_edge,
    w_msg,
    ln_gain,
    w_out,
):
    grid_rows = grid_latent[0]
    mesh_rows = mesh_latent[0]
    points, channels = grid_rows.shape
    owned = mesh_rows.shape[0]
    halo = send_rows.shape[1]
    edges = neighbours.shape[1]
    feats = w_edge.shape[0]
    lanes = 128
    fields = -(-w_out.shape[1] // lanes) * lanes
    block = min(points, 256)
    sds = jax.ShapeDtypeStruct
    members = lax.axis_size("member")
    bands = lax.axis_size("band")
    near_swap = swap(range(0, bands - 1, 2))
    far_swap = swap(range(1, bands - 1, 2))
    vmem, far_memory = pltpu.VMEM, pltpu.HBM
    slots = neighbours.T
    gain = ln_gain[None, :]
    w_out = w_out.T
    weight = field_weight[None, :]

    far_shapes = [sds((halo // 2, channels), BF16)] * 2
    third = -(-halo // 48) * 16
    near_shapes = [sds((size, channels), BF16) for size in (third, third, halo - 2 * third)]
    far = call(
        far_kernel,
        [far_memory] * 3,
        [vmem] * len(far_shapes),
        far_shapes,
        2 * owned * channels * halo,
        2 * owned * channels,
        [
            vmem((owned, channels), BF16),
            vmem((channels, channels), BF16),
            vmem((2, halo), jnp.int32),
            pltpu.SemaphoreType.DMA((4,)),
        ],
    )(hbm(mesh_rows), hbm(w_src), hbm(send_rows))
    far = [lax.ppermute(piece, "band", far_swap) for piece in far]

    src, *near = call(
        near_kernel,
        [vmem] * 3,
        [vmem] * (1 + len(near_shapes)),
        [sds((owned, channels), BF16), *near_shapes],
        *IN_SHADOW,
    )(mesh_rows, w_src, send_rows)
    near = [lax.ppermute(piece, "band", near_swap) for piece in near]

    [pre] = call(
        functools.partial(own_kernel, block),
        [vmem] * (6 + len(near)),
        [vmem],
        [sds((edges, points, channels), BF16)],
        *IN_SHADOW,
        [
            vmem((points // block, block, channels), F32),
            vmem((edges, lanes, channels), BF16),
            vmem((feats * edges, points), F32),
            vmem((halo, channels), BF16),
        ],
    )(slots, src, grid_rows, w_dst, edge_attr, w_edge, *near)

    chunks = 2
    part = points // chunks
    ahead = []
    for c in range(chunks):
        pred, pred_bf, sg, zhat, rstd = call(
            functools.partial(forward_kernel, c * part, block, owned, fields),
            [vmem] * (6 + len(far)),
            [vmem] * 5,
            [
                sds((fields, part), F32),
                sds((fields, part), BF16),
                sds((edges, part, channels), BF16),
                sds((part, channels), BF16),
                sds((part, lanes), F32),
            ],
            2 * part * channels * (edges * halo + channels),
            part * channels * edges * 4,
        )(slots, pre, grid_rows, w_msg, gain, w_out, *far)
        if members == 2:
            others = lax.ppermute(pred_bf, "member", [(0, 1), (1, 0)])[None]
        else:
            others = lax.all_gather(pred_bf[None], "member", axis=0, tiled=True)
        ahead.append((pred, others, sg, zhat, rstd))

    coeff = ALPHA / (members - 1) + (1.0 - ALPHA) / members
    far = []
    d_zs, d_pres = [], []
    for c, (pred, others, sg, zhat, rstd) in enumerate(ahead):
        rim_shapes = far_shapes if c == chunks - 1 else [sds((halo, channels), F32)]
        d_z, d_pre, *far = call(
            functools.partial(backward_kernel, c * part, block, owned, coeff, len(far)),
            [vmem] * (11 + len(far)),
            [vmem] * (2 + len(rim_shapes)),
            [sds((part, channels), BF16), sds((edges, part, channels), BF16), *rim_shapes],
            2 * part * channels * (edges * halo + channels),
            part * channels * edges * 4,
        )(slots, pred, others, target, weight, w_out, gain, zhat, rstd, w_msg, sg, *far)
        d_zs.append(d_z)
        d_pres.append(d_pre)
    far = [lax.ppermute(piece, "band", far_swap) for piece in far]

    near = call(
        functools.partial(rim_kernel, owned, chunks),
        [vmem] * (1 + chunks),
        [vmem] * len(near_shapes),
        near_shapes,
        *IN_SHADOW,
        [vmem((halo, channels), F32)],
    )(slots, *d_pres)
    near = [lax.ppermute(piece, "band", near_swap) for piece in near]

    d_grid, own = call(
        functools.partial(own_grad_kernel, chunks),
        [vmem] * (2 + 2 * chunks),
        [far_memory, vmem],
        [sds((points, channels), BF16), sds((owned, channels), F32)],
        *IN_SHADOW,
        [vmem((points, channels), BF16), pltpu.SemaphoreType.DMA((chunks,))],
    )(slots, w_dst, *[ref for pair in zip(d_zs, d_pres) for ref in pair])

    base, far_hot = call(
        merge_kernel,
        [vmem] * (3 + len(near)),
        [vmem] * 2,
        [sds((owned, channels), F32), sds((owned, halo), BF16)],
        *IN_SHADOW,
        [vmem((halo, channels), BF16)],
    )(send_rows, own, w_src, *near)

    [d_mesh] = call(
        mesh_kernel,
        [vmem] * (3 + len(far)),
        [far_memory],
        [sds((owned, channels), BF16)],
        2 * owned * channels * (channels + halo),
        owned * channels * 8,
        [
            vmem((halo, channels), BF16),
            vmem((owned, channels), BF16),
            pltpu.SemaphoreType.DMA((4,)),
        ],
    )(far_hot, base, w_src, *far)
    return (d_grid[None], d_mesh[None])


def solution(mesh):
    placed = (
        P("member", "band", None),
        P("member", "band", None),
        P(None, None, "band"),
        P("band", None),
        P("band", None),
        P(None, "band"),
        P(),
        P(),
        P(),
        P(),
        P(),
        P(),
        P(),
    )
    return jax.shard_map(
        per_device,
        mesh=mesh,
        in_specs=placed,
        out_specs=(P("member", "band", None), P("member", "band", None)),
        check_vma=False,
    )
```

```python
import functools

import jax
import jax.numpy as jnp
from jax import lax
from jax.experimental import pallas as pl
from jax.experimental.pallas import tpu as pltpu
from jax.sharding import PartitionSpec as P

DELTA_SQ = 0.0625
ALPHA = 0.95
LN_EPS = 1e-05
F32 = jnp.float32
BF16 = jnp.bfloat16
IN_SHADOW = (1, 1)
VMEM_LIMIT = 28 * 1024 * 1024


def slope(diff):
    return diff * lax.rsqrt(diff * diff + DELTA_SQ)


def mm(left, right):
    return jnp.dot(left, right, preferred_element_type=F32)


def mm_t(left, right):
    return lax.dot_general(left, right, (((1,), (1,)), ((), ())), preferred_element_type=F32)


def column_hot(ids, base, slots):
    lanes = 128
    rows = ids.shape[1]
    column = jnp.broadcast_to((ids - base).astype(F32), (lanes, rows)).T.astype(jnp.int16)
    lane = lax.broadcasted_iota(jnp.int16, (rows, lanes), 1)
    parts = [
        jnp.where(column == lane + jnp.int16(first), BF16(1), BF16(0))
        for first in range(0, slots, lanes)
    ]
    return jnp.concatenate(parts, axis=1)


def row_hot(ids, base, slots):
    row = (ids - base).astype(jnp.int16)
    return jnp.where(
        row == lax.broadcasted_iota(jnp.int16, (slots, ids.shape[1]), 0), BF16(1), BF16(0)
    )


def row_hots(ids, base, slots):
    return jnp.concatenate(
        [row_hot(ids[k : k + 1, :], base, slots) for k in range(ids.shape[0])], axis=1
    )


def swap(firsts):
    return [pair for i in firsts for pair in ((i, i + 1), (i + 1, i))]


def hbm(array):
    return pltpu.with_memory_space_constraint(array, pltpu.HBM)


def call(body, places, out_places, out_shape, flops, nbytes, scratch=()):
    def specs(memories):
        return [pl.BlockSpec(memory_space=memory) for memory in memories]

    return pl.pallas_call(
        body,
        in_specs=specs(places),
        out_specs=specs(out_places),
        out_shape=out_shape,
        scratch_shapes=scratch,
        compiler_params=pltpu.CompilerParams(vmem_limit_bytes=VMEM_LIMIT),
        cost_estimate=pl.CostEstimate(flops=flops, bytes_accessed=nbytes, transcendentals=0),
    )


def near_far(low, high):
    odd = lax.axis_index("band") % 2 == 1
    return jnp.where(odd, low, high), jnp.where(odd, high, low)


def rim_bases(owned, halo):
    return near_far(owned, owned + halo)


def rows_to(array, rows):
    array = array.astype(F32)
    return jnp.concatenate([array, jnp.zeros((rows - array.shape[0], array.shape[1]), F32)], axis=0)


def pieces(rows, size):
    return [slice(first, first + size) for first in range(0, rows, size)]


def placed_rows(refs):
    first, out = 0, []
    for ref in refs:
        out.append((slice(first, first + ref.shape[0]), ref))
        first += ref.shape[0]
    return out


def join(refs, whole_ref):
    for rows, ref in placed_rows(refs):
        whole_ref[rows, :] = ref[...]


def far_kernel(mesh_hbm, w_src_hbm, send_hbm, *refs):
    *far_refs, mesh_ref, w_src_ref, send_ref, sems = refs
    owned = mesh_ref.shape[0]
    parts = pieces(owned, owned // 2)
    lists = pltpu.make_async_copy(send_hbm, send_ref, sems.at[0])
    lists.start()
    loads = []
    for i, part in enumerate(parts):
        loads.append(pltpu.make_async_copy(mesh_hbm.at[part], mesh_ref.at[part], sems.at[2 + i]))
        loads[-1].start()
    weights = pltpu.make_async_copy(w_src_hbm, w_src_ref, sems.at[1])
    weights.start()
    lists.wait()
    far = near_far(send_ref[0:1, :], send_ref[1:2, :])[1]
    hots = [column_hot(far, part.start, part.stop - part.start) for part in parts]
    rows = None
    for load, part, hot in zip(loads, parts, hots):
        load.wait()
        picked = mm(hot, mesh_ref[part])
        rows = picked if rows is None else rows + picked
    weights.wait()
    rows = mm(rows.astype(BF16), w_src_ref[...]).astype(BF16)
    size = far_refs[0].shape[0]
    for i, far_ref in enumerate(far_refs):
        far_ref[...] = rows[i * size : (i + 1) * size, :]


def near_kernel(mesh_ref, w_src_ref, send_ref, src_ref, *near_refs):
    src = mm(mesh_ref[...], w_src_ref[...]).astype(BF16)
    src_ref[...] = src
    near = near_far(send_ref[0:1, :], send_ref[1:2, :])[0]
    rows = mm(column_hot(near, 0, src.shape[0]), src_ref[...]).astype(BF16)
    for part, near_ref in placed_rows(near_refs):
        near_ref[...] = rows[part, :]


def own_kernel(
    block,
    slots_ref,
    src_ref,
    grid_ref,
    w_dst_ref,
    attr_ref,
    w_edge_ref,
    *refs,
):
    *near_refs, pre_ref, dst_ref, embed_ref, attr_f32, near_ref = refs
    join(near_refs, near_ref)
    edges, lanes, channels = embed_ref.shape
    feats = w_edge_ref.shape[0]
    row = lax.broadcasted_iota(jnp.int32, (lanes, channels), 0)
    w_edge = w_edge_ref[...].astype(F32)
    for k in range(edges):
        spread = jnp.zeros((lanes, channels), F32)
        for e in range(feats):
            spread = jnp.where(row == e * edges + k, w_edge[e : e + 1, :], spread)
        embed_ref[k] = spread.astype(BF16)
    for e in range(feats):
        attr_f32[e * edges : (e + 1) * edges, :] = attr_ref[e].astype(F32)
    owned = src_ref.shape[0]
    halo = near_ref.shape[0]
    base = rim_bases(owned, halo)[0]
    for at, rows in enumerate(pieces(grid_ref.shape[0], block)):
        dst_ref[at] = mm(grid_ref[rows, :], w_dst_ref[...])
        attr = rows_to(attr_f32[:, rows], lanes).T.astype(BF16)
        for k in range(edges):
            ids = slots_ref[k : k + 1, rows]
            picked = mm(column_hot(ids, 0, owned), src_ref[...])
            picked = picked + mm(column_hot(ids, base, halo), near_ref[...])
            embed = mm(attr, embed_ref[k])
            pre_ref[k, rows, :] = (picked + embed + dst_ref[at]).astype(BF16)


def forward_kernel(
    first,
    block,
    owned,
    fields,
    slots_ref,
    pre_ref,
    grid_ref,
    w_msg_ref,
    gain_ref,
    w_out_ref,
    *refs,
):
    *far_refs, pred_ref, pred_bf_ref, sg_ref, zhat_ref, rstd_ref = refs
    half = BF16(0.5)
    size = far_refs[0].shape[0]
    base = rim_bases(owned, size * len(far_refs))[1]
    w_out = rows_to(w_out_ref[...], fields).astype(BF16)
    for rows in pieces(zhat_ref.shape[0], block):
        source = slice(first + rows.start, first + rows.stop)
        acts = []
        for k in range(slots_ref.shape[0]):
            ids = slots_ref[k : k + 1, source]
            picked = None
            for i, far_ref in enumerate(far_refs):
                rows_i = mm(column_hot(ids, base + i * size, size), far_ref[...])
                picked = rows_i if picked is None else picked + rows_i
            pre = pre_ref[k, source, :] + picked.astype(BF16)
            sigma = half + half * jnp.tanh(half * pre)
            act = pre * sigma
            acts.append(act)
            sg_ref[k, rows, :] = sigma + (act - act * sigma)
        while len(acts) > 1:
            acts = [sum(acts[i : i + 2][1:], acts[i]) for i in range(0, len(acts), 2)]
        z = grid_ref[source, :].astype(F32) + mm(acts[0], w_msg_ref[...])
        centre = z - jnp.mean(z, axis=1, keepdims=True)
        rstd = lax.rsqrt(jnp.mean(centre * centre, axis=1, keepdims=True) + LN_EPS)
        zhat = centre * rstd
        pred = mm_t(w_out, (zhat * gain_ref[...]).astype(BF16))
        pred_ref[:, rows] = pred
        pred_bf_ref[:, rows] = pred.astype(BF16)
        zhat_ref[rows, :] = zhat.astype(BF16)
        rstd_ref[rows, :] = jnp.broadcast_to(rstd, (block, rstd_ref.shape[1]))


def backward_kernel(
    first,
    block,
    owned,
    coeff,
    given,
    slots_ref,
    pred_ref,
    others_ref,
    target_ref,
    weight_ref,
    w_out_ref,
    gain_ref,
    zhat_ref,
    rstd_ref,
    w_msg_ref,
    sg_ref,
    *refs,
):
    prior, (dz_ref, dpre_ref, *far_refs) = refs[:given], refs[given:]
    fields = pred_ref.shape[0]
    weight = weight_ref[...]
    weight = jnp.concatenate([weight, jnp.zeros((1, fields - weight.shape[1]), F32)], axis=1)
    w_out = rows_to(w_out_ref[...], fields).astype(BF16)
    edges, points, channels = dpre_ref.shape
    for rows in pieces(points, block):
        source = slice(first + rows.start, first + rows.stop)
        pred = pred_ref[:, rows]
        spread = jnp.zeros_like(pred)
        for other in range(others_ref.shape[0]):
            spread = spread + slope(pred - others_ref[other, :, rows].astype(F32))
        d_pred = slope(pred - rows_to(target_ref[:, source], fields)) - coeff * spread
        d_pred = (weight * d_pred.T).astype(BF16)
        scaled = mm(d_pred, w_out) * gain_ref[...]
        zhat = zhat_ref[rows, :].astype(F32)
        d_z = rstd_ref[rows, :1] * (
            scaled
            - jnp.mean(scaled, axis=1, keepdims=True)
            - zhat * jnp.mean(scaled * zhat, axis=1, keepdims=True)
        )
        d_zb = d_z.astype(BF16)
        dz_ref[rows, :] = d_zb
        d_act = mm_t(d_zb, w_msg_ref[...]).astype(BF16)
        for k in range(edges):
            dpre_ref[k, rows, :] = d_act * sg_ref[k, rows, :]
    slots = slots_ref[:, first : first + points]
    d_pre = dpre_ref[...].reshape(edges * points, channels)
    size = far_refs[0].shape[0]
    halo = size * len(far_refs)
    far = mm(row_hots(slots, rim_bases(owned, halo)[1], halo), d_pre)
    if prior:
        far = far + prior[0][...]
    for i, far_ref in enumerate(far_refs):
        far_ref[...] = far[i * size : (i + 1) * size, :].astype(far_ref.dtype)


def rim_kernel(owned, chunks, slots_ref, *refs):
    dpre_refs = refs[:chunks]
    *near_refs, acc = refs[chunks:]
    base = rim_bases(owned, acc.shape[0])[0]
    first = 0
    for c, dpre_ref in enumerate(dpre_refs):
        edges, points, channels = dpre_ref.shape
        slots = slots_ref[:, first : first + points]
        first += points
        added = mm(
            row_hots(slots, base, acc.shape[0]), dpre_ref[...].reshape(edges * points, channels)
        )
        acc[...] = added if c == 0 else acc[...] + added
    for rows, near_ref in placed_rows(near_refs):
        near_ref[...] = acc[rows, :].astype(BF16)


def own_grad_kernel(chunks, slots_ref, w_dst_ref, *refs):
    grid_hbm, own_ref, grid_ref, sems = refs[-4:]
    owned = own_ref.shape[0]
    stores = []
    for c in range(chunks):
        dz_ref, dpre_ref = refs[2 * c : 2 * c + 2]
        points = dz_ref.shape[0]
        rows = slice(c * points, (c + 1) * points)
        d_sum = sum(dpre_ref[k].astype(F32) for k in range(dpre_ref.shape[0]))
        d_grid = dz_ref[...].astype(F32) + mm_t(d_sum.astype(BF16), w_dst_ref[...])
        grid_ref[rows, :] = d_grid.astype(BF16)
        stores.append(pltpu.make_async_copy(grid_ref.at[rows], grid_hbm.at[rows], sems.at[c]))
        stores[-1].start()
    for c in range(chunks):
        dpre_ref = refs[2 * c + 1]
        edges, points, channels = dpre_ref.shape
        slots = slots_ref[:, c * points : (c + 1) * points]
        d_pre = dpre_ref[...].reshape(edges * points, channels)
        added = mm(row_hots(slots, 0, owned), d_pre)
        own_ref[...] = added if c == 0 else own_ref[...] + added
    for store in stores:
        store.wait()


def merge_kernel(send_ref, own_ref, w_src_ref, *refs):
    *near_refs, base_ref, hot_ref, near_ref = refs
    join(near_refs, near_ref)
    owned = own_ref.shape[0]
    near, far = near_far(send_ref[0:1, :], send_ref[1:2, :])
    total = own_ref[...] + mm(row_hot(near, 0, owned), near_ref[...])
    base_ref[...] = mm_t(total.astype(BF16), w_src_ref[...])
    hot_ref[...] = row_hot(far, 0, owned)


def mesh_kernel(hot_ref, base_ref, w_src_ref, *refs):
    *far_refs, mesh_hbm, rows_ref, out_ref, sems = refs
    owned = base_ref.shape[0]
    size = far_refs[0].shape[0]
    for i, far_ref in enumerate(far_refs):
        rows_ref[i * size : (i + 1) * size, :] = mm_t(far_ref[...], w_src_ref[...]).astype(BF16)
    stores = []
    for i, part in enumerate(pieces(owned, owned // 4)):
        out = base_ref[part, :] + mm(hot_ref[part, :], rows_ref[...])
        out_ref[part, :] = out.astype(BF16)
        stores.append(pltpu.make_async_copy(out_ref.at[part], mesh_hbm.at[part], sems.at[i]))
        stores[-1].start()
    for store in stores:
        store.wait()


def per_device(
    grid_latent,
    mesh_latent,
    edge_attr,
    neighbours,
    send_rows,
    target,
    field_weight,
    w_src,
    w_dst,
    w_edge,
    w_msg,
    ln_gain,
    w_out,
):
    grid_rows = grid_latent[0]
    mesh_rows = mesh_latent[0]
    points, channels = grid_rows.shape
    owned = mesh_rows.shape[0]
    halo = send_rows.shape[1]
    edges = neighbours.shape[1]
    feats = w_edge.shape[0]
    lanes = 128
    fields = -(-w_out.shape[1] // lanes) * lanes
    block = min(points, 512)
    sds = jax.ShapeDtypeStruct
    members = lax.axis_size("member")
    bands = lax.axis_size("band")
    near_swap = swap(range(0, bands - 1, 2))
    far_swap = swap(range(1, bands - 1, 2))
    vmem, far_memory = pltpu.VMEM, pltpu.HBM
    slots = neighbours.T
    gain = ln_gain[None, :]
    w_out = w_out.T
    weight = field_weight[None, :]

    far_shapes = [sds((halo, channels), BF16)]
    near_shapes = [sds((halo // 2, channels), BF16)] * 2
    far = call(
        far_kernel,
        [far_memory] * 3,
        [vmem] * len(far_shapes),
        far_shapes,
        2 * owned * channels * halo,
        2 * owned * channels,
        [
            vmem((owned, channels), BF16),
            vmem((channels, channels), BF16),
            vmem((2, halo), jnp.int32),
            pltpu.SemaphoreType.DMA((4,)),
        ],
    )(hbm(mesh_rows), hbm(w_src), hbm(send_rows))
    far = [lax.ppermute(piece, "band", far_swap) for piece in far]

    src, *near = call(
        near_kernel,
        [vmem] * 3,
        [vmem] * (1 + len(near_shapes)),
        [sds((owned, channels), BF16), *near_shapes],
        *IN_SHADOW,
    )(mesh_rows, w_src, send_rows)
    near = [lax.ppermute(piece, "band", near_swap) for piece in near]

    [pre] = call(
        functools.partial(own_kernel, block),
        [vmem] * (6 + len(near)),
        [vmem],
        [sds((edges, points, channels), BF16)],
        *IN_SHADOW,
        [
            vmem((points // block, block, channels), F32),
            vmem((edges, lanes, channels), BF16),
            vmem((feats * edges, points), F32),
            vmem((halo, channels), BF16),
        ],
    )(slots, src, grid_rows, w_dst, edge_attr, w_edge, *near)

    chunks = 2
    part = points // chunks
    ahead = []
    for c in range(chunks):
        pred, pred_bf, sg, zhat, rstd = call(
            functools.partial(forward_kernel, c * part, block, owned, fields),
            [vmem] * (6 + len(far)),
            [vmem] * 5,
            [
                sds((fields, part), F32),
                sds((fields, part), BF16),
                sds((edges, part, channels), BF16),
                sds((part, channels), BF16),
                sds((part, lanes), F32),
            ],
            2 * part * channels * (edges * halo + channels),
            part * channels * edges * 4,
        )(slots, pre, grid_rows, w_msg, gain, w_out, *far)
        if members == 2:
            others = lax.ppermute(pred_bf, "member", [(0, 1), (1, 0)])[None]
        else:
            others = lax.all_gather(pred_bf[None], "member", axis=0, tiled=True)
        ahead.append((pred, others, sg, zhat, rstd))

    coeff = ALPHA / (members - 1) + (1.0 - ALPHA) / members
    far = []
    d_zs, d_pres = [], []
    for c, (pred, others, sg, zhat, rstd) in enumerate(ahead):
        rim_shapes = far_shapes if c == chunks - 1 else [sds((halo, channels), F32)]
        d_z, d_pre, *far = call(
            functools.partial(backward_kernel, c * part, block, owned, coeff, len(far)),
            [vmem] * (11 + len(far)),
            [vmem] * (2 + len(rim_shapes)),
            [sds((part, channels), BF16), sds((edges, part, channels), BF16), *rim_shapes],
            2 * part * channels * (edges * halo + channels),
            part * channels * edges * 4,
        )(slots, pred, others, target, weight, w_out, gain, zhat, rstd, w_msg, sg, *far)
        d_zs.append(d_z)
        d_pres.append(d_pre)
    far = [lax.ppermute(piece, "band", far_swap) for piece in far]

    near = call(
        functools.partial(rim_kernel, owned, chunks),
        [vmem] * (1 + chunks),
        [vmem] * len(near_shapes),
        near_shapes,
        *IN_SHADOW,
        [vmem((halo, channels), F32)],
    )(slots, *d_pres)
    near = [lax.ppermute(piece, "band", near_swap) for piece in near]

    d_grid, own = call(
        functools.partial(own_grad_kernel, chunks),
        [vmem] * (2 + 2 * chunks),
        [far_memory, vmem],
        [sds((points, channels), BF16), sds((owned, channels), F32)],
        *IN_SHADOW,
        [vmem((points, channels), BF16), pltpu.SemaphoreType.DMA((chunks,))],
    )(slots, w_dst, *[ref for pair in zip(d_zs, d_pres) for ref in pair])

    base, far_hot = call(
        merge_kernel,
        [vmem] * (3 + len(near)),
        [vmem] * 2,
        [sds((owned, channels), F32), sds((owned, halo), BF16)],
        *IN_SHADOW,
        [vmem((halo, channels), BF16)],
    )(send_rows, own, w_src, *near)

    [d_mesh] = call(
        mesh_kernel,
        [vmem] * (3 + len(far)),
        [far_memory],
        [sds((owned, channels), BF16)],
        2 * owned * channels * (channels + halo),
        owned * channels * 8,
        [
            vmem((halo, channels), BF16),
            vmem((owned, channels), BF16),
            pltpu.SemaphoreType.DMA((4,)),
        ],
    )(far_hot, base, w_src, *far)
    return (d_grid[None], d_mesh[None])


def solution(mesh):
    placed = (
        P("member", "band", None),
        P("member", "band", None),
        P(None, None, "band"),
        P("band", None),
        P("band", None),
        P(None, "band"),
        P(),
        P(),
        P(),
        P(),
        P(),
        P(),
        P(),
    )
    return jax.shard_map(
        per_device,
        mesh=mesh,
        in_specs=placed,
        out_specs=(P("member", "band", None), P("member", "band", None)),
        check_vma=False,
    )
```

```python
import functools

import jax
import jax.numpy as jnp
from jax import lax
from jax.experimental import pallas as pl
from jax.experimental.pallas import tpu as pltpu
from jax.sharding import PartitionSpec as P

DELTA_SQ = 0.0625
ALPHA = 0.95
LN_EPS = 1e-05
F32 = jnp.float32
BF16 = jnp.bfloat16
IN_SHADOW = (1, 1)
VMEM_LIMIT = 28 * 1024 * 1024


def slope(diff):
    return diff * lax.rsqrt(diff * diff + DELTA_SQ)


def mm(left, right):
    return jnp.dot(left, right, preferred_element_type=F32)


def mm_t(left, right):
    return lax.dot_general(left, right, (((1,), (1,)), ((), ())), preferred_element_type=F32)


def column_hot(ids, base, slots):
    lanes = 128
    rows = ids.shape[1]
    column = jnp.broadcast_to((ids - base).astype(F32), (lanes, rows)).T.astype(jnp.int16)
    lane = lax.broadcasted_iota(jnp.int16, (rows, lanes), 1)
    parts = [
        jnp.where(column == lane + jnp.int16(first), BF16(1), BF16(0))
        for first in range(0, slots, lanes)
    ]
    return jnp.concatenate(parts, axis=1)


def row_hot(ids, base, slots):
    row = (ids - base).astype(jnp.int16)
    return jnp.where(
        row == lax.broadcasted_iota(jnp.int16, (slots, ids.shape[1]), 0), BF16(1), BF16(0)
    )


def row_hots(ids, base, slots):
    return jnp.concatenate(
        [row_hot(ids[k : k + 1, :], base, slots) for k in range(ids.shape[0])], axis=1
    )


def swap(firsts):
    return [pair for i in firsts for pair in ((i, i + 1), (i + 1, i))]


def hbm(array):
    return pltpu.with_memory_space_constraint(array, pltpu.HBM)


def call(body, places, out_places, out_shape, flops, nbytes, scratch=()):
    def specs(memories):
        return [pl.BlockSpec(memory_space=memory) for memory in memories]

    return pl.pallas_call(
        body,
        in_specs=specs(places),
        out_specs=specs(out_places),
        out_shape=out_shape,
        scratch_shapes=scratch,
        compiler_params=pltpu.CompilerParams(vmem_limit_bytes=VMEM_LIMIT),
        cost_estimate=pl.CostEstimate(flops=flops, bytes_accessed=nbytes, transcendentals=0),
    )


def near_far(low, high):
    odd = lax.axis_index("band") % 2 == 1
    return jnp.where(odd, low, high), jnp.where(odd, high, low)


def rim_bases(owned, halo):
    return near_far(owned, owned + halo)


def rows_to(array, rows):
    array = array.astype(F32)
    return jnp.concatenate([array, jnp.zeros((rows - array.shape[0], array.shape[1]), F32)], axis=0)


def pieces(rows, size):
    return [slice(first, first + size) for first in range(0, rows, size)]


def placed_rows(refs):
    first, out = 0, []
    for ref in refs:
        out.append((slice(first, first + ref.shape[0]), ref))
        first += ref.shape[0]
    return out


def join(refs, whole_ref):
    for rows, ref in placed_rows(refs):
        whole_ref[rows, :] = ref[...]


def far_kernel(held, mesh_hbm, w_src_hbm, send_hbm, *refs):
    held_hbm, (far_ref, mesh_ref, w_src_ref, *held_refs) = refs[:held], refs[held:-2]
    send_ref, sems = refs[-2:]
    owned = mesh_ref.shape[0]
    parts = pieces(owned, owned // 2)
    moves = [(send_hbm, send_ref)]
    moves += [(mesh_hbm.at[part], mesh_ref.at[part]) for part in parts]
    moves += [(w_src_hbm, w_src_ref), *zip(held_hbm, held_refs)]
    loads = [pltpu.make_async_copy(*move, sems.at[i]) for i, move in enumerate(moves)]
    for load in loads:
        load.start()
    loads[0].wait()
    far = near_far(send_ref[0:1, :], send_ref[1:2, :])[1]
    hots = [column_hot(far, part.start, part.stop - part.start) for part in parts]
    rows = None
    for load, part, hot in zip(loads[1:], parts, hots):
        load.wait()
        picked = mm(hot, mesh_ref[part])
        rows = picked if rows is None else rows + picked
    loads[1 + len(parts)].wait()
    far_ref[...] = mm(rows.astype(BF16), w_src_ref[...]).astype(BF16)
    for load in loads[2 + len(parts) :]:
        load.wait()


def near_kernel(mesh_ref, w_src_ref, send_ref, src_ref, *near_refs):
    src = mm(mesh_ref[...], w_src_ref[...]).astype(BF16)
    src_ref[...] = src
    near = near_far(send_ref[0:1, :], send_ref[1:2, :])[0]
    rows = mm(column_hot(near, 0, src.shape[0]), src_ref[...]).astype(BF16)
    for part, near_ref in placed_rows(near_refs):
        near_ref[...] = rows[part, :]


def own_kernel(
    block,
    slots_ref,
    src_ref,
    grid_ref,
    w_dst_ref,
    attr_ref,
    w_edge_ref,
    *refs,
):
    *near_refs, pre_ref, dst_ref, embed_ref, attr_f32, near_ref = refs
    join(near_refs, near_ref)
    edges, lanes, channels = embed_ref.shape
    feats = w_edge_ref.shape[0]
    row = lax.broadcasted_iota(jnp.int32, (lanes, channels), 0)
    w_edge = w_edge_ref[...].astype(F32)
    for k in range(edges):
        spread = jnp.zeros((lanes, channels), F32)
        for e in range(feats):
            spread = jnp.where(row == e * edges + k, w_edge[e : e + 1, :], spread)
        embed_ref[k] = spread.astype(BF16)
    for e in range(feats):
        attr_f32[e * edges : (e + 1) * edges, :] = attr_ref[e].astype(F32)
    owned = src_ref.shape[0]
    halo = near_ref.shape[0]
    base = rim_bases(owned, halo)[0]
    for at, rows in enumerate(pieces(grid_ref.shape[0], block)):
        dst_ref[at] = mm(grid_ref[rows, :], w_dst_ref[...])
        attr = rows_to(attr_f32[:, rows], lanes).T.astype(BF16)
        for k in range(edges):
            ids = slots_ref[k : k + 1, rows]
            picked = mm(column_hot(ids, 0, owned), src_ref[...])
            picked = picked + mm(column_hot(ids, base, halo), near_ref[...])
            embed = mm(attr, embed_ref[k])
            pre_ref[k, rows, :] = (picked + embed + dst_ref[at]).astype(BF16)


def forward_kernel(
    first,
    block,
    owned,
    fields,
    slots_ref,
    pre_ref,
    grid_ref,
    w_msg_ref,
    gain_ref,
    w_out_ref,
    *refs,
):
    *far_refs, pred_ref, pred_bf_ref, sg_ref, zhat_ref, rstd_ref = refs
    half = BF16(0.5)
    size = far_refs[0].shape[0]
    base = rim_bases(owned, size * len(far_refs))[1]
    w_out = rows_to(w_out_ref[...], fields).astype(BF16)
    for rows in pieces(zhat_ref.shape[0], block):
        source = slice(first + rows.start, first + rows.stop)
        acts = []
        edges = slots_ref.shape[0]
        picked = None
        for i, far_ref in enumerate(far_refs):
            hots = [
                column_hot(slots_ref[k : k + 1, source], base + i * size, size)
                for k in range(edges)
            ]
            added = mm(jnp.concatenate(hots, axis=0), far_ref[...])
            picked = added if picked is None else picked + added
        for k in range(edges):
            pre = pre_ref[k, source, :] + picked[k * block : (k + 1) * block, :].astype(BF16)
            sigma = half + half * jnp.tanh(half * pre)
            act = pre * sigma
            acts.append(act)
            sg_ref[k, rows, :] = sigma + (act - act * sigma)
        while len(acts) > 1:
            acts = [sum(acts[i : i + 2][1:], acts[i]) for i in range(0, len(acts), 2)]
        z = grid_ref[source, :].astype(F32) + mm(acts[0], w_msg_ref[...])
        centre = z - jnp.mean(z, axis=1, keepdims=True)
        rstd = lax.rsqrt(jnp.mean(centre * centre, axis=1, keepdims=True) + LN_EPS)
        zhat = centre * rstd
        pred = mm_t(w_out, (zhat * gain_ref[...]).astype(BF16))
        pred_ref[:, rows] = pred
        pred_bf_ref[:, rows] = pred[: pred_bf_ref.shape[0], :].astype(BF16)
        zhat_ref[rows, :] = zhat.astype(BF16)
        rstd_ref[rows, :] = jnp.broadcast_to(rstd, (block, rstd_ref.shape[1]))


def backward_kernel(
    first,
    block,
    owned,
    coeff,
    given,
    slots_ref,
    pred_ref,
    others_ref,
    target_ref,
    weight_ref,
    w_out_ref,
    gain_ref,
    zhat_ref,
    rstd_ref,
    w_msg_ref,
    sg_ref,
    *refs,
):
    prior, (dz_ref, dpre_ref, *far_refs) = refs[:given], refs[given:]
    fields = pred_ref.shape[0]
    weight = weight_ref[...]
    weight = jnp.concatenate([weight, jnp.zeros((1, fields - weight.shape[1]), F32)], axis=1)
    w_out = rows_to(w_out_ref[...], fields).astype(BF16)
    edges, points, channels = dpre_ref.shape
    for rows in pieces(points, block):
        source = slice(first + rows.start, first + rows.stop)
        pred = pred_ref[:, rows]
        sent = others_ref.shape[1]
        spread = jnp.zeros((sent, block), F32)
        for other in range(others_ref.shape[0]):
            spread = spread + slope(pred[:sent, :] - others_ref[other, :, rows].astype(F32))
        d_pred = slope(pred - rows_to(target_ref[:, source], fields))
        d_pred = d_pred - coeff * rows_to(spread, fields)
        d_pred = (weight * d_pred.T).astype(BF16)
        scaled = mm(d_pred, w_out) * gain_ref[...]
        zhat = zhat_ref[rows, :].astype(F32)
        d_z = rstd_ref[rows, :1] * (
            scaled
            - jnp.mean(scaled, axis=1, keepdims=True)
            - zhat * jnp.mean(scaled * zhat, axis=1, keepdims=True)
        )
        d_zb = d_z.astype(BF16)
        dz_ref[rows, :] = d_zb
        d_act = mm_t(d_zb, w_msg_ref[...]).astype(BF16)
        for k in range(edges):
            dpre_ref[k, rows, :] = d_act * sg_ref[k, rows, :]
    slots = slots_ref[:, first : first + points]
    d_pre = dpre_ref[...].reshape(edges * points, channels)
    size = far_refs[0].shape[0]
    halo = size * len(far_refs)
    far = mm(row_hots(slots, rim_bases(owned, halo)[1], halo), d_pre)
    if prior:
        far = far + prior[0][...]
    for i, far_ref in enumerate(far_refs):
        far_ref[...] = far[i * size : (i + 1) * size, :].astype(far_ref.dtype)


def rim_kernel(owned, chunks, slots_ref, *refs):
    dpre_refs = refs[:chunks]
    *near_refs, acc = refs[chunks:]
    base = rim_bases(owned, acc.shape[0])[0]
    first = 0
    for c, dpre_ref in enumerate(dpre_refs):
        edges, points, channels = dpre_ref.shape
        slots = slots_ref[:, first : first + points]
        first += points
        added = mm(
            row_hots(slots, base, acc.shape[0]), dpre_ref[...].reshape(edges * points, channels)
        )
        acc[...] = added if c == 0 else acc[...] + added
    for rows, near_ref in placed_rows(near_refs):
        near_ref[...] = acc[rows, :].astype(BF16)


def own_grad_kernel(chunks, slots_ref, w_dst_ref, *refs):
    grid_hbm, own_ref, grid_ref, sems = refs[-4:]
    owned = own_ref.shape[0]
    stores = []
    for c in range(chunks):
        dz_ref, dpre_ref = refs[2 * c : 2 * c + 2]
        points = dz_ref.shape[0]
        rows = slice(c * points, (c + 1) * points)
        d_sum = sum(dpre_ref[k].astype(F32) for k in range(dpre_ref.shape[0]))
        d_grid = dz_ref[...].astype(F32) + mm_t(d_sum.astype(BF16), w_dst_ref[...])
        grid_ref[rows, :] = d_grid.astype(BF16)
        stores.append(pltpu.make_async_copy(grid_ref.at[rows], grid_hbm.at[rows], sems.at[c]))
        stores[-1].start()
    for c in range(chunks):
        dpre_ref = refs[2 * c + 1]
        edges, points, channels = dpre_ref.shape
        slots = slots_ref[:, c * points : (c + 1) * points]
        d_pre = dpre_ref[...].reshape(edges * points, channels)
        added = mm(row_hots(slots, 0, owned), d_pre)
        own_ref[...] = added if c == 0 else own_ref[...] + added
    for store in stores:
        store.wait()


def merge_kernel(send_ref, own_ref, w_src_ref, *refs):
    *near_refs, base_ref, hot_ref, near_ref = refs
    join(near_refs, near_ref)
    owned = own_ref.shape[0]
    near, far = near_far(send_ref[0:1, :], send_ref[1:2, :])
    total = own_ref[...] + mm(row_hot(near, 0, owned), near_ref[...])
    base_ref[...] = mm_t(total.astype(BF16), w_src_ref[...])
    hot_ref[...] = row_hot(far, 0, owned)


def mesh_kernel(hot_ref, base_ref, w_src_ref, *refs):
    *far_refs, mesh_hbm, rows_ref, out_ref, sems = refs
    owned = base_ref.shape[0]
    size = far_refs[0].shape[0]
    for i, far_ref in enumerate(far_refs):
        rows_ref[i * size : (i + 1) * size, :] = mm_t(far_ref[...], w_src_ref[...]).astype(BF16)
    stores = []
    for i, part in enumerate(pieces(owned, owned // 4)):
        out = base_ref[part, :] + mm(hot_ref[part, :], rows_ref[...])
        out_ref[part, :] = out.astype(BF16)
        stores.append(pltpu.make_async_copy(out_ref.at[part], mesh_hbm.at[part], sems.at[i]))
        stores[-1].start()
    for store in stores:
        store.wait()


def per_device(
    grid_latent,
    mesh_latent,
    edge_attr,
    neighbours,
    send_rows,
    target,
    field_weight,
    w_src,
    w_dst,
    w_edge,
    w_msg,
    ln_gain,
    w_out,
):
    grid_rows = grid_latent[0]
    mesh_rows = mesh_latent[0]
    points, channels = grid_rows.shape
    owned = mesh_rows.shape[0]
    halo = send_rows.shape[1]
    edges = neighbours.shape[1]
    feats = w_edge.shape[0]
    lanes = 128
    fields = -(-w_out.shape[1] // lanes) * lanes
    sent = -(-w_out.shape[1] // 16) * 16
    block = min(points, 512)
    sds = jax.ShapeDtypeStruct
    members = lax.axis_size("member")
    bands = lax.axis_size("band")
    near_swap = swap(range(0, bands - 1, 2))
    far_swap = swap(range(1, bands - 1, 2))
    vmem, far_memory = pltpu.VMEM, pltpu.HBM
    slots = neighbours.T
    gain = ln_gain[None, :]
    w_out = w_out.T
    weight = field_weight[None, :]

    far_shapes = [sds((halo, channels), BF16)]
    near_shapes = [sds((halo // 2, channels), BF16)] * 2
    held = [grid_rows, w_dst]
    *far, mesh_rows, w_src, grid_rows, w_dst = call(
        functools.partial(far_kernel, len(held)),
        [far_memory] * (3 + len(held)),
        [vmem] * (3 + len(held)),
        far_shapes + [sds(array.shape, BF16) for array in (mesh_rows, w_src, *held)],
        2 * owned * channels * halo,
        2 * owned * channels,
        [vmem((2, halo), jnp.int32), pltpu.SemaphoreType.DMA((4 + len(held),))],
    )(*map(hbm, (mesh_rows, w_src, send_rows, *held)))
    far = [lax.ppermute(piece, "band", far_swap) for piece in far]

    src, *near = call(
        near_kernel,
        [vmem] * 3,
        [vmem] * (1 + len(near_shapes)),
        [sds((owned, channels), BF16), *near_shapes],
        *IN_SHADOW,
    )(mesh_rows, w_src, send_rows)
    near = [lax.ppermute(piece, "band", near_swap) for piece in near]

    [pre] = call(
        functools.partial(own_kernel, block),
        [vmem] * (6 + len(near)),
        [vmem],
        [sds((edges, points, channels), BF16)],
        *IN_SHADOW,
        [
            vmem((points // block, block, channels), F32),
            vmem((edges, lanes, channels), BF16),
            vmem((feats * edges, points), F32),
            vmem((halo, channels), BF16),
        ],
    )(slots, src, grid_rows, w_dst, edge_attr, w_edge, *near)

    chunks = 2
    part = points // chunks
    ahead = []
    for c in range(chunks):
        pred, pred_bf, sg, zhat, rstd = call(
            functools.partial(forward_kernel, c * part, block, owned, fields),
            [vmem] * (6 + len(far)),
            [vmem] * 5,
            [
                sds((fields, part), F32),
                sds((sent, part), BF16),
                sds((edges, part, channels), BF16),
                sds((part, channels), BF16),
                sds((part, lanes), F32),
            ],
            2 * part * channels * (edges * halo + channels),
            part * channels * edges * 4,
        )(slots, pre, grid_rows, w_msg, gain, w_out, *far)
        if members == 2:
            others = lax.ppermute(pred_bf, "member", [(0, 1), (1, 0)])[None]
        else:
            others = lax.all_gather(pred_bf[None], "member", axis=0, tiled=True)
        ahead.append((pred, others, sg, zhat, rstd))

    coeff = ALPHA / (members - 1) + (1.0 - ALPHA) / members
    far = []
    d_zs, d_pres = [], []
    for c, (pred, others, sg, zhat, rstd) in enumerate(ahead):
        rim_shapes = far_shapes if c == chunks - 1 else [sds((halo, channels), F32)]
        d_z, d_pre, *far = call(
            functools.partial(backward_kernel, c * part, block, owned, coeff, len(far)),
            [vmem] * (11 + len(far)),
            [vmem] * (2 + len(rim_shapes)),
            [sds((part, channels), BF16), sds((edges, part, channels), BF16), *rim_shapes],
            2 * part * channels * (edges * halo + channels),
            part * channels * edges * 4,
        )(slots, pred, others, target, weight, w_out, gain, zhat, rstd, w_msg, sg, *far)
        d_zs.append(d_z)
        d_pres.append(d_pre)
    far = [lax.ppermute(piece, "band", far_swap) for piece in far]

    near = call(
        functools.partial(rim_kernel, owned, chunks),
        [vmem] * (1 + chunks),
        [vmem] * len(near_shapes),
        near_shapes,
        *IN_SHADOW,
        [vmem((halo, channels), F32)],
    )(slots, *d_pres)
    near = [lax.ppermute(piece, "band", near_swap) for piece in near]

    d_grid, own = call(
        functools.partial(own_grad_kernel, chunks),
        [vmem] * (2 + 2 * chunks),
        [far_memory, vmem],
        [sds((points, channels), BF16), sds((owned, channels), F32)],
        *IN_SHADOW,
        [vmem((points, channels), BF16), pltpu.SemaphoreType.DMA((chunks,))],
    )(slots, w_dst, *[ref for pair in zip(d_zs, d_pres) for ref in pair])

    base, far_hot = call(
        merge_kernel,
        [vmem] * (3 + len(near)),
        [vmem] * 2,
        [sds((owned, channels), F32), sds((owned, halo), BF16)],
        *IN_SHADOW,
        [vmem((halo, channels), BF16)],
    )(send_rows, own, w_src, *near)

    [d_mesh] = call(
        mesh_kernel,
        [vmem] * (3 + len(far)),
        [far_memory],
        [sds((owned, channels), BF16)],
        2 * owned * channels * (channels + halo),
        owned * channels * 8,
        [
            vmem((halo, channels), BF16),
            vmem((owned, channels), BF16),
            pltpu.SemaphoreType.DMA((4,)),
        ],
    )(far_hot, base, w_src, *far)
    return (d_grid[None], d_mesh[None])


def solution(mesh):
    placed = (
        P("member", "band", None),
        P("member", "band", None),
        P(None, None, "band"),
        P("band", None),
        P("band", None),
        P(None, "band"),
        P(),
        P(),
        P(),
        P(),
        P(),
        P(),
        P(),
    )
    return jax.shard_map(
        per_device,
        mesh=mesh,
        in_specs=placed,
        out_specs=(P("member", "band", None), P("member", "band", None)),
        check_vma=False,
    )
```

```python
import functools

import jax
import jax.numpy as jnp
from jax import lax
from jax.experimental import pallas as pl
from jax.experimental.pallas import tpu as pltpu
from jax.sharding import PartitionSpec as P

DELTA_SQ = 0.0625
ALPHA = 0.95
LN_EPS = 1e-05
F32 = jnp.float32
BF16 = jnp.bfloat16
IN_SHADOW = (1, 1)
VMEM_LIMIT = 28 * 1024 * 1024


def slope(diff):
    return diff * lax.rsqrt(diff * diff + DELTA_SQ)


def mm(left, right):
    return jnp.dot(left, right, preferred_element_type=F32)


def mm_t(left, right):
    return lax.dot_general(left, right, (((1,), (1,)), ((), ())), preferred_element_type=F32)


STRIP = 16


def strips(rows, size=STRIP):
    return [slice(first, first + size) for first in range(0, rows, size)]


def fill_columns(hot_ref, ids, base):
    lanes = 128
    rows = ids.shape[1]
    column = jnp.broadcast_to((ids - base).astype(F32), (lanes, rows)).T.astype(jnp.int16)
    lane = lax.broadcasted_iota(jnp.int16, (STRIP, lanes), 1)
    for part in strips(rows):
        offset = column[part, :] - lane
        for first in range(0, hot_ref.shape[1], lanes):
            hot_ref[part, first : first + lanes] = jnp.where(
                offset == jnp.int16(first), BF16(1), BF16(0)
            )


def fill_rows(hot_ref, ids, base):
    edges, points = ids.shape
    sublane = lax.broadcasted_iota(jnp.int16, (STRIP, points), 0)
    for k in range(edges):
        row = jnp.broadcast_to(ids[k : k + 1, :] - base, (STRIP, points)).astype(jnp.int16)
        offset = row - sublane
        for part in strips(hot_ref.shape[0]):
            hot_ref[part, k * points : (k + 1) * points] = jnp.where(
                offset == jnp.int16(part.start), BF16(1), BF16(0)
            )


def swap(firsts):
    return [pair for i in firsts for pair in ((i, i + 1), (i + 1, i))]


def hbm(array):
    return pltpu.with_memory_space_constraint(array, pltpu.HBM)


def call(body, places, out_places, out_shape, flops, nbytes, scratch=()):
    def specs(memories):
        return [pl.BlockSpec(memory_space=memory) for memory in memories]

    return pl.pallas_call(
        body,
        in_specs=specs(places),
        out_specs=specs(out_places),
        out_shape=out_shape,
        scratch_shapes=scratch,
        compiler_params=pltpu.CompilerParams(vmem_limit_bytes=VMEM_LIMIT),
        cost_estimate=pl.CostEstimate(flops=flops, bytes_accessed=nbytes, transcendentals=0),
    )


def near_far(low, high):
    odd = lax.axis_index("band") % 2 == 1
    return jnp.where(odd, low, high), jnp.where(odd, high, low)


def rim_bases(owned, halo):
    return near_far(owned, owned + halo)


def rows_to(array, rows):
    array = array.astype(F32)
    return jnp.concatenate([array, jnp.zeros((rows - array.shape[0], array.shape[1]), F32)], axis=0)


def pieces(rows, size):
    return [slice(first, first + size) for first in range(0, rows, size)]


def placed_rows(refs):
    first, out = 0, []
    for ref in refs:
        out.append((slice(first, first + ref.shape[0]), ref))
        first += ref.shape[0]
    return out


def join(refs, whole_ref):
    for rows, ref in placed_rows(refs):
        whole_ref[rows, :] = ref[...]


def far_kernel(held, mesh_hbm, w_src_hbm, send_hbm, *refs):
    held_hbm, (far_ref, mesh_ref, w_src_ref, *held_refs) = refs[:held], refs[held:-3]
    send_ref, hot_ref, sems = refs[-3:]
    owned = mesh_ref.shape[0]
    parts = pieces(owned, owned // 2)
    moves = [(send_hbm, send_ref)]
    moves += [(mesh_hbm.at[part], mesh_ref.at[part]) for part in parts]
    moves += [(w_src_hbm, w_src_ref), *zip(held_hbm, held_refs)]
    loads = [pltpu.make_async_copy(*move, sems.at[i]) for i, move in enumerate(moves)]
    for load in loads:
        load.start()
    loads[0].wait()
    far = near_far(send_ref[0:1, :], send_ref[1:2, :])[1]
    fill_columns(hot_ref, far, 0)
    rows = None
    for load, part in zip(loads[1:], parts):
        load.wait()
        picked = mm(hot_ref[:, part], mesh_ref[part])
        rows = picked if rows is None else rows + picked
    loads[1 + len(parts)].wait()
    far_ref[...] = mm(rows.astype(BF16), w_src_ref[...]).astype(BF16)
    for load in loads[2 + len(parts) :]:
        load.wait()


def near_kernel(mesh_ref, w_src_ref, send_ref, src_ref, *refs):
    *near_refs, hot_ref = refs
    src = mm(mesh_ref[...], w_src_ref[...]).astype(BF16)
    src_ref[...] = src
    near = near_far(send_ref[0:1, :], send_ref[1:2, :])[0]
    fill_columns(hot_ref, near, 0)
    rows = mm(hot_ref[...], src_ref[...]).astype(BF16)
    for part, near_ref in placed_rows(near_refs):
        near_ref[...] = rows[part, :]


def own_kernel(
    block,
    slots_ref,
    src_ref,
    grid_ref,
    w_dst_ref,
    attr_ref,
    w_edge_ref,
    *refs,
):
    *near_refs, pre_ref, dst_ref, embed_ref, attr_f32, near_ref, own_hot, near_hot, sum_ref = refs
    join(near_refs, near_ref)
    edges, lanes, channels = embed_ref.shape
    feats = w_edge_ref.shape[0]
    row = lax.broadcasted_iota(jnp.int32, (lanes, channels), 0)
    w_edge = w_edge_ref[...].astype(F32)
    for k in range(edges):
        spread = jnp.zeros((lanes, channels), F32)
        for e in range(feats):
            spread = jnp.where(row == e * edges + k, w_edge[e : e + 1, :], spread)
        embed_ref[k] = spread.astype(BF16)
    for e in range(feats):
        attr_f32[e * edges : (e + 1) * edges, :] = attr_ref[e].astype(F32)
    owned = src_ref.shape[0]
    halo = near_ref.shape[0]
    base = rim_bases(owned, halo)[0]
    for at, rows in enumerate(pieces(grid_ref.shape[0], block)):
        dst_ref[at] = mm(grid_ref[rows, :], w_dst_ref[...])
        attr = rows_to(attr_f32[:, rows], lanes).T.astype(BF16)
        for k in range(edges):
            ids = slots_ref[k : k + 1, rows]
            fill_columns(own_hot.at[k % 2], ids, 0)
            fill_columns(near_hot.at[k % 2], ids, base)
            picked = mm(own_hot[k % 2], src_ref[...]) + mm(near_hot[k % 2], near_ref[...])
            sum_ref[k % 2] = picked + mm(attr, embed_ref[k])
            for part in strips(block):
                at_rows = slice(rows.start + part.start, rows.start + part.stop)
                pre_ref[k, at_rows, :] = (sum_ref[k % 2, part, :] + dst_ref[at, part, :]).astype(BF16)


def forward_kernel(
    first,
    block,
    owned,
    fields,
    slots_ref,
    pre_ref,
    grid_ref,
    w_msg_ref,
    gain_ref,
    w_out_ref,
    far_ref,
    pred_ref,
    pred_bf_ref,
    sg_ref,
    zhat_ref,
    rstd_ref,
    hot_ref,
    picked_ref,
    act_ref,
    z_ref,
    u_ref,
):
    half = BF16(0.5)
    base = rim_bases(owned, far_ref.shape[0])[1]
    edges = slots_ref.shape[0]
    w_out = rows_to(w_out_ref[...], fields).astype(BF16)
    gain = gain_ref[...]
    for rows in pieces(zhat_ref.shape[0], block):
        source = slice(first + rows.start, first + rows.stop)
        for k in range(edges):
            fill_columns(hot_ref.at[k, rows], slots_ref[k : k + 1, source], base)
            picked_ref[k, rows, :] = mm(hot_ref[k, rows, :], far_ref[...])
        for part in strips(block):
            part = slice(rows.start + part.start, rows.start + part.stop)
            acts = []
            for k in range(edges):
                pre = pre_ref[k, first + part.start : first + part.stop, :]
                pre = pre + picked_ref[k, part, :].astype(BF16)
                sigma = half + half * jnp.tanh(half * pre)
                act = pre * sigma
                acts.append(act)
                sg_ref[k, part, :] = sigma + (act - act * sigma)
            while len(acts) > 1:
                acts = [sum(acts[i : i + 2][1:], acts[i]) for i in range(0, len(acts), 2)]
            act_ref[part, :] = acts[0]
        z_ref[rows, :] = mm(act_ref[rows, :], w_msg_ref[...])
        for part in strips(block, 32):
            part = slice(rows.start + part.start, rows.start + part.stop)
            z = grid_ref[first + part.start : first + part.stop, :].astype(F32) + z_ref[part, :]
            centre = z - jnp.mean(z, axis=1, keepdims=True)
            rstd = lax.rsqrt(jnp.mean(centre * centre, axis=1, keepdims=True) + LN_EPS)
            zhat = centre * rstd
            u_ref[part, :] = (zhat * gain).astype(BF16)
            zhat_ref[part, :] = zhat.astype(BF16)
            rstd_ref[part, :] = jnp.broadcast_to(rstd, (32, rstd_ref.shape[1]))
        pred = mm_t(w_out, u_ref[rows, :])
        pred_ref[:, rows] = pred
        pred_bf_ref[:, rows] = pred[: pred_bf_ref.shape[0], :].astype(BF16)


def backward_kernel(
    first,
    block,
    owned,
    coeff,
    given,
    slots_ref,
    pred_ref,
    others_ref,
    target_ref,
    weight_ref,
    w_out_ref,
    gain_ref,
    zhat_ref,
    rstd_ref,
    w_msg_ref,
    sg_ref,
    *refs,
):
    prior, (dz_ref, dpre_ref, far_ref, hot_ref, dpred_ref, wide_ref) = refs[:given], refs[given:]
    fields = pred_ref.shape[0]
    edges, points, channels = dpre_ref.shape
    slots = slots_ref[:, first : first + points]
    fill_rows(hot_ref, slots, rim_bases(owned, far_ref.shape[0])[1])
    weight = weight_ref[...]
    weight = jnp.concatenate([weight, jnp.zeros((1, fields - weight.shape[1]), F32)], axis=1)
    w_out = rows_to(w_out_ref[...], fields).astype(BF16)
    gain = gain_ref[...]
    sent = others_ref.shape[1]
    for rows in pieces(points, block):
        for part in strips(block, 128):
            part = slice(rows.start + part.start, rows.start + part.stop)
            pred = pred_ref[:, part]
            spread = jnp.zeros((sent, 128), F32)
            for other in range(others_ref.shape[0]):
                spread = spread + slope(pred[:sent, :] - others_ref[other, :, part].astype(F32))
            target = target_ref[:, first + part.start : first + part.stop]
            d_pred = slope(pred - rows_to(target, fields)) - coeff * rows_to(spread, fields)
            dpred_ref[part, :] = (weight * d_pred.T).astype(BF16)
        wide_ref[rows, :] = mm(dpred_ref[rows, :], w_out)
        for part in strips(block, 32):
            part = slice(rows.start + part.start, rows.start + part.stop)
            scaled = wide_ref[part, :] * gain
            zhat = zhat_ref[part, :].astype(F32)
            d_z = rstd_ref[part, :1] * (
                scaled
                - jnp.mean(scaled, axis=1, keepdims=True)
                - zhat * jnp.mean(scaled * zhat, axis=1, keepdims=True)
            )
            dz_ref[part, :] = d_z.astype(BF16)
        wide_ref[rows, :] = mm_t(dz_ref[rows, :], w_msg_ref[...])
        for part in strips(block):
            part = slice(rows.start + part.start, rows.start + part.stop)
            d_act = wide_ref[part, :].astype(BF16)
            for k in range(edges):
                dpre_ref[k, part, :] = d_act * sg_ref[k, part, :]
    far = mm(hot_ref[...], dpre_ref[...].reshape(edges * points, channels))
    if prior:
        far = far + prior[0][...]
    far_ref[...] = far.astype(far_ref.dtype)


def rim_kernel(owned, chunks, slots_ref, *refs):
    dpre_refs = refs[:chunks]
    *near_refs, acc, hot_ref = refs[chunks:]
    base = rim_bases(owned, acc.shape[0])[0]
    first = 0
    for c, dpre_ref in enumerate(dpre_refs):
        edges, points, channels = dpre_ref.shape
        fill_rows(hot_ref.at[c], slots_ref[:, first : first + points], base)
        first += points
        added = mm(hot_ref[c], dpre_ref[...].reshape(edges * points, channels))
        acc[...] = added if c == 0 else acc[...] + added
    for rows, near_ref in placed_rows(near_refs):
        near_ref[...] = acc[rows, :].astype(BF16)


def own_grad_kernel(chunks, slots_ref, w_dst_ref, *refs):
    grid_hbm, own_ref, grid_ref, dsum_ref, wide_ref, hot_ref, sems = refs[-7:]
    stores = []
    for c in range(chunks):
        dz_ref, dpre_ref = refs[2 * c : 2 * c + 2]
        edges, points, channels = dpre_ref.shape
        rows = slice(c * points, (c + 1) * points)
        for part in strips(points):
            d_sum = sum(dpre_ref[k, part, :].astype(F32) for k in range(edges))
            dsum_ref[part, :] = d_sum.astype(BF16)
        wide_ref[...] = mm_t(dsum_ref[...], w_dst_ref[...])
        for part in strips(points):
            d_grid = dz_ref[part, :].astype(F32) + wide_ref[part, :]
            grid_ref[rows.start + part.start : rows.start + part.stop, :] = d_grid.astype(BF16)
        stores.append(pltpu.make_async_copy(grid_ref.at[rows], grid_hbm.at[rows], sems.at[c]))
        stores[-1].start()
        fill_rows(hot_ref.at[c], slots_ref[:, rows], 0)
        added = mm(hot_ref[c], dpre_ref[...].reshape(edges * points, channels))
        own_ref[...] = added if c == 0 else own_ref[...] + added
    for store in stores:
        store.wait()


def merge_kernel(send_ref, own_ref, w_src_ref, *refs):
    *near_refs, base_ref, hot_ref, near_ref, near_hot = refs
    join(near_refs, near_ref)
    near, far = near_far(send_ref[0:1, :], send_ref[1:2, :])
    fill_rows(near_hot, near, 0)
    total = own_ref[...] + mm(near_hot[...], near_ref[...])
    base_ref[...] = mm_t(total.astype(BF16), w_src_ref[...])
    fill_rows(hot_ref, far, 0)


def mesh_kernel(hot_ref, base_ref, w_src_ref, *refs):
    *far_refs, mesh_hbm, rows_ref, out_ref, sems = refs
    owned = base_ref.shape[0]
    size = far_refs[0].shape[0]
    for i, far_ref in enumerate(far_refs):
        rows_ref[i * size : (i + 1) * size, :] = mm_t(far_ref[...], w_src_ref[...]).astype(BF16)
    stores = []
    for i, part in enumerate(pieces(owned, owned // 4)):
        out = base_ref[part, :] + mm(hot_ref[part, :], rows_ref[...])
        out_ref[part, :] = out.astype(BF16)
        stores.append(pltpu.make_async_copy(out_ref.at[part], mesh_hbm.at[part], sems.at[i]))
        stores[-1].start()
    for store in stores:
        store.wait()


def per_device(
    grid_latent,
    mesh_latent,
    edge_attr,
    neighbours,
    send_rows,
    target,
    field_weight,
    w_src,
    w_dst,
    w_edge,
    w_msg,
    ln_gain,
    w_out,
):
    grid_rows = grid_latent[0]
    mesh_rows = mesh_latent[0]
    points, channels = grid_rows.shape
    owned = mesh_rows.shape[0]
    halo = send_rows.shape[1]
    edges = neighbours.shape[1]
    feats = w_edge.shape[0]
    lanes = 128
    fields = -(-w_out.shape[1] // lanes) * lanes
    sent = -(-w_out.shape[1] // 16) * 16
    block = min(points, 512)
    sds = jax.ShapeDtypeStruct
    members = lax.axis_size("member")
    bands = lax.axis_size("band")
    near_swap = swap(range(0, bands - 1, 2))
    far_swap = swap(range(1, bands - 1, 2))
    vmem, far_memory = pltpu.VMEM, pltpu.HBM
    slots = neighbours.T
    gain = ln_gain[None, :]
    w_out = w_out.T
    weight = field_weight[None, :]

    far_shapes = [sds((halo, channels), BF16)]
    near_shapes = [sds((halo // 2, channels), BF16)] * 2
    held = [grid_rows, w_dst]
    *far, mesh_rows, w_src, grid_rows, w_dst = call(
        functools.partial(far_kernel, len(held)),
        [far_memory] * (3 + len(held)),
        [vmem] * (3 + len(held)),
        far_shapes + [sds(array.shape, BF16) for array in (mesh_rows, w_src, *held)],
        2 * owned * channels * halo,
        2 * owned * channels,
        [
            vmem((2, halo), jnp.int32),
            vmem((halo, owned), BF16),
            pltpu.SemaphoreType.DMA((4 + len(held),)),
        ],
    )(*map(hbm, (mesh_rows, w_src, send_rows, *held)))
    far = [lax.ppermute(piece, "band", far_swap) for piece in far]

    src, *near = call(
        near_kernel,
        [vmem] * 3,
        [vmem] * (1 + len(near_shapes)),
        [sds((owned, channels), BF16), *near_shapes],
        *IN_SHADOW,
        [vmem((halo, owned), BF16)],
    )(mesh_rows, w_src, send_rows)
    near = [lax.ppermute(piece, "band", near_swap) for piece in near]

    [pre] = call(
        functools.partial(own_kernel, block),
        [vmem] * (6 + len(near)),
        [vmem],
        [sds((edges, points, channels), BF16)],
        *IN_SHADOW,
        [
            vmem((points // block, block, channels), F32),
            vmem((edges, lanes, channels), BF16),
            vmem((feats * edges, points), F32),
            vmem((halo, channels), BF16),
            vmem((2, block, owned), BF16),
            vmem((2, block, halo), BF16),
            vmem((2, block, channels), F32),
        ],
    )(slots, src, grid_rows, w_dst, edge_attr, w_edge, *near)

    chunks = 2
    part = points // chunks
    ahead = []
    for c in range(chunks):
        pred, pred_bf, sg, zhat, rstd = call(
            functools.partial(forward_kernel, c * part, block, owned, fields),
            [vmem] * (6 + len(far)),
            [vmem] * 5,
            [
                sds((fields, part), F32),
                sds((sent, part), BF16),
                sds((edges, part, channels), BF16),
                sds((part, channels), BF16),
                sds((part, lanes), F32),
            ],
            2 * part * channels * (edges * halo + channels),
            part * channels * edges * 4,
            [
                vmem((edges, part, halo), BF16),
                vmem((edges, part, channels), F32),
                vmem((part, channels), BF16),
                vmem((part, channels), F32),
                vmem((part, channels), BF16),
            ],
        )(slots, pre, grid_rows, w_msg, gain, w_out, *far)
        if members == 2:
            others = lax.ppermute(pred_bf, "member", [(0, 1), (1, 0)])[None]
        else:
            others = lax.all_gather(pred_bf[None], "member", axis=0, tiled=True)
        ahead.append((pred, others, sg, zhat, rstd))

    coeff = ALPHA / (members - 1) + (1.0 - ALPHA) / members
    far = []
    d_zs, d_pres = [], []
    for c, (pred, others, sg, zhat, rstd) in enumerate(ahead):
        rim_shapes = far_shapes if c == chunks - 1 else [sds((halo, channels), F32)]
        d_z, d_pre, *far = call(
            functools.partial(backward_kernel, c * part, block, owned, coeff, len(far)),
            [vmem] * (11 + len(far)),
            [vmem] * (2 + len(rim_shapes)),
            [sds((part, channels), BF16), sds((edges, part, channels), BF16), *rim_shapes],
            2 * part * channels * (edges * halo + channels),
            part * channels * edges * 4,
            [
                vmem((halo, edges * part), BF16),
                vmem((part, fields), BF16),
                vmem((part, channels), F32),
            ],
        )(slots, pred, others, target, weight, w_out, gain, zhat, rstd, w_msg, sg, *far)
        d_zs.append(d_z)
        d_pres.append(d_pre)
    far = [lax.ppermute(piece, "band", far_swap) for piece in far]

    near = call(
        functools.partial(rim_kernel, owned, chunks),
        [vmem] * (1 + chunks),
        [vmem] * len(near_shapes),
        near_shapes,
        *IN_SHADOW,
        [vmem((halo, channels), F32), vmem((chunks, halo, edges * part), BF16)],
    )(slots, *d_pres)
    near = [lax.ppermute(piece, "band", near_swap) for piece in near]

    d_grid, own = call(
        functools.partial(own_grad_kernel, chunks),
        [vmem] * (2 + 2 * chunks),
        [far_memory, vmem],
        [sds((points, channels), BF16), sds((owned, channels), F32)],
        *IN_SHADOW,
        [
            vmem((points, channels), BF16),
            vmem((part, channels), BF16),
            vmem((part, channels), F32),
            vmem((chunks, owned, edges * part), BF16),
            pltpu.SemaphoreType.DMA((chunks,)),
        ],
    )(slots, w_dst, *[ref for pair in zip(d_zs, d_pres) for ref in pair])

    base, far_hot = call(
        merge_kernel,
        [vmem] * (3 + len(near)),
        [vmem] * 2,
        [sds((owned, channels), F32), sds((owned, halo), BF16)],
        *IN_SHADOW,
        [vmem((halo, channels), BF16), vmem((owned, halo), BF16)],
    )(send_rows, own, w_src, *near)

    [d_mesh] = call(
        mesh_kernel,
        [vmem] * (3 + len(far)),
        [far_memory],
        [sds((owned, channels), BF16)],
        2 * owned * channels * (channels + halo),
        owned * channels * 8,
        [
            vmem((halo, channels), BF16),
            vmem((owned, channels), BF16),
            pltpu.SemaphoreType.DMA((4,)),
        ],
    )(far_hot, base, w_src, *far)
    return (d_grid[None], d_mesh[None])


def solution(mesh):
    placed = (
        P("member", "band", None),
        P("member", "band", None),
        P(None, None, "band"),
        P("band", None),
        P("band", None),
        P(None, "band"),
        P(),
        P(),
        P(),
        P(),
        P(),
        P(),
        P(),
    )
    return jax.shard_map(
        per_device,
        mesh=mesh,
        in_specs=placed,
        out_specs=(P("member", "band", None), P("member", "band", None)),
        check_vma=False,
    )
```

```python
import functools

import jax
import jax.numpy as jnp
from jax import lax
from jax.experimental import pallas as pl
from jax.experimental.pallas import tpu as pltpu
from jax.sharding import PartitionSpec as P

DELTA_SQ = 0.0625
ALPHA = 0.95
LN_EPS = 1e-05
F32 = jnp.float32
BF16 = jnp.bfloat16
IN_SHADOW = (1, 1)
VMEM_LIMIT = 28 * 1024 * 1024


def slope(diff):
    return diff * lax.rsqrt(diff * diff + DELTA_SQ)


def mm(left, right):
    return jnp.dot(left, right, preferred_element_type=F32)


def mm_t(left, right):
    return lax.dot_general(left, right, (((1,), (1,)), ((), ())), preferred_element_type=F32)


STRIP = 16


def strips(rows, size=STRIP):
    return [slice(first, first + size) for first in range(0, rows, size)]


def column_of(ids):
    lanes = 128
    rows = ids.shape[1]
    column = jnp.broadcast_to(ids.astype(F32), (lanes, rows)).T.astype(jnp.int16)
    return column - lax.broadcasted_iota(jnp.int16, (rows, lanes), 1)


def column_hot(column, base, slots):
    offset = column - jnp.broadcast_to(base, column.shape).astype(jnp.int16)
    parts = [
        jnp.where(offset == jnp.int16(first), BF16(1), BF16(0))
        for first in range(0, slots, column.shape[1])
    ]
    return jnp.concatenate(parts, axis=1)


def fill_rows(hot_ref, ids, base):
    edges, points = ids.shape
    sublane = lax.broadcasted_iota(jnp.int16, (STRIP, points), 0)
    for k in range(edges):
        row = jnp.broadcast_to(ids[k : k + 1, :] - base, (STRIP, points)).astype(jnp.int16)
        offset = row - sublane
        for part in strips(hot_ref.shape[0]):
            hot_ref[part, k * points : (k + 1) * points] = jnp.where(
                offset == jnp.int16(part.start), BF16(1), BF16(0)
            )


def swap(firsts):
    return [pair for i in firsts for pair in ((i, i + 1), (i + 1, i))]


def hbm(array):
    return pltpu.with_memory_space_constraint(array, pltpu.HBM)


def call(body, places, out_places, out_shape, flops, nbytes, scratch=()):
    def specs(memories):
        return [pl.BlockSpec(memory_space=memory) for memory in memories]

    return pl.pallas_call(
        body,
        in_specs=specs(places),
        out_specs=specs(out_places),
        out_shape=out_shape,
        scratch_shapes=scratch,
        compiler_params=pltpu.CompilerParams(vmem_limit_bytes=VMEM_LIMIT),
        cost_estimate=pl.CostEstimate(flops=flops, bytes_accessed=nbytes, transcendentals=0),
    )


def near_far(low, high):
    odd = lax.axis_index("band") % 2 == 1
    return jnp.where(odd, low, high), jnp.where(odd, high, low)


def rim_bases(owned, halo):
    return near_far(owned, owned + halo)


def rows_to(array, rows):
    array = array.astype(F32)
    return jnp.concatenate([array, jnp.zeros((rows - array.shape[0], array.shape[1]), F32)], axis=0)


def pieces(rows, size):
    return [slice(first, first + size) for first in range(0, rows, size)]


def placed_rows(refs):
    first, out = 0, []
    for ref in refs:
        out.append((slice(first, first + ref.shape[0]), ref))
        first += ref.shape[0]
    return out


def join(refs, whole_ref):
    for rows, ref in placed_rows(refs):
        whole_ref[rows, :] = ref[...]


def far_kernel(held, mesh_hbm, w_src_hbm, send_hbm, *refs):
    held_hbm, (far_ref, mesh_ref, w_src_ref, *held_refs) = refs[:held], refs[held:-2]
    send_ref, sems = refs[-2:]
    owned = mesh_ref.shape[0]
    parts = pieces(owned, owned // 2)
    moves = [(send_hbm, send_ref)]
    moves += [(mesh_hbm.at[part], mesh_ref.at[part]) for part in parts]
    moves += [(w_src_hbm, w_src_ref), *zip(held_hbm, held_refs)]
    loads = [pltpu.make_async_copy(*move, sems.at[i]) for i, move in enumerate(moves)]
    for load in loads:
        load.start()
    loads[0].wait()
    far = near_far(send_ref[0:1, :], send_ref[1:2, :])[1]
    column = column_of(far)
    hots = [column_hot(column, part.start, part.stop - part.start) for part in parts]
    rows = None
    for load, part, hot in zip(loads[1:], parts, hots):
        load.wait()
        picked = mm(hot, mesh_ref[part])
        rows = picked if rows is None else rows + picked
    loads[1 + len(parts)].wait()
    far_ref[...] = mm(rows.astype(BF16), w_src_ref[...]).astype(BF16)
    for load in loads[2 + len(parts) :]:
        load.wait()


def near_kernel(mesh_ref, w_src_ref, send_ref, src_ref, *near_refs):
    src = mm(mesh_ref[...], w_src_ref[...]).astype(BF16)
    src_ref[...] = src
    near = near_far(send_ref[0:1, :], send_ref[1:2, :])[0]
    rows = mm(column_hot(column_of(near), 0, src.shape[0]), src_ref[...]).astype(BF16)
    for part, near_ref in placed_rows(near_refs):
        near_ref[...] = rows[part, :]


def own_kernel(
    block,
    slots_ref,
    src_ref,
    grid_ref,
    w_dst_ref,
    attr_ref,
    w_edge_ref,
    *refs,
):
    *near_refs, pre_ref, columns_ref, rows_ref, dst_ref, embed_ref, attr_f32, near_ref = refs
    join(near_refs, near_ref)
    edges, lanes, channels = embed_ref.shape
    feats = w_edge_ref.shape[0]
    row = lax.broadcasted_iota(jnp.int32, (lanes, channels), 0)
    w_edge = w_edge_ref[...].astype(F32)
    for k in range(edges):
        spread = jnp.zeros((lanes, channels), F32)
        for e in range(feats):
            spread = jnp.where(row == e * edges + k, w_edge[e : e + 1, :], spread)
        embed_ref[k] = spread.astype(BF16)
    for e in range(feats):
        attr_f32[e * edges : (e + 1) * edges, :] = attr_ref[e].astype(F32)
    owned = src_ref.shape[0]
    halo = near_ref.shape[0]
    base, far = rim_bases(owned, halo)
    for at, rows in enumerate(pieces(grid_ref.shape[0], block)):
        dst_ref[at] = mm(grid_ref[rows, :], w_dst_ref[...])
        attr = rows_to(attr_f32[:, rows], lanes).T.astype(BF16)
        for k in range(edges):
            column = column_of(slots_ref[k : k + 1, rows])
            picked = mm(column_hot(column, 0, owned), src_ref[...])
            picked = picked + mm(column_hot(column, base, halo), near_ref[...])
            embed = mm(attr, embed_ref[k])
            pre_ref[k, rows, :] = (picked + embed + dst_ref[at]).astype(BF16)
            columns_ref[k, rows, :] = column_hot(column, far, halo)
    chunks, _, width = rows_ref.shape
    part = width // edges
    for c in range(chunks):
        fill_rows(rows_ref.at[c], slots_ref[:, c * part : (c + 1) * part], far)


def forward_kernel(
    first,
    block,
    fields,
    columns_ref,
    pre_ref,
    grid_ref,
    w_msg_ref,
    gain_ref,
    w_out_ref,
    far_ref,
    pred_ref,
    pred_bf_ref,
    sg_ref,
    zhat_ref,
    rstd_ref,
):
    half = BF16(0.5)
    w_out = rows_to(w_out_ref[...], fields).astype(BF16)
    for rows in pieces(zhat_ref.shape[0], block):
        source = slice(first + rows.start, first + rows.stop)
        acts = []
        for k in range(columns_ref.shape[0]):
            picked = mm(columns_ref[k, source, :], far_ref[...])
            pre = pre_ref[k, source, :] + picked.astype(BF16)
            sigma = half + half * jnp.tanh(half * pre)
            act = pre * sigma
            acts.append(act)
            sg_ref[k, rows, :] = sigma + (act - act * sigma)
        while len(acts) > 1:
            acts = [sum(acts[i : i + 2][1:], acts[i]) for i in range(0, len(acts), 2)]
        z = grid_ref[source, :].astype(F32) + mm(acts[0], w_msg_ref[...])
        centre = z - jnp.mean(z, axis=1, keepdims=True)
        rstd = lax.rsqrt(jnp.mean(centre * centre, axis=1, keepdims=True) + LN_EPS)
        zhat = centre * rstd
        pred = mm_t(w_out, (zhat * gain_ref[...]).astype(BF16))
        pred_ref[:, rows] = pred
        pred_bf_ref[:, rows] = pred[: pred_bf_ref.shape[0], :].astype(BF16)
        zhat_ref[rows, :] = zhat.astype(BF16)
        rstd_ref[rows, :] = jnp.broadcast_to(rstd, (block, rstd_ref.shape[1]))


def backward_kernel(
    chunk,
    block,
    coeff,
    given,
    hot_ref,
    pred_ref,
    others_ref,
    target_ref,
    weight_ref,
    w_out_ref,
    gain_ref,
    zhat_ref,
    rstd_ref,
    w_msg_ref,
    sg_ref,
    *refs,
):
    prior, (dz_ref, dpre_ref, far_ref, dpred_ref, wide_ref) = refs[:given], refs[given:]
    fields = pred_ref.shape[0]
    edges, points, channels = dpre_ref.shape
    first = chunk * points
    weight = weight_ref[...]
    weight = jnp.concatenate([weight, jnp.zeros((1, fields - weight.shape[1]), F32)], axis=1)
    w_out = rows_to(w_out_ref[...], fields).astype(BF16)
    gain = gain_ref[...]
    sent = others_ref.shape[1]
    for rows in pieces(points, block):
        for part in strips(block, 128):
            part = slice(rows.start + part.start, rows.start + part.stop)
            pred = pred_ref[:, part]
            spread = jnp.zeros((sent, 128), F32)
            for other in range(others_ref.shape[0]):
                spread = spread + slope(pred[:sent, :] - others_ref[other, :, part].astype(F32))
            target = target_ref[:, first + part.start : first + part.stop]
            d_pred = slope(pred - rows_to(target, fields)) - coeff * rows_to(spread, fields)
            dpred_ref[part, :] = (weight * d_pred.T).astype(BF16)
        wide_ref[rows, :] = mm(dpred_ref[rows, :], w_out)
        for part in strips(block, 32):
            part = slice(rows.start + part.start, rows.start + part.stop)
            scaled = wide_ref[part, :] * gain
            zhat = zhat_ref[part, :].astype(F32)
            d_z = rstd_ref[part, :1] * (
                scaled
                - jnp.mean(scaled, axis=1, keepdims=True)
                - zhat * jnp.mean(scaled * zhat, axis=1, keepdims=True)
            )
            dz_ref[part, :] = d_z.astype(BF16)
        wide_ref[rows, :] = mm_t(dz_ref[rows, :], w_msg_ref[...])
        for part in strips(block):
            part = slice(rows.start + part.start, rows.start + part.stop)
            d_act = wide_ref[part, :].astype(BF16)
            for k in range(edges):
                dpre_ref[k, part, :] = d_act * sg_ref[k, part, :]
    far = mm(hot_ref[chunk], dpre_ref[...].reshape(edges * points, channels))
    if prior:
        far = far + prior[0][...]
    far_ref[...] = far.astype(far_ref.dtype)


def rim_kernel(owned, chunks, slots_ref, *refs):
    dpre_refs = refs[:chunks]
    *near_refs, acc, hot_ref = refs[chunks:]
    base = rim_bases(owned, acc.shape[0])[0]
    first = 0
    for c, dpre_ref in enumerate(dpre_refs):
        edges, points, channels = dpre_ref.shape
        fill_rows(hot_ref.at[c], slots_ref[:, first : first + points], base)
        first += points
        added = mm(hot_ref[c], dpre_ref[...].reshape(edges * points, channels))
        acc[...] = added if c == 0 else acc[...] + added
    for rows, near_ref in placed_rows(near_refs):
        near_ref[...] = acc[rows, :].astype(BF16)


def own_grad_kernel(chunks, slots_ref, w_dst_ref, *refs):
    grid_hbm, own_ref, grid_ref, dsum_ref, wide_ref, hot_ref, sems = refs[-7:]
    stores = []
    for c in range(chunks):
        dz_ref, dpre_ref = refs[2 * c : 2 * c + 2]
        edges, points, channels = dpre_ref.shape
        rows = slice(c * points, (c + 1) * points)
        for part in strips(points):
            d_sum = sum(dpre_ref[k, part, :].astype(F32) for k in range(edges))
            dsum_ref[part, :] = d_sum.astype(BF16)
        wide_ref[...] = mm_t(dsum_ref[...], w_dst_ref[...])
        for part in strips(points):
            d_grid = dz_ref[part, :].astype(F32) + wide_ref[part, :]
            grid_ref[rows.start + part.start : rows.start + part.stop, :] = d_grid.astype(BF16)
        stores.append(pltpu.make_async_copy(grid_ref.at[rows], grid_hbm.at[rows], sems.at[c]))
        stores[-1].start()
        fill_rows(hot_ref.at[c], slots_ref[:, rows], 0)
        added = mm(hot_ref[c], dpre_ref[...].reshape(edges * points, channels))
        own_ref[...] = added if c == 0 else own_ref[...] + added
    for store in stores:
        store.wait()


def merge_kernel(send_ref, own_ref, w_src_ref, *refs):
    *near_refs, base_ref, hot_ref, near_ref, near_hot = refs
    join(near_refs, near_ref)
    near, far = near_far(send_ref[0:1, :], send_ref[1:2, :])
    fill_rows(near_hot, near, 0)
    total = own_ref[...] + mm(near_hot[...], near_ref[...])
    base_ref[...] = mm_t(total.astype(BF16), w_src_ref[...])
    fill_rows(hot_ref, far, 0)


def mesh_kernel(hot_ref, base_ref, w_src_ref, *refs):
    *far_refs, mesh_hbm, rows_ref, out_ref, sems = refs
    owned = base_ref.shape[0]
    size = far_refs[0].shape[0]
    for i, far_ref in enumerate(far_refs):
        rows_ref[i * size : (i + 1) * size, :] = mm_t(far_ref[...], w_src_ref[...]).astype(BF16)
    stores = []
    for i, part in enumerate(pieces(owned, owned // 4)):
        out = base_ref[part, :] + mm(hot_ref[part, :], rows_ref[...])
        out_ref[part, :] = out.astype(BF16)
        stores.append(pltpu.make_async_copy(out_ref.at[part], mesh_hbm.at[part], sems.at[i]))
        stores[-1].start()
    for store in stores:
        store.wait()


def per_device(
    grid_latent,
    mesh_latent,
    edge_attr,
    neighbours,
    send_rows,
    target,
    field_weight,
    w_src,
    w_dst,
    w_edge,
    w_msg,
    ln_gain,
    w_out,
):
    grid_rows = grid_latent[0]
    mesh_rows = mesh_latent[0]
    points, channels = grid_rows.shape
    owned = mesh_rows.shape[0]
    halo = send_rows.shape[1]
    edges = neighbours.shape[1]
    feats = w_edge.shape[0]
    lanes = 128
    fields = -(-w_out.shape[1] // lanes) * lanes
    sent = -(-w_out.shape[1] // 16) * 16
    block = min(points, 512)
    sds = jax.ShapeDtypeStruct
    members = lax.axis_size("member")
    bands = lax.axis_size("band")
    near_swap = swap(range(0, bands - 1, 2))
    far_swap = swap(range(1, bands - 1, 2))
    vmem, far_memory = pltpu.VMEM, pltpu.HBM
    slots = neighbours.T
    gain = ln_gain[None, :]
    w_out = w_out.T
    weight = field_weight[None, :]

    far_shapes = [sds((halo, channels), BF16)]
    near_shapes = [sds((halo // 2, channels), BF16)] * 2
    held = [grid_rows, w_dst]
    *far, mesh_rows, w_src, grid_rows, w_dst = call(
        functools.partial(far_kernel, len(held)),
        [far_memory] * (3 + len(held)),
        [vmem] * (3 + len(held)),
        far_shapes + [sds(array.shape, BF16) for array in (mesh_rows, w_src, *held)],
        2 * owned * channels * halo,
        2 * owned * channels,
        [
            vmem((2, halo), jnp.int32),
            pltpu.SemaphoreType.DMA((4 + len(held),)),
        ],
    )(*map(hbm, (mesh_rows, w_src, send_rows, *held)))
    far = [lax.ppermute(piece, "band", far_swap) for piece in far]

    src, *near = call(
        near_kernel,
        [vmem] * 3,
        [vmem] * (1 + len(near_shapes)),
        [sds((owned, channels), BF16), *near_shapes],
        *IN_SHADOW,
    )(mesh_rows, w_src, send_rows)
    near = [lax.ppermute(piece, "band", near_swap) for piece in near]

    chunks = 2
    part = points // chunks
    pre, columns, rows = call(
        functools.partial(own_kernel, block),
        [vmem] * (6 + len(near)),
        [vmem] * 3,
        [
            sds((edges, points, channels), BF16),
            sds((edges, points, halo), BF16),
            sds((chunks, halo, edges * part), BF16),
        ],
        *IN_SHADOW,
        [
            vmem((points // block, block, channels), F32),
            vmem((edges, lanes, channels), BF16),
            vmem((feats * edges, points), F32),
            vmem((halo, channels), BF16),
        ],
    )(slots, src, grid_rows, w_dst, edge_attr, w_edge, *near)

    ahead = []
    for c in range(chunks):
        pred, pred_bf, sg, zhat, rstd = call(
            functools.partial(forward_kernel, c * part, block, fields),
            [vmem] * (6 + len(far)),
            [vmem] * 5,
            [
                sds((fields, part), F32),
                sds((sent, part), BF16),
                sds((edges, part, channels), BF16),
                sds((part, channels), BF16),
                sds((part, lanes), F32),
            ],
            2 * part * channels * (edges * halo + channels),
            part * channels * edges * 4,
        )(columns, pre, grid_rows, w_msg, gain, w_out, *far)
        if members == 2:
            others = lax.ppermute(pred_bf, "member", [(0, 1), (1, 0)])[None]
        else:
            others = lax.all_gather(pred_bf[None], "member", axis=0, tiled=True)
        ahead.append((pred, others, sg, zhat, rstd))

    coeff = ALPHA / (members - 1) + (1.0 - ALPHA) / members
    far = []
    d_zs, d_pres = [], []
    for c, (pred, others, sg, zhat, rstd) in enumerate(ahead):
        rim_shapes = far_shapes if c == chunks - 1 else [sds((halo, channels), F32)]
        d_z, d_pre, *far = call(
            functools.partial(backward_kernel, c, block, coeff, len(far)),
            [vmem] * (11 + len(far)),
            [vmem] * (2 + len(rim_shapes)),
            [sds((part, channels), BF16), sds((edges, part, channels), BF16), *rim_shapes],
            2 * part * channels * (edges * halo + channels),
            part * channels * edges * 4,
            [
                vmem((part, fields), BF16),
                vmem((part, channels), F32),
            ],
        )(rows, pred, others, target, weight, w_out, gain, zhat, rstd, w_msg, sg, *far)
        d_zs.append(d_z)
        d_pres.append(d_pre)
    far = [lax.ppermute(piece, "band", far_swap) for piece in far]

    near = call(
        functools.partial(rim_kernel, owned, chunks),
        [vmem] * (1 + chunks),
        [vmem] * len(near_shapes),
        near_shapes,
        *IN_SHADOW,
        [vmem((halo, channels), F32), vmem((chunks, halo, edges * part), BF16)],
    )(slots, *d_pres)
    near = [lax.ppermute(piece, "band", near_swap) for piece in near]

    d_grid, own = call(
        functools.partial(own_grad_kernel, chunks),
        [vmem] * (2 + 2 * chunks),
        [far_memory, vmem],
        [sds((points, channels), BF16), sds((owned, channels), F32)],
        *IN_SHADOW,
        [
            vmem((points, channels), BF16),
            vmem((part, channels), BF16),
            vmem((part, channels), F32),
            vmem((chunks, owned, edges * part), BF16),
            pltpu.SemaphoreType.DMA((chunks,)),
        ],
    )(slots, w_dst, *[ref for pair in zip(d_zs, d_pres) for ref in pair])

    base, far_hot = call(
        merge_kernel,
        [vmem] * (3 + len(near)),
        [vmem] * 2,
        [sds((owned, channels), F32), sds((owned, halo), BF16)],
        *IN_SHADOW,
        [vmem((halo, channels), BF16), vmem((owned, halo), BF16)],
    )(send_rows, own, w_src, *near)

    [d_mesh] = call(
        mesh_kernel,
        [vmem] * (3 + len(far)),
        [far_memory],
        [sds((owned, channels), BF16)],
        2 * owned * channels * (channels + halo),
        owned * channels * 8,
        [
            vmem((halo, channels), BF16),
            vmem((owned, channels), BF16),
            pltpu.SemaphoreType.DMA((4,)),
        ],
    )(far_hot, base, w_src, *far)
    return (d_grid[None], d_mesh[None])


def solution(mesh):
    placed = (
        P("member", "band", None),
        P("member", "band", None),
        P(None, None, "band"),
        P("band", None),
        P("band", None),
        P(None, "band"),
        P(),
        P(),
        P(),
        P(),
        P(),
        P(),
        P(),
    )
    return jax.shard_map(
        per_device,
        mesh=mesh,
        in_specs=placed,
        out_specs=(P("member", "band", None), P("member", "band", None)),
        check_vma=False,
    )
```

```python
import functools

import jax
import jax.numpy as jnp
from jax import lax
from jax.experimental import pallas as pl
from jax.experimental.pallas import tpu as pltpu
from jax.sharding import PartitionSpec as P

DELTA_SQ = 0.0625
ALPHA = 0.95
LN_EPS = 1e-05
F32 = jnp.float32
BF16 = jnp.bfloat16
IN_SHADOW = (1, 1)
VMEM_LIMIT = 28 * 1024 * 1024


def slope(diff):
    return diff * lax.rsqrt(diff * diff + DELTA_SQ)


def mm(left, right):
    return jnp.dot(left, right, preferred_element_type=F32)


def mm_t(left, right):
    return lax.dot_general(left, right, (((1,), (1,)), ((), ())), preferred_element_type=F32)


STRIP = 16


def strips(rows, size=STRIP):
    return [slice(first, first + size) for first in range(0, rows, size)]


def column_of(ids):
    lanes = 128
    rows = ids.shape[1]
    column = jnp.broadcast_to(ids.astype(F32), (lanes, rows)).T.astype(jnp.int16)
    return column - lax.broadcasted_iota(jnp.int16, (rows, lanes), 1)


def column_hot(column, base, slots):
    offset = column - jnp.broadcast_to(base, column.shape).astype(jnp.int16)
    parts = [
        jnp.where(offset == jnp.int16(first), BF16(1), BF16(0))
        for first in range(0, slots, column.shape[1])
    ]
    return jnp.concatenate(parts, axis=1)


def fill_rows(hot_ref, ids, base):
    edges, points = ids.shape
    sublane = lax.broadcasted_iota(jnp.int16, (STRIP, points), 0)
    for k in range(edges):
        row = jnp.broadcast_to(ids[k : k + 1, :] - base, (STRIP, points)).astype(jnp.int16)
        offset = row - sublane
        for part in strips(hot_ref.shape[0]):
            hot_ref[part, k * points : (k + 1) * points] = jnp.where(
                offset == jnp.int16(part.start), BF16(1), BF16(0)
            )


def swap(firsts):
    return [pair for i in firsts for pair in ((i, i + 1), (i + 1, i))]


def hbm(array):
    return pltpu.with_memory_space_constraint(array, pltpu.HBM)


def call(body, places, out_places, out_shape, flops, nbytes, scratch=()):
    def specs(memories):
        return [pl.BlockSpec(memory_space=memory) for memory in memories]

    return pl.pallas_call(
        body,
        in_specs=specs(places),
        out_specs=specs(out_places),
        out_shape=out_shape,
        scratch_shapes=scratch,
        compiler_params=pltpu.CompilerParams(vmem_limit_bytes=VMEM_LIMIT),
        cost_estimate=pl.CostEstimate(flops=flops, bytes_accessed=nbytes, transcendentals=0),
    )


def near_far(low, high):
    odd = lax.axis_index("band") % 2 == 1
    return jnp.where(odd, low, high), jnp.where(odd, high, low)


def rim_bases(owned, halo):
    return near_far(owned, owned + halo)


def rows_to(array, rows):
    array = array.astype(F32)
    return jnp.concatenate([array, jnp.zeros((rows - array.shape[0], array.shape[1]), F32)], axis=0)


def pieces(rows, size):
    return [slice(first, first + size) for first in range(0, rows, size)]


def placed_rows(refs):
    first, out = 0, []
    for ref in refs:
        out.append((slice(first, first + ref.shape[0]), ref))
        first += ref.shape[0]
    return out


def join(refs, whole_ref):
    for rows, ref in placed_rows(refs):
        whole_ref[rows, :] = ref[...]


def far_kernel(held, mesh_hbm, w_src_hbm, send_hbm, *refs):
    held_hbm, (far_ref, mesh_ref, w_src_ref, *held_refs) = refs[:held], refs[held:-2]
    send_ref, sems = refs[-2:]
    owned = mesh_ref.shape[0]
    parts = pieces(owned, owned // 2)
    moves = [(send_hbm, send_ref)]
    moves += [(mesh_hbm.at[part], mesh_ref.at[part]) for part in parts]
    moves += [(w_src_hbm, w_src_ref), *zip(held_hbm, held_refs)]
    loads = [pltpu.make_async_copy(*move, sems.at[i]) for i, move in enumerate(moves)]
    for load in loads:
        load.start()
    loads[0].wait()
    far = near_far(send_ref[0:1, :], send_ref[1:2, :])[1]
    column = column_of(far)
    hots = [column_hot(column, part.start, part.stop - part.start) for part in parts]
    rows = None
    for load, part, hot in zip(loads[1:], parts, hots):
        load.wait()
        picked = mm(hot, mesh_ref[part])
        rows = picked if rows is None else rows + picked
    loads[1 + len(parts)].wait()
    far_ref[...] = mm(rows.astype(BF16), w_src_ref[...]).astype(BF16)
    for load in loads[2 + len(parts) :]:
        load.wait()


def near_kernel(mesh_ref, w_src_ref, send_ref, src_ref, *near_refs):
    src = mm(mesh_ref[...], w_src_ref[...]).astype(BF16)
    src_ref[...] = src
    near = near_far(send_ref[0:1, :], send_ref[1:2, :])[0]
    rows = mm(column_hot(column_of(near), 0, src.shape[0]), src_ref[...]).astype(BF16)
    for part, near_ref in placed_rows(near_refs):
        near_ref[...] = rows[part, :]


def ready_kernel(owned, slots_ref, grid_ref, w_dst_ref, dst_ref, columns_ref, rows_ref):
    dst_ref[...] = mm(grid_ref[...], w_dst_ref[...])
    edges, _, halo = columns_ref.shape
    chunks, _, width = rows_ref.shape
    far = rim_bases(owned, halo)[1]
    part = width // edges
    for c in range(chunks):
        points = slice(c * part, (c + 1) * part)
        for k in range(edges):
            column = column_of(slots_ref[k : k + 1, points])
            columns_ref[k, points, :] = column_hot(column, far, halo)
        fill_rows(rows_ref.at[c], slots_ref[:, points], far)


def own_kernel(block, slots_ref, src_ref, dst_ref, attr_ref, w_edge_ref, *refs):
    *near_refs, pre_ref, embed_ref, attr_f32, near_ref = refs
    join(near_refs, near_ref)
    edges, lanes, channels = embed_ref.shape
    feats = w_edge_ref.shape[0]
    row = lax.broadcasted_iota(jnp.int32, (lanes, channels), 0)
    w_edge = w_edge_ref[...].astype(F32)
    for k in range(edges):
        spread = jnp.zeros((lanes, channels), F32)
        for e in range(feats):
            spread = jnp.where(row == e * edges + k, w_edge[e : e + 1, :], spread)
        embed_ref[k] = spread.astype(BF16)
    for e in range(feats):
        attr_f32[e * edges : (e + 1) * edges, :] = attr_ref[e].astype(F32)
    owned = src_ref.shape[0]
    halo = near_ref.shape[0]
    base = rim_bases(owned, halo)[0]
    for rows in pieces(dst_ref.shape[0], block):
        attr = rows_to(attr_f32[:, rows], lanes).T.astype(BF16)
        for k in range(edges):
            column = column_of(slots_ref[k : k + 1, rows])
            picked = mm(column_hot(column, 0, owned), src_ref[...])
            picked = picked + mm(column_hot(column, base, halo), near_ref[...])
            embed = mm(attr, embed_ref[k])
            pre_ref[k, rows, :] = (picked + embed + dst_ref[rows, :]).astype(BF16)


def forward_kernel(
    first,
    block,
    fields,
    columns_ref,
    pre_ref,
    grid_ref,
    w_msg_ref,
    gain_ref,
    w_out_ref,
    far_ref,
    pred_ref,
    pred_bf_ref,
    sg_ref,
    zhat_ref,
    rstd_ref,
):
    half = BF16(0.5)
    w_out = rows_to(w_out_ref[...], fields).astype(BF16)
    for rows in pieces(zhat_ref.shape[0], block):
        source = slice(first + rows.start, first + rows.stop)
        acts = []
        for k in range(columns_ref.shape[0]):
            picked = mm(columns_ref[k, source, :], far_ref[...])
            pre = pre_ref[k, source, :] + picked.astype(BF16)
            sigma = half + half * jnp.tanh(half * pre)
            act = pre * sigma
            acts.append(act)
            sg_ref[k, rows, :] = sigma + (act - act * sigma)
        while len(acts) > 1:
            acts = [sum(acts[i : i + 2][1:], acts[i]) for i in range(0, len(acts), 2)]
        z = grid_ref[source, :].astype(F32) + mm(acts[0], w_msg_ref[...])
        centre = z - jnp.mean(z, axis=1, keepdims=True)
        rstd = lax.rsqrt(jnp.mean(centre * centre, axis=1, keepdims=True) + LN_EPS)
        zhat = centre * rstd
        pred = mm_t(w_out, (zhat * gain_ref[...]).astype(BF16))
        pred_ref[:, rows] = pred
        pred_bf_ref[:, rows] = pred[: pred_bf_ref.shape[0], :].astype(BF16)
        zhat_ref[rows, :] = zhat.astype(BF16)
        rstd_ref[rows, :] = jnp.broadcast_to(rstd, (block, rstd_ref.shape[1]))


def backward_kernel(
    chunk,
    block,
    coeff,
    given,
    hot_ref,
    pred_ref,
    others_ref,
    target_ref,
    weight_ref,
    w_out_ref,
    gain_ref,
    zhat_ref,
    rstd_ref,
    w_msg_ref,
    sg_ref,
    *refs,
):
    prior, (dz_ref, dpre_ref, far_ref) = refs[:given], refs[given:]
    fields = pred_ref.shape[0]
    edges, points, channels = dpre_ref.shape
    first = chunk * points
    weight = weight_ref[...]
    weight = jnp.concatenate([weight, jnp.zeros((1, fields - weight.shape[1]), F32)], axis=1)
    w_out = rows_to(w_out_ref[...], fields).astype(BF16)
    gain = gain_ref[...]
    sent = others_ref.shape[1]
    for rows in pieces(points, block):
        source = slice(first + rows.start, first + rows.stop)
        pred = pred_ref[:, rows]
        spread = jnp.zeros((sent, block), F32)
        for other in range(others_ref.shape[0]):
            spread = spread + slope(pred[:sent, :] - others_ref[other, :, rows].astype(F32))
        d_pred = slope(pred - rows_to(target_ref[:, source], fields))
        d_pred = d_pred - coeff * rows_to(spread, fields)
        d_pred = (weight * d_pred.T).astype(BF16)
        scaled = mm(d_pred, w_out) * gain
        zhat = zhat_ref[rows, :].astype(F32)
        d_z = rstd_ref[rows, :1] * (
            scaled
            - jnp.mean(scaled, axis=1, keepdims=True)
            - zhat * jnp.mean(scaled * zhat, axis=1, keepdims=True)
        )
        d_zb = d_z.astype(BF16)
        dz_ref[rows, :] = d_zb
        d_act = mm_t(d_zb, w_msg_ref[...]).astype(BF16)
        for k in range(edges):
            dpre_ref[k, rows, :] = d_act * sg_ref[k, rows, :]
    far = mm(hot_ref[chunk], dpre_ref[...].reshape(edges * points, channels))
    if prior:
        far = far + prior[0][...]
    far_ref[...] = far.astype(far_ref.dtype)


def rim_kernel(owned, chunks, slots_ref, *refs):
    dpre_refs = refs[:chunks]
    *near_refs, acc, hot_ref = refs[chunks:]
    base = rim_bases(owned, acc.shape[0])[0]
    first = 0
    for c, dpre_ref in enumerate(dpre_refs):
        edges, points, channels = dpre_ref.shape
        fill_rows(hot_ref.at[c], slots_ref[:, first : first + points], base)
        first += points
        added = mm(hot_ref[c], dpre_ref[...].reshape(edges * points, channels))
        acc[...] = added if c == 0 else acc[...] + added
    for rows, near_ref in placed_rows(near_refs):
        near_ref[...] = acc[rows, :].astype(BF16)


def own_grad_kernel(chunks, slots_ref, w_dst_ref, *refs):
    grid_hbm, own_ref, grid_ref, dsum_ref, wide_ref, hot_ref, sems = refs[-7:]
    stores = []
    for c in range(chunks):
        dz_ref, dpre_ref = refs[2 * c : 2 * c + 2]
        edges, points, channels = dpre_ref.shape
        rows = slice(c * points, (c + 1) * points)
        for part in strips(points):
            d_sum = sum(dpre_ref[k, part, :].astype(F32) for k in range(edges))
            dsum_ref[part, :] = d_sum.astype(BF16)
        wide_ref[...] = mm_t(dsum_ref[...], w_dst_ref[...])
        for part in strips(points):
            d_grid = dz_ref[part, :].astype(F32) + wide_ref[part, :]
            grid_ref[rows.start + part.start : rows.start + part.stop, :] = d_grid.astype(BF16)
        stores.append(pltpu.make_async_copy(grid_ref.at[rows], grid_hbm.at[rows], sems.at[c]))
        stores[-1].start()
        fill_rows(hot_ref.at[c], slots_ref[:, rows], 0)
        added = mm(hot_ref[c], dpre_ref[...].reshape(edges * points, channels))
        own_ref[...] = added if c == 0 else own_ref[...] + added
    for store in stores:
        store.wait()


def merge_kernel(send_ref, own_ref, w_src_ref, *refs):
    *near_refs, base_ref, hot_ref, near_ref, near_hot = refs
    join(near_refs, near_ref)
    near, far = near_far(send_ref[0:1, :], send_ref[1:2, :])
    fill_rows(near_hot, near, 0)
    total = own_ref[...] + mm(near_hot[...], near_ref[...])
    base_ref[...] = mm_t(total.astype(BF16), w_src_ref[...])
    fill_rows(hot_ref, far, 0)


def mesh_kernel(hot_ref, base_ref, w_src_ref, *refs):
    *far_refs, mesh_hbm, rows_ref, out_ref, sems = refs
    owned = base_ref.shape[0]
    size = far_refs[0].shape[0]
    for i, far_ref in enumerate(far_refs):
        rows_ref[i * size : (i + 1) * size, :] = mm_t(far_ref[...], w_src_ref[...]).astype(BF16)
    stores = []
    for i, part in enumerate(pieces(owned, owned // 4)):
        out = base_ref[part, :] + mm(hot_ref[part, :], rows_ref[...])
        out_ref[part, :] = out.astype(BF16)
        stores.append(pltpu.make_async_copy(out_ref.at[part], mesh_hbm.at[part], sems.at[i]))
        stores[-1].start()
    for store in stores:
        store.wait()


def per_device(
    grid_latent,
    mesh_latent,
    edge_attr,
    neighbours,
    send_rows,
    target,
    field_weight,
    w_src,
    w_dst,
    w_edge,
    w_msg,
    ln_gain,
    w_out,
):
    grid_rows = grid_latent[0]
    mesh_rows = mesh_latent[0]
    points, channels = grid_rows.shape
    owned = mesh_rows.shape[0]
    halo = send_rows.shape[1]
    edges = neighbours.shape[1]
    feats = w_edge.shape[0]
    lanes = 128
    fields = -(-w_out.shape[1] // lanes) * lanes
    sent = -(-w_out.shape[1] // 16) * 16
    block = min(points, 512)
    sds = jax.ShapeDtypeStruct
    members = lax.axis_size("member")
    bands = lax.axis_size("band")
    near_swap = swap(range(0, bands - 1, 2))
    far_swap = swap(range(1, bands - 1, 2))
    vmem, far_memory = pltpu.VMEM, pltpu.HBM
    slots = neighbours.T
    gain = ln_gain[None, :]
    w_out = w_out.T
    weight = field_weight[None, :]

    far_shapes = [sds((halo, channels), BF16)]
    near_shapes = [sds((halo // 2, channels), BF16)] * 2
    held = [grid_rows, w_dst]
    *far, mesh_rows, w_src, grid_rows, w_dst = call(
        functools.partial(far_kernel, len(held)),
        [far_memory] * (3 + len(held)),
        [vmem] * (3 + len(held)),
        far_shapes + [sds(array.shape, BF16) for array in (mesh_rows, w_src, *held)],
        2 * owned * channels * halo,
        2 * owned * channels,
        [
            vmem((2, halo), jnp.int32),
            pltpu.SemaphoreType.DMA((4 + len(held),)),
        ],
    )(*map(hbm, (mesh_rows, w_src, send_rows, *held)))
    far = [lax.ppermute(piece, "band", far_swap) for piece in far]

    src, *near = call(
        near_kernel,
        [vmem] * 3,
        [vmem] * (1 + len(near_shapes)),
        [sds((owned, channels), BF16), *near_shapes],
        *IN_SHADOW,
    )(mesh_rows, w_src, send_rows)
    near = [lax.ppermute(piece, "band", near_swap) for piece in near]

    chunks = 2
    part = points // chunks
    dst, columns, rows = call(
        functools.partial(ready_kernel, owned),
        [vmem] * 3,
        [vmem] * 3,
        [
            sds((points, channels), F32),
            sds((edges, points, halo), BF16),
            sds((chunks, halo, edges * part), BF16),
        ],
        *IN_SHADOW,
    )(slots, grid_rows, w_dst)

    [pre] = call(
        functools.partial(own_kernel, block),
        [vmem] * (5 + len(near)),
        [vmem],
        [sds((edges, points, channels), BF16)],
        *IN_SHADOW,
        [
            vmem((edges, lanes, channels), BF16),
            vmem((feats * edges, points), F32),
            vmem((halo, channels), BF16),
        ],
    )(slots, src, dst, edge_attr, w_edge, *near)

    ahead = []
    for c in range(chunks):
        pred, pred_bf, sg, zhat, rstd = call(
            functools.partial(forward_kernel, c * part, block, fields),
            [vmem] * (6 + len(far)),
            [vmem] * 5,
            [
                sds((fields, part), F32),
                sds((sent, part), BF16),
                sds((edges, part, channels), BF16),
                sds((part, channels), BF16),
                sds((part, lanes), F32),
            ],
            2 * part * channels * (edges * halo + channels),
            part * channels * edges * 4,
        )(columns, pre, grid_rows, w_msg, gain, w_out, *far)
        if members == 2:
            others = lax.ppermute(pred_bf, "member", [(0, 1), (1, 0)])[None]
        else:
            others = lax.all_gather(pred_bf[None], "member", axis=0, tiled=True)
        ahead.append((pred, others, sg, zhat, rstd))

    coeff = ALPHA / (members - 1) + (1.0 - ALPHA) / members
    far = []
    d_zs, d_pres = [], []
    for c, (pred, others, sg, zhat, rstd) in enumerate(ahead):
        rim_shapes = far_shapes if c == chunks - 1 else [sds((halo, channels), F32)]
        d_z, d_pre, *far = call(
            functools.partial(backward_kernel, c, block, coeff, len(far)),
            [vmem] * (11 + len(far)),
            [vmem] * (2 + len(rim_shapes)),
            [sds((part, channels), BF16), sds((edges, part, channels), BF16), *rim_shapes],
            2 * part * channels * (edges * halo + channels),
            part * channels * edges * 4,
        )(rows, pred, others, target, weight, w_out, gain, zhat, rstd, w_msg, sg, *far)
        d_zs.append(d_z)
        d_pres.append(d_pre)
    far = [lax.ppermute(piece, "band", far_swap) for piece in far]

    near = call(
        functools.partial(rim_kernel, owned, chunks),
        [vmem] * (1 + chunks),
        [vmem] * len(near_shapes),
        near_shapes,
        *IN_SHADOW,
        [vmem((halo, channels), F32), vmem((chunks, halo, edges * part), BF16)],
    )(slots, *d_pres)
    near = [lax.ppermute(piece, "band", near_swap) for piece in near]

    d_grid, own = call(
        functools.partial(own_grad_kernel, chunks),
        [vmem] * (2 + 2 * chunks),
        [far_memory, vmem],
        [sds((points, channels), BF16), sds((owned, channels), F32)],
        *IN_SHADOW,
        [
            vmem((points, channels), BF16),
            vmem((part, channels), BF16),
            vmem((part, channels), F32),
            vmem((chunks, owned, edges * part), BF16),
            pltpu.SemaphoreType.DMA((chunks,)),
        ],
    )(slots, w_dst, *[ref for pair in zip(d_zs, d_pres) for ref in pair])

    base, far_hot = call(
        merge_kernel,
        [vmem] * (3 + len(near)),
        [vmem] * 2,
        [sds((owned, channels), F32), sds((owned, halo), BF16)],
        *IN_SHADOW,
        [vmem((halo, channels), BF16), vmem((owned, halo), BF16)],
    )(send_rows, own, w_src, *near)

    [d_mesh] = call(
        mesh_kernel,
        [vmem] * (3 + len(far)),
        [far_memory],
        [sds((owned, channels), BF16)],
        2 * owned * channels * (channels + halo),
        owned * channels * 8,
        [
            vmem((halo, channels), BF16),
            vmem((owned, channels), BF16),
            pltpu.SemaphoreType.DMA((4,)),
        ],
    )(far_hot, base, w_src, *far)
    return (d_grid[None], d_mesh[None])


def solution(mesh):
    placed = (
        P("member", "band", None),
        P("member", "band", None),
        P(None, None, "band"),
        P("band", None),
        P("band", None),
        P(None, "band"),
        P(),
        P(),
        P(),
        P(),
        P(),
        P(),
        P(),
    )
    return jax.shard_map(
        per_device,
        mesh=mesh,
        in_specs=placed,
        out_specs=(P("member", "band", None), P("member", "band", None)),
        check_vma=False,
    )
```

```python
import functools

import jax
import jax.numpy as jnp
from jax import lax
from jax.experimental import pallas as pl
from jax.experimental.pallas import tpu as pltpu
from jax.sharding import PartitionSpec as P

DELTA_SQ = 0.0625
ALPHA = 0.95
LN_EPS = 1e-05
F32 = jnp.float32
BF16 = jnp.bfloat16
IN_SHADOW = (1, 1)
VMEM_LIMIT = 28 * 1024 * 1024


def slope(diff):
    return diff * lax.rsqrt(diff * diff + DELTA_SQ)


def mm(left, right):
    return jnp.dot(left, right, preferred_element_type=F32)


def mm_t(left, right):
    return lax.dot_general(left, right, (((1,), (1,)), ((), ())), preferred_element_type=F32)


STRIP = 16


def strips(rows, size=STRIP):
    return [slice(first, first + size) for first in range(0, rows, size)]


def column_of(ids):
    lanes = 128
    rows = ids.shape[1]
    column = jnp.broadcast_to(ids.astype(F32), (lanes, rows)).T.astype(jnp.int16)
    return column - lax.broadcasted_iota(jnp.int16, (rows, lanes), 1)


def column_hot(column, base, slots):
    offset = column - jnp.broadcast_to(base, column.shape).astype(jnp.int16)
    parts = [
        jnp.where(offset == jnp.int16(first), BF16(1), BF16(0))
        for first in range(0, slots, column.shape[1])
    ]
    return jnp.concatenate(parts, axis=1)


def fill_rows(hot_ref, ids, base):
    edges, points = ids.shape
    sublane = lax.broadcasted_iota(jnp.int16, (STRIP, points), 0)
    for k in range(edges):
        row = jnp.broadcast_to(ids[k : k + 1, :] - base, (STRIP, points)).astype(jnp.int16)
        offset = row - sublane
        for part in strips(hot_ref.shape[0]):
            hot_ref[part, k * points : (k + 1) * points] = jnp.where(
                offset == jnp.int16(part.start), BF16(1), BF16(0)
            )


def swap(firsts):
    return [pair for i in firsts for pair in ((i, i + 1), (i + 1, i))]


def hbm(array):
    return pltpu.with_memory_space_constraint(array, pltpu.HBM)


def call(body, places, out_places, out_shape, flops, nbytes, scratch=()):
    def specs(memories):
        return [pl.BlockSpec(memory_space=memory) for memory in memories]

    return pl.pallas_call(
        body,
        in_specs=specs(places),
        out_specs=specs(out_places),
        out_shape=out_shape,
        scratch_shapes=scratch,
        compiler_params=pltpu.CompilerParams(vmem_limit_bytes=VMEM_LIMIT),
        cost_estimate=pl.CostEstimate(flops=flops, bytes_accessed=nbytes, transcendentals=0),
    )


def near_far(low, high):
    odd = lax.axis_index("band") % 2 == 1
    return jnp.where(odd, low, high), jnp.where(odd, high, low)


def rim_bases(owned, halo):
    return near_far(owned, owned + halo)


def rows_to(array, rows):
    array = array.astype(F32)
    return jnp.concatenate([array, jnp.zeros((rows - array.shape[0], array.shape[1]), F32)], axis=0)


def pieces(rows, size):
    return [slice(first, first + size) for first in range(0, rows, size)]


def placed_rows(refs):
    first, out = 0, []
    for ref in refs:
        out.append((slice(first, first + ref.shape[0]), ref))
        first += ref.shape[0]
    return out


def join(refs, whole_ref):
    for rows, ref in placed_rows(refs):
        whole_ref[rows, :] = ref[...]


def far_kernel(held, mesh_hbm, w_src_hbm, send_hbm, *refs):
    held_hbm, (far_ref, mesh_ref, w_src_ref, *held_refs) = refs[:held], refs[held:-2]
    send_ref, sems = refs[-2:]
    owned = mesh_ref.shape[0]
    parts = pieces(owned, owned // 2)
    moves = [(send_hbm, send_ref)]
    moves += [(mesh_hbm.at[part], mesh_ref.at[part]) for part in parts]
    moves += [(w_src_hbm, w_src_ref), *zip(held_hbm, held_refs)]
    loads = [pltpu.make_async_copy(*move, sems.at[i]) for i, move in enumerate(moves)]
    for load in loads:
        load.start()
    loads[0].wait()
    far = near_far(send_ref[0:1, :], send_ref[1:2, :])[1]
    column = column_of(far)
    hots = [column_hot(column, part.start, part.stop - part.start) for part in parts]
    rows = None
    for load, part, hot in zip(loads[1:], parts, hots):
        load.wait()
        picked = mm(hot, mesh_ref[part])
        rows = picked if rows is None else rows + picked
    loads[1 + len(parts)].wait()
    far_ref[...] = mm(rows.astype(BF16), w_src_ref[...]).astype(BF16)
    for load in loads[2 + len(parts) :]:
        load.wait()


def near_kernel(mesh_ref, w_src_ref, send_ref, src_ref, *near_refs):
    src = mm(mesh_ref[...], w_src_ref[...]).astype(BF16)
    src_ref[...] = src
    near = near_far(send_ref[0:1, :], send_ref[1:2, :])[0]
    rows = mm(column_hot(column_of(near), 0, src.shape[0]), src_ref[...]).astype(BF16)
    for part, near_ref in placed_rows(near_refs):
        near_ref[...] = rows[part, :]


def ready_kernel(
    owned,
    slots_ref,
    grid_ref,
    w_dst_ref,
    w_msg_ref,
    w_src_ref,
    w_out_ref,
    target_ref,
    weight_ref,
    dst_ref,
    columns_ref,
    rows_ref,
    w_msg_t_ref,
    w_src_t_ref,
    w_out_all_ref,
    target_all_ref,
    weight_all_ref,
):
    dst_ref[...] = mm(grid_ref[...], w_dst_ref[...])
    w_msg_t_ref[...] = w_msg_ref[...].T
    w_src_t_ref[...] = w_src_ref[...].T
    fields = target_all_ref.shape[0]
    w_out_all_ref[...] = rows_to(w_out_ref[...], fields).astype(BF16)
    target_all_ref[...] = rows_to(target_ref[...], fields)
    weight = weight_ref[...]
    weight_all_ref[...] = jnp.concatenate(
        [weight, jnp.zeros((1, fields - weight.shape[1]), F32)], axis=1
    )
    edges, _, halo = columns_ref.shape
    chunks, _, width = rows_ref.shape
    far = rim_bases(owned, halo)[1]
    part = width // edges
    for c in range(chunks):
        points = slice(c * part, (c + 1) * part)
        for k in range(edges):
            column = column_of(slots_ref[k : k + 1, points])
            columns_ref[k, points, :] = column_hot(column, far, halo)
        fill_rows(rows_ref.at[c], slots_ref[:, points], far)


def own_kernel(block, slots_ref, src_ref, dst_ref, attr_ref, w_edge_ref, *refs):
    *near_refs, pre_ref, embed_ref, attr_f32, near_ref = refs
    join(near_refs, near_ref)
    edges, lanes, channels = embed_ref.shape
    feats = w_edge_ref.shape[0]
    row = lax.broadcasted_iota(jnp.int32, (lanes, channels), 0)
    w_edge = w_edge_ref[...].astype(F32)
    for k in range(edges):
        spread = jnp.zeros((lanes, channels), F32)
        for e in range(feats):
            spread = jnp.where(row == e * edges + k, w_edge[e : e + 1, :], spread)
        embed_ref[k] = spread.astype(BF16)
    for e in range(feats):
        attr_f32[e * edges : (e + 1) * edges, :] = attr_ref[e].astype(F32)
    owned = src_ref.shape[0]
    halo = near_ref.shape[0]
    base = rim_bases(owned, halo)[0]
    for rows in pieces(dst_ref.shape[0], block):
        attr = rows_to(attr_f32[:, rows], lanes).T.astype(BF16)
        for k in range(edges):
            column = column_of(slots_ref[k : k + 1, rows])
            picked = mm(column_hot(column, 0, owned), src_ref[...])
            picked = picked + mm(column_hot(column, base, halo), near_ref[...])
            embed = mm(attr, embed_ref[k])
            pre_ref[k, rows, :] = (picked + embed + dst_ref[rows, :]).astype(BF16)


def forward_kernel(
    first,
    block,
    columns_ref,
    pre_ref,
    grid_ref,
    w_msg_ref,
    gain_ref,
    w_out_ref,
    far_ref,
    pred_ref,
    pred_bf_ref,
    sg_ref,
    zhat_ref,
    rstd_ref,
):
    half = BF16(0.5)
    for rows in pieces(zhat_ref.shape[0], block):
        source = slice(first + rows.start, first + rows.stop)
        acts = []
        for k in range(columns_ref.shape[0]):
            picked = mm(columns_ref[k, source, :], far_ref[...])
            pre = pre_ref[k, source, :] + picked.astype(BF16)
            sigma = half + half * jnp.tanh(half * pre)
            act = pre * sigma
            acts.append(act)
            sg_ref[k, rows, :] = sigma + (act - act * sigma)
        while len(acts) > 1:
            acts = [sum(acts[i : i + 2][1:], acts[i]) for i in range(0, len(acts), 2)]
        z = grid_ref[source, :].astype(F32) + mm(acts[0], w_msg_ref[...])
        centre = z - jnp.mean(z, axis=1, keepdims=True)
        rstd = lax.rsqrt(jnp.mean(centre * centre, axis=1, keepdims=True) + LN_EPS)
        zhat = centre * rstd
        pred = mm_t(w_out_ref[...], (zhat * gain_ref[...]).astype(BF16))
        pred_ref[:, rows] = pred
        pred_bf_ref[:, rows] = pred[: pred_bf_ref.shape[0], :].astype(BF16)
        zhat_ref[rows, :] = zhat.astype(BF16)
        rstd_ref[rows, :] = jnp.broadcast_to(rstd, (block, rstd_ref.shape[1]))


def backward_kernel(
    chunk,
    block,
    coeff,
    given,
    hot_ref,
    pred_ref,
    others_ref,
    target_ref,
    weight_ref,
    w_out_ref,
    gain_ref,
    zhat_ref,
    rstd_ref,
    w_msg_t_ref,
    sg_ref,
    *refs,
):
    prior, (dz_ref, dpre_ref, far_ref) = refs[:given], refs[given:]
    fields = pred_ref.shape[0]
    edges, points, channels = dpre_ref.shape
    first = chunk * points
    gain = gain_ref[...]
    sent = others_ref.shape[1]
    for rows in pieces(points, block):
        source = slice(first + rows.start, first + rows.stop)
        pred = pred_ref[:, rows]
        spread = jnp.zeros((sent, block), F32)
        for other in range(others_ref.shape[0]):
            spread = spread + slope(pred[:sent, :] - others_ref[other, :, rows].astype(F32))
        d_pred = slope(pred - target_ref[:, source])
        d_pred = d_pred - coeff * rows_to(spread, fields)
        d_pred = (weight_ref[...] * d_pred.T).astype(BF16)
        scaled = mm(d_pred, w_out_ref[...]) * gain
        zhat = zhat_ref[rows, :].astype(F32)
        d_z = rstd_ref[rows, :1] * (
            scaled
            - jnp.mean(scaled, axis=1, keepdims=True)
            - zhat * jnp.mean(scaled * zhat, axis=1, keepdims=True)
        )
        d_zb = d_z.astype(BF16)
        dz_ref[rows, :] = d_zb
        d_act = mm(d_zb, w_msg_t_ref[...]).astype(BF16)
        for k in range(edges):
            dpre_ref[k, rows, :] = d_act * sg_ref[k, rows, :]
    far = mm(hot_ref[chunk], dpre_ref[...].reshape(edges * points, channels))
    if prior:
        far = far + prior[0][...]
    far_ref[...] = far.astype(far_ref.dtype)


def rim_kernel(owned, chunks, slots_ref, *refs):
    dpre_refs = refs[:chunks]
    *near_refs, acc, hot_ref = refs[chunks:]
    base = rim_bases(owned, acc.shape[0])[0]
    first = 0
    for c, dpre_ref in enumerate(dpre_refs):
        edges, points, channels = dpre_ref.shape
        fill_rows(hot_ref.at[c], slots_ref[:, first : first + points], base)
        first += points
        added = mm(hot_ref[c], dpre_ref[...].reshape(edges * points, channels))
        acc[...] = added if c == 0 else acc[...] + added
    for rows, near_ref in placed_rows(near_refs):
        near_ref[...] = acc[rows, :].astype(BF16)


def own_grad_kernel(chunks, slots_ref, w_dst_ref, *refs):
    grid_hbm, own_ref, grid_ref, dsum_ref, wide_ref, hot_ref, sems = refs[-7:]
    stores = []
    for c in range(chunks):
        dz_ref, dpre_ref = refs[2 * c : 2 * c + 2]
        edges, points, channels = dpre_ref.shape
        rows = slice(c * points, (c + 1) * points)
        for part in strips(points):
            d_sum = sum(dpre_ref[k, part, :].astype(F32) for k in range(edges))
            dsum_ref[part, :] = d_sum.astype(BF16)
        wide_ref[...] = mm_t(dsum_ref[...], w_dst_ref[...])
        for part in strips(points):
            d_grid = dz_ref[part, :].astype(F32) + wide_ref[part, :]
            grid_ref[rows.start + part.start : rows.start + part.stop, :] = d_grid.astype(BF16)
        stores.append(pltpu.make_async_copy(grid_ref.at[rows], grid_hbm.at[rows], sems.at[c]))
        stores[-1].start()
        fill_rows(hot_ref.at[c], slots_ref[:, rows], 0)
        added = mm(hot_ref[c], dpre_ref[...].reshape(edges * points, channels))
        own_ref[...] = added if c == 0 else own_ref[...] + added
    for store in stores:
        store.wait()


def merge_kernel(send_ref, own_ref, w_src_t_ref, *refs):
    *near_refs, base_ref, hot_ref, near_ref, near_hot = refs
    join(near_refs, near_ref)
    near, far = near_far(send_ref[0:1, :], send_ref[1:2, :])
    fill_rows(near_hot, near, 0)
    total = own_ref[...] + mm(near_hot[...], near_ref[...])
    base_ref[...] = mm(total.astype(BF16), w_src_t_ref[...])
    fill_rows(hot_ref, far, 0)


def mesh_kernel(hot_ref, base_ref, w_src_t_ref, *refs):
    *far_refs, mesh_hbm, rows_ref, out_ref, sems = refs
    owned = base_ref.shape[0]
    size = far_refs[0].shape[0]
    for i, far_ref in enumerate(far_refs):
        rows_ref[i * size : (i + 1) * size, :] = mm(far_ref[...], w_src_t_ref[...]).astype(BF16)
    stores = []
    for i, part in enumerate(pieces(owned, owned // 4)):
        out = base_ref[part, :] + mm(hot_ref[part, :], rows_ref[...])
        out_ref[part, :] = out.astype(BF16)
        stores.append(pltpu.make_async_copy(out_ref.at[part], mesh_hbm.at[part], sems.at[i]))
        stores[-1].start()
    for store in stores:
        store.wait()


def per_device(
    grid_latent,
    mesh_latent,
    edge_attr,
    neighbours,
    send_rows,
    target,
    field_weight,
    w_src,
    w_dst,
    w_edge,
    w_msg,
    ln_gain,
    w_out,
):
    grid_rows = grid_latent[0]
    mesh_rows = mesh_latent[0]
    points, channels = grid_rows.shape
    owned = mesh_rows.shape[0]
    halo = send_rows.shape[1]
    edges = neighbours.shape[1]
    feats = w_edge.shape[0]
    lanes = 128
    fields = -(-w_out.shape[1] // lanes) * lanes
    sent = -(-w_out.shape[1] // 16) * 16
    block = min(points, 512)
    sds = jax.ShapeDtypeStruct
    members = lax.axis_size("member")
    bands = lax.axis_size("band")
    near_swap = swap(range(0, bands - 1, 2))
    far_swap = swap(range(1, bands - 1, 2))
    vmem, far_memory = pltpu.VMEM, pltpu.HBM
    slots = neighbours.T
    gain = ln_gain[None, :]
    w_out = w_out.T
    weight = field_weight[None, :]

    far_shapes = [sds((halo, channels), BF16)]
    near_shapes = [sds((halo // 2, channels), BF16)] * 2
    held = [grid_rows, w_dst, w_msg, target]
    *far, mesh_rows, w_src, grid_rows, w_dst, w_msg, target = call(
        functools.partial(far_kernel, len(held)),
        [far_memory] * (3 + len(held)),
        [vmem] * (3 + len(held)),
        far_shapes + [sds(array.shape, array.dtype) for array in (mesh_rows, w_src, *held)],
        2 * owned * channels * halo,
        2 * owned * channels,
        [
            vmem((2, halo), jnp.int32),
            pltpu.SemaphoreType.DMA((4 + len(held),)),
        ],
    )(*map(hbm, (mesh_rows, w_src, send_rows, *held)))
    far = [lax.ppermute(piece, "band", far_swap) for piece in far]

    src, *near = call(
        near_kernel,
        [vmem] * 3,
        [vmem] * (1 + len(near_shapes)),
        [sds((owned, channels), BF16), *near_shapes],
        *IN_SHADOW,
    )(mesh_rows, w_src, send_rows)
    near = [lax.ppermute(piece, "band", near_swap) for piece in near]

    chunks = 2
    part = points // chunks
    dst, columns, rows, w_msg_t, w_src_t, w_out, target, weight = call(
        functools.partial(ready_kernel, owned),
        [vmem] * 8,
        [vmem] * 8,
        [
            sds((points, channels), F32),
            sds((edges, points, halo), BF16),
            sds((chunks, halo, edges * part), BF16),
            sds(w_msg.shape, BF16),
            sds(w_src.shape, BF16),
            sds((fields, channels), BF16),
            sds((fields, points), F32),
            sds((1, fields), F32),
        ],
        *IN_SHADOW,
    )(slots, grid_rows, w_dst, w_msg, w_src, w_out, target, weight)

    [pre] = call(
        functools.partial(own_kernel, block),
        [vmem] * (5 + len(near)),
        [vmem],
        [sds((edges, points, channels), BF16)],
        *IN_SHADOW,
        [
            vmem((edges, lanes, channels), BF16),
            vmem((feats * edges, points), F32),
            vmem((halo, channels), BF16),
        ],
    )(slots, src, dst, edge_attr, w_edge, *near)

    ahead = []
    for c in range(chunks):
        pred, pred_bf, sg, zhat, rstd = call(
            functools.partial(forward_kernel, c * part, block),
            [vmem] * (6 + len(far)),
            [vmem] * 5,
            [
                sds((fields, part), F32),
                sds((sent, part), BF16),
                sds((edges, part, channels), BF16),
                sds((part, channels), BF16),
                sds((part, lanes), F32),
            ],
            2 * part * channels * (edges * halo + channels),
            part * channels * edges * 4,
        )(columns, pre, grid_rows, w_msg, gain, w_out, *far)
        if members == 2:
            others = lax.ppermute(pred_bf, "member", [(0, 1), (1, 0)])[None]
        else:
            others = lax.all_gather(pred_bf[None], "member", axis=0, tiled=True)
        ahead.append((pred, others, sg, zhat, rstd))

    coeff = ALPHA / (members - 1) + (1.0 - ALPHA) / members
    far = []
    d_zs, d_pres = [], []
    for c, (pred, others, sg, zhat, rstd) in enumerate(ahead):
        rim_shapes = far_shapes if c == chunks - 1 else [sds((halo, channels), F32)]
        d_z, d_pre, *far = call(
            functools.partial(backward_kernel, c, block, coeff, len(far)),
            [vmem] * (11 + len(far)),
            [vmem] * (2 + len(rim_shapes)),
            [sds((part, channels), BF16), sds((edges, part, channels), BF16), *rim_shapes],
            2 * part * channels * (edges * halo + channels),
            part * channels * edges * 4,
        )(rows, pred, others, target, weight, w_out, gain, zhat, rstd, w_msg_t, sg, *far)
        d_zs.append(d_z)
        d_pres.append(d_pre)
    far = [lax.ppermute(piece, "band", far_swap) for piece in far]

    near = call(
        functools.partial(rim_kernel, owned, chunks),
        [vmem] * (1 + chunks),
        [vmem] * len(near_shapes),
        near_shapes,
        *IN_SHADOW,
        [vmem((halo, channels), F32), vmem((chunks, halo, edges * part), BF16)],
    )(slots, *d_pres)
    near = [lax.ppermute(piece, "band", near_swap) for piece in near]

    d_grid, own = call(
        functools.partial(own_grad_kernel, chunks),
        [vmem] * (2 + 2 * chunks),
        [far_memory, vmem],
        [sds((points, channels), BF16), sds((owned, channels), F32)],
        *IN_SHADOW,
        [
            vmem((points, channels), BF16),
            vmem((part, channels), BF16),
            vmem((part, channels), F32),
            vmem((chunks, owned, edges * part), BF16),
            pltpu.SemaphoreType.DMA((chunks,)),
        ],
    )(slots, w_dst, *[ref for pair in zip(d_zs, d_pres) for ref in pair])

    base, far_hot = call(
        merge_kernel,
        [vmem] * (3 + len(near)),
        [vmem] * 2,
        [sds((owned, channels), F32), sds((owned, halo), BF16)],
        *IN_SHADOW,
        [vmem((halo, channels), BF16), vmem((owned, halo), BF16)],
    )(send_rows, own, w_src_t, *near)

    [d_mesh] = call(
        mesh_kernel,
        [vmem] * (3 + len(far)),
        [far_memory],
        [sds((owned, channels), BF16)],
        2 * owned * channels * (channels + halo),
        owned * channels * 8,
        [
            vmem((halo, channels), BF16),
            vmem((owned, channels), BF16),
            pltpu.SemaphoreType.DMA((4,)),
        ],
    )(far_hot, base, w_src_t, *far)
    return (d_grid[None], d_mesh[None])


def solution(mesh):
    placed = (
        P("member", "band", None),
        P("member", "band", None),
        P(None, None, "band"),
        P("band", None),
        P("band", None),
        P(None, "band"),
        P(),
        P(),
        P(),
        P(),
        P(),
        P(),
        P(),
    )
    return jax.shard_map(
        per_device,
        mesh=mesh,
        in_specs=placed,
        out_specs=(P("member", "band", None), P("member", "band", None)),
        check_vma=False,
    )
```

```python
import functools

import jax
import jax.numpy as jnp
from jax import lax
from jax.experimental import pallas as pl
from jax.experimental.pallas import tpu as pltpu
from jax.sharding import PartitionSpec as P

DELTA_SQ = 0.0625
ALPHA = 0.95
LN_EPS = 1e-05
F32 = jnp.float32
BF16 = jnp.bfloat16
IN_SHADOW = (1, 1)
VMEM_LIMIT = 28 * 1024 * 1024


def slope(diff):
    return diff * lax.rsqrt(diff * diff + DELTA_SQ)


def mm(left, right):
    return jnp.dot(left, right, preferred_element_type=F32)


def mm_t(left, right):
    return lax.dot_general(left, right, (((1,), (1,)), ((), ())), preferred_element_type=F32)


STRIP = 16


def strips(rows, size=STRIP):
    return [slice(first, first + size) for first in range(0, rows, size)]


def column_of(ids):
    lanes = 128
    rows = ids.shape[1]
    column = jnp.broadcast_to(ids.astype(F32), (lanes, rows)).T.astype(jnp.int16)
    return column - lax.broadcasted_iota(jnp.int16, (rows, lanes), 1)


def column_hot(column, base, slots):
    offset = column - jnp.broadcast_to(base, column.shape).astype(jnp.int16)
    parts = [
        jnp.where(offset == jnp.int16(first), BF16(1), BF16(0))
        for first in range(0, slots, column.shape[1])
    ]
    return jnp.concatenate(parts, axis=1)


def fill_rows(hot_ref, ids, base):
    edges, points = ids.shape
    sublane = lax.broadcasted_iota(jnp.int16, (STRIP, points), 0)
    for k in range(edges):
        row = jnp.broadcast_to(ids[k : k + 1, :] - base, (STRIP, points)).astype(jnp.int16)
        offset = row - sublane
        for part in strips(hot_ref.shape[0]):
            hot_ref[part, k * points : (k + 1) * points] = jnp.where(
                offset == jnp.int16(part.start), BF16(1), BF16(0)
            )


def swap(firsts):
    return [pair for i in firsts for pair in ((i, i + 1), (i + 1, i))]


def hbm(array):
    return pltpu.with_memory_space_constraint(array, pltpu.HBM)


def call(body, places, out_places, out_shape, flops, nbytes, scratch=()):
    def specs(memories):
        return [pl.BlockSpec(memory_space=memory) for memory in memories]

    return pl.pallas_call(
        body,
        in_specs=specs(places),
        out_specs=specs(out_places),
        out_shape=out_shape,
        scratch_shapes=scratch,
        compiler_params=pltpu.CompilerParams(vmem_limit_bytes=VMEM_LIMIT),
        cost_estimate=pl.CostEstimate(flops=flops, bytes_accessed=nbytes, transcendentals=0),
    )


def near_far(low, high):
    odd = lax.axis_index("band") % 2 == 1
    return jnp.where(odd, low, high), jnp.where(odd, high, low)


def rim_bases(owned, halo):
    return near_far(owned, owned + halo)


def rows_to(array, rows):
    array = array.astype(F32)
    return jnp.concatenate([array, jnp.zeros((rows - array.shape[0], array.shape[1]), F32)], axis=0)


def pieces(rows, size):
    return [slice(first, first + size) for first in range(0, rows, size)]


def placed_rows(refs):
    first, out = 0, []
    for ref in refs:
        out.append((slice(first, first + ref.shape[0]), ref))
        first += ref.shape[0]
    return out


def join(refs, whole_ref):
    for rows, ref in placed_rows(refs):
        whole_ref[rows, :] = ref[...]


def far_kernel(held, mesh_hbm, w_src_hbm, send_hbm, *refs):
    held_hbm, (far_ref, mesh_ref, w_src_ref, *held_refs) = refs[:held], refs[held:-2]
    send_ref, sems = refs[-2:]
    owned = mesh_ref.shape[0]
    parts = pieces(owned, owned // 2)
    moves = [(send_hbm, send_ref)]
    moves += [(mesh_hbm.at[part], mesh_ref.at[part]) for part in parts]
    moves += [(w_src_hbm, w_src_ref), *zip(held_hbm, held_refs)]
    loads = [pltpu.make_async_copy(*move, sems.at[i]) for i, move in enumerate(moves)]
    for load in loads:
        load.start()
    loads[0].wait()
    far = near_far(send_ref[0:1, :], send_ref[1:2, :])[1]
    column = column_of(far)
    hots = [column_hot(column, part.start, part.stop - part.start) for part in parts]
    rows = None
    for load, part, hot in zip(loads[1:], parts, hots):
        load.wait()
        picked = mm(hot, mesh_ref[part])
        rows = picked if rows is None else rows + picked
    loads[1 + len(parts)].wait()
    far_ref[...] = mm(rows.astype(BF16), w_src_ref[...]).astype(BF16)
    for load in loads[2 + len(parts) :]:
        load.wait()


def near_kernel(mesh_ref, w_src_ref, send_ref, src_ref, *near_refs):
    src = mm(mesh_ref[...], w_src_ref[...]).astype(BF16)
    src_ref[...] = src
    near = near_far(send_ref[0:1, :], send_ref[1:2, :])[0]
    rows = mm(column_hot(column_of(near), 0, src.shape[0]), src_ref[...]).astype(BF16)
    for part, near_ref in placed_rows(near_refs):
        near_ref[...] = rows[part, :]


def ready_kernel(
    owned,
    slots_ref,
    grid_ref,
    w_dst_ref,
    w_msg_ref,
    w_src_ref,
    w_out_ref,
    target_ref,
    weight_ref,
    dst_ref,
    columns_ref,
    rows_ref,
    w_msg_t_ref,
    w_src_t_ref,
    w_out_all_ref,
    target_all_ref,
    weight_all_ref,
):
    dst_ref[...] = mm(grid_ref[...], w_dst_ref[...])
    w_msg_t_ref[...] = w_msg_ref[...].T
    w_src_t_ref[...] = w_src_ref[...].T
    fields = target_all_ref.shape[0]
    w_out_all_ref[...] = rows_to(w_out_ref[...], fields).astype(BF16)
    target_all_ref[...] = rows_to(target_ref[...], fields)
    weight = weight_ref[...]
    weight_all_ref[...] = jnp.concatenate(
        [weight, jnp.zeros((1, fields - weight.shape[1]), F32)], axis=1
    )
    edges, _, halo = columns_ref.shape
    chunks, _, width = rows_ref.shape
    far = rim_bases(owned, halo)[1]
    part = width // edges
    for c in range(chunks):
        points = slice(c * part, (c + 1) * part)
        for k in range(edges):
            column = column_of(slots_ref[k : k + 1, points])
            columns_ref[k, points, :] = column_hot(column, far, halo)
        fill_rows(rows_ref.at[c], slots_ref[:, points], far)


def own_kernel(block, slots_ref, src_ref, dst_ref, attr_ref, w_edge_ref, *refs):
    *near_refs, pre_ref, embed_ref, attr_f32, near_ref = refs
    join(near_refs, near_ref)
    edges, lanes, channels = embed_ref.shape
    feats = w_edge_ref.shape[0]
    row = lax.broadcasted_iota(jnp.int32, (lanes, channels), 0)
    w_edge = w_edge_ref[...].astype(F32)
    for k in range(edges):
        spread = jnp.zeros((lanes, channels), F32)
        for e in range(feats):
            spread = jnp.where(row == e * edges + k, w_edge[e : e + 1, :], spread)
        embed_ref[k] = spread.astype(BF16)
    for e in range(feats):
        attr_f32[e * edges : (e + 1) * edges, :] = attr_ref[e].astype(F32)
    owned = src_ref.shape[0]
    halo = near_ref.shape[0]
    base = rim_bases(owned, halo)[0]
    for rows in pieces(dst_ref.shape[0], block):
        attr = rows_to(attr_f32[:, rows], lanes).T.astype(BF16)
        for k in range(edges):
            column = column_of(slots_ref[k : k + 1, rows])
            picked = mm(column_hot(column, 0, owned), src_ref[...])
            picked = picked + mm(column_hot(column, base, halo), near_ref[...])
            embed = mm(attr, embed_ref[k])
            pre_ref[k, rows, :] = (picked + embed + dst_ref[rows, :]).astype(BF16)


def forward_kernel(
    first,
    block,
    columns_ref,
    pre_ref,
    grid_ref,
    w_msg_ref,
    gain_ref,
    w_out_ref,
    far_ref,
    pred_ref,
    pred_bf_ref,
    sg_ref,
    zhat_ref,
    rstd_ref,
):
    half = BF16(0.5)
    totals = []
    for rows in pieces(zhat_ref.shape[0], block):
        source = slice(first + rows.start, first + rows.stop)
        acts = []
        for k in range(columns_ref.shape[0]):
            picked = mm(columns_ref[k, source, :], far_ref[...])
            pre = pre_ref[k, source, :] + picked.astype(BF16)
            sigma = half + half * jnp.tanh(half * pre)
            act = pre * sigma
            acts.append(act)
            sg_ref[k, rows, :] = sigma + (act - act * sigma)
        while len(acts) > 1:
            acts = [sum(acts[i : i + 2][1:], acts[i]) for i in range(0, len(acts), 2)]
        totals.append((rows, source, acts[0]))
    for rows, source, total in totals:
        z = grid_ref[source, :].astype(F32) + mm(total, w_msg_ref[...])
        centre = z - jnp.mean(z, axis=1, keepdims=True)
        rstd = lax.rsqrt(jnp.mean(centre * centre, axis=1, keepdims=True) + LN_EPS)
        zhat = centre * rstd
        pred = mm_t(w_out_ref[...], (zhat * gain_ref[...]).astype(BF16))
        pred_ref[:, rows] = pred
        pred_bf_ref[:, rows] = pred[: pred_bf_ref.shape[0], :].astype(BF16)
        zhat_ref[rows, :] = zhat.astype(BF16)
        rstd_ref[rows, :] = jnp.broadcast_to(rstd, (block, rstd_ref.shape[1]))


def backward_kernel(
    chunk,
    block,
    coeff,
    given,
    hot_ref,
    pred_ref,
    others_ref,
    target_ref,
    weight_ref,
    w_out_ref,
    gain_ref,
    zhat_ref,
    rstd_ref,
    w_msg_t_ref,
    sg_ref,
    *refs,
):
    prior, (dz_ref, dpre_ref, far_ref) = refs[:given], refs[given:]
    fields = pred_ref.shape[0]
    edges, points, channels = dpre_ref.shape
    first = chunk * points
    gain = gain_ref[...]
    sent = others_ref.shape[1]
    far = prior[0][...] if prior else None
    for rows in pieces(points, block):
        source = slice(first + rows.start, first + rows.stop)
        pred = pred_ref[:, rows]
        spread = jnp.zeros((sent, block), F32)
        for other in range(others_ref.shape[0]):
            spread = spread + slope(pred[:sent, :] - others_ref[other, :, rows].astype(F32))
        d_pred = slope(pred - target_ref[:, source])
        d_pred = d_pred - coeff * rows_to(spread, fields)
        d_pred = (weight_ref[...] * d_pred.T).astype(BF16)
        scaled = mm(d_pred, w_out_ref[...]) * gain
        zhat = zhat_ref[rows, :].astype(F32)
        d_z = rstd_ref[rows, :1] * (
            scaled
            - jnp.mean(scaled, axis=1, keepdims=True)
            - zhat * jnp.mean(scaled * zhat, axis=1, keepdims=True)
        )
        d_zb = d_z.astype(BF16)
        dz_ref[rows, :] = d_zb
        d_act = mm(d_zb, w_msg_t_ref[...]).astype(BF16)
        hots, d_pres = [], []
        for k in range(edges):
            d_pre = d_act * sg_ref[k, rows, :]
            dpre_ref[k, rows, :] = d_pre
            d_pres.append(d_pre)
            hots.append(hot_ref[chunk, :, k * points + rows.start : k * points + rows.stop])
        added = mm(jnp.concatenate(hots, axis=1), jnp.concatenate(d_pres, axis=0))
        far = added if far is None else far + added
    far_ref[...] = far.astype(far_ref.dtype)


def rim_kernel(owned, chunks, slots_ref, *refs):
    dpre_refs = refs[:chunks]
    *near_refs, acc, hot_ref = refs[chunks:]
    base = rim_bases(owned, acc.shape[0])[0]
    first = 0
    for c, dpre_ref in enumerate(dpre_refs):
        edges, points, channels = dpre_ref.shape
        fill_rows(hot_ref.at[c], slots_ref[:, first : first + points], base)
        first += points
        added = mm(hot_ref[c], dpre_ref[...].reshape(edges * points, channels))
        acc[...] = added if c == 0 else acc[...] + added
    for rows, near_ref in placed_rows(near_refs):
        near_ref[...] = acc[rows, :].astype(BF16)


def own_grad_kernel(chunks, slots_ref, w_dst_ref, *refs):
    grid_hbm, own_ref, grid_ref, dsum_ref, wide_ref, hot_ref, sems = refs[-7:]
    stores = []
    for c in range(chunks):
        dz_ref, dpre_ref = refs[2 * c : 2 * c + 2]
        edges, points, channels = dpre_ref.shape
        rows = slice(c * points, (c + 1) * points)
        for part in strips(points):
            d_sum = sum(dpre_ref[k, part, :].astype(F32) for k in range(edges))
            dsum_ref[part, :] = d_sum.astype(BF16)
        wide_ref[...] = mm_t(dsum_ref[...], w_dst_ref[...])
        for part in strips(points):
            d_grid = dz_ref[part, :].astype(F32) + wide_ref[part, :]
            grid_ref[rows.start + part.start : rows.start + part.stop, :] = d_grid.astype(BF16)
        stores.append(pltpu.make_async_copy(grid_ref.at[rows], grid_hbm.at[rows], sems.at[c]))
        stores[-1].start()
        fill_rows(hot_ref.at[c], slots_ref[:, rows], 0)
        added = mm(hot_ref[c], dpre_ref[...].reshape(edges * points, channels))
        own_ref[...] = added if c == 0 else own_ref[...] + added
    for store in stores:
        store.wait()


def merge_kernel(send_ref, own_ref, w_src_t_ref, *refs):
    *near_refs, base_ref, hot_ref, near_ref, near_hot = refs
    join(near_refs, near_ref)
    near, far = near_far(send_ref[0:1, :], send_ref[1:2, :])
    fill_rows(near_hot, near, 0)
    total = own_ref[...] + mm(near_hot[...], near_ref[...])
    base_ref[...] = mm(total.astype(BF16), w_src_t_ref[...])
    fill_rows(hot_ref, far, 0)


def mesh_kernel(hot_ref, base_ref, w_src_t_ref, *refs):
    *far_refs, mesh_hbm, rows_ref, out_ref, sems = refs
    owned = base_ref.shape[0]
    size = far_refs[0].shape[0]
    for i, far_ref in enumerate(far_refs):
        rows_ref[i * size : (i + 1) * size, :] = mm(far_ref[...], w_src_t_ref[...]).astype(BF16)
    stores = []
    for i, part in enumerate(pieces(owned, owned // 4)):
        out = base_ref[part, :] + mm(hot_ref[part, :], rows_ref[...])
        out_ref[part, :] = out.astype(BF16)
        stores.append(pltpu.make_async_copy(out_ref.at[part], mesh_hbm.at[part], sems.at[i]))
        stores[-1].start()
    for store in stores:
        store.wait()


def per_device(
    grid_latent,
    mesh_latent,
    edge_attr,
    neighbours,
    send_rows,
    target,
    field_weight,
    w_src,
    w_dst,
    w_edge,
    w_msg,
    ln_gain,
    w_out,
):
    grid_rows = grid_latent[0]
    mesh_rows = mesh_latent[0]
    points, channels = grid_rows.shape
    owned = mesh_rows.shape[0]
    halo = send_rows.shape[1]
    edges = neighbours.shape[1]
    feats = w_edge.shape[0]
    lanes = 128
    fields = -(-w_out.shape[1] // lanes) * lanes
    sent = -(-w_out.shape[1] // 16) * 16
    block = min(points, 512)
    sds = jax.ShapeDtypeStruct
    members = lax.axis_size("member")
    bands = lax.axis_size("band")
    near_swap = swap(range(0, bands - 1, 2))
    far_swap = swap(range(1, bands - 1, 2))
    vmem, far_memory = pltpu.VMEM, pltpu.HBM
    slots = neighbours.T
    gain = ln_gain[None, :]
    w_out = w_out.T
    weight = field_weight[None, :]

    far_shapes = [sds((halo, channels), BF16)]
    near_shapes = [sds((halo // 2, channels), BF16)] * 2
    held = [grid_rows, w_dst, w_msg, target]
    *far, mesh_rows, w_src, grid_rows, w_dst, w_msg, target = call(
        functools.partial(far_kernel, len(held)),
        [far_memory] * (3 + len(held)),
        [vmem] * (3 + len(held)),
        far_shapes + [sds(array.shape, array.dtype) for array in (mesh_rows, w_src, *held)],
        2 * owned * channels * halo,
        2 * owned * channels,
        [
            vmem((2, halo), jnp.int32),
            pltpu.SemaphoreType.DMA((4 + len(held),)),
        ],
    )(*map(hbm, (mesh_rows, w_src, send_rows, *held)))
    far = [lax.ppermute(piece, "band", far_swap) for piece in far]

    src, *near = call(
        near_kernel,
        [vmem] * 3,
        [vmem] * (1 + len(near_shapes)),
        [sds((owned, channels), BF16), *near_shapes],
        *IN_SHADOW,
    )(mesh_rows, w_src, send_rows)
    near = [lax.ppermute(piece, "band", near_swap) for piece in near]

    chunks = 2
    part = points // chunks
    dst, columns, rows, w_msg_t, w_src_t, w_out, target, weight = call(
        functools.partial(ready_kernel, owned),
        [vmem] * 8,
        [vmem] * 8,
        [
            sds((points, channels), F32),
            sds((edges, points, halo), BF16),
            sds((chunks, halo, edges * part), BF16),
            sds(w_msg.shape, BF16),
            sds(w_src.shape, BF16),
            sds((fields, channels), BF16),
            sds((fields, points), F32),
            sds((1, fields), F32),
        ],
        *IN_SHADOW,
    )(slots, grid_rows, w_dst, w_msg, w_src, w_out, target, weight)

    [pre] = call(
        functools.partial(own_kernel, block),
        [vmem] * (5 + len(near)),
        [vmem],
        [sds((edges, points, channels), BF16)],
        *IN_SHADOW,
        [
            vmem((edges, lanes, channels), BF16),
            vmem((feats * edges, points), F32),
            vmem((halo, channels), BF16),
        ],
    )(slots, src, dst, edge_attr, w_edge, *near)

    ahead = []
    for c in range(chunks):
        pred, pred_bf, sg, zhat, rstd = call(
            functools.partial(forward_kernel, c * part, part // 2),
            [vmem] * (6 + len(far)),
            [vmem] * 5,
            [
                sds((fields, part), F32),
                sds((sent, part), BF16),
                sds((edges, part, channels), BF16),
                sds((part, channels), BF16),
                sds((part, lanes), F32),
            ],
            2 * part * channels * (edges * halo + channels),
            part * channels * edges * 4,
        )(columns, pre, grid_rows, w_msg, gain, w_out, *far)
        if members == 2:
            others = lax.ppermute(pred_bf, "member", [(0, 1), (1, 0)])[None]
        else:
            others = lax.all_gather(pred_bf[None], "member", axis=0, tiled=True)
        ahead.append((pred, others, sg, zhat, rstd))

    coeff = ALPHA / (members - 1) + (1.0 - ALPHA) / members
    far = []
    d_zs, d_pres = [], []
    for c, (pred, others, sg, zhat, rstd) in enumerate(ahead):
        rim_shapes = far_shapes if c == chunks - 1 else [sds((halo, channels), F32)]
        d_z, d_pre, *far = call(
            functools.partial(backward_kernel, c, part // 2, coeff, len(far)),
            [vmem] * (11 + len(far)),
            [vmem] * (2 + len(rim_shapes)),
            [sds((part, channels), BF16), sds((edges, part, channels), BF16), *rim_shapes],
            2 * part * channels * (edges * halo + channels),
            part * channels * edges * 4,
        )(rows, pred, others, target, weight, w_out, gain, zhat, rstd, w_msg_t, sg, *far)
        d_zs.append(d_z)
        d_pres.append(d_pre)
    far = [lax.ppermute(piece, "band", far_swap) for piece in far]

    near = call(
        functools.partial(rim_kernel, owned, chunks),
        [vmem] * (1 + chunks),
        [vmem] * len(near_shapes),
        near_shapes,
        *IN_SHADOW,
        [vmem((halo, channels), F32), vmem((chunks, halo, edges * part), BF16)],
    )(slots, *d_pres)
    near = [lax.ppermute(piece, "band", near_swap) for piece in near]

    d_grid, own = call(
        functools.partial(own_grad_kernel, chunks),
        [vmem] * (2 + 2 * chunks),
        [far_memory, vmem],
        [sds((points, channels), BF16), sds((owned, channels), F32)],
        *IN_SHADOW,
        [
            vmem((points, channels), BF16),
            vmem((part, channels), BF16),
            vmem((part, channels), F32),
            vmem((chunks, owned, edges * part), BF16),
            pltpu.SemaphoreType.DMA((chunks,)),
        ],
    )(slots, w_dst, *[ref for pair in zip(d_zs, d_pres) for ref in pair])

    base, far_hot = call(
        merge_kernel,
        [vmem] * (3 + len(near)),
        [vmem] * 2,
        [sds((owned, channels), F32), sds((owned, halo), BF16)],
        *IN_SHADOW,
        [vmem((halo, channels), BF16), vmem((owned, halo), BF16)],
    )(send_rows, own, w_src_t, *near)

    [d_mesh] = call(
        mesh_kernel,
        [vmem] * (3 + len(far)),
        [far_memory],
        [sds((owned, channels), BF16)],
        2 * owned * channels * (channels + halo),
        owned * channels * 8,
        [
            vmem((halo, channels), BF16),
            vmem((owned, channels), BF16),
            pltpu.SemaphoreType.DMA((4,)),
        ],
    )(far_hot, base, w_src_t, *far)
    return (d_grid[None], d_mesh[None])


def solution(mesh):
    placed = (
        P("member", "band", None),
        P("member", "band", None),
        P(None, None, "band"),
        P("band", None),
        P("band", None),
        P(None, "band"),
        P(),
        P(),
        P(),
        P(),
        P(),
        P(),
        P(),
    )
    return jax.shard_map(
        per_device,
        mesh=mesh,
        in_specs=placed,
        out_specs=(P("member", "band", None), P("member", "band", None)),
        check_vma=False,
    )
```

```python
import functools

import jax
import jax.numpy as jnp
from jax import lax
from jax.experimental import pallas as pl
from jax.experimental.pallas import tpu as pltpu
from jax.sharding import PartitionSpec as P

DELTA_SQ = 0.0625
ALPHA = 0.95
LN_EPS = 1e-05
F32 = jnp.float32
BF16 = jnp.bfloat16
IN_SHADOW = (1, 1)
VMEM_LIMIT = 28 * 1024 * 1024


def slope(diff):
    return diff * lax.rsqrt(diff * diff + DELTA_SQ)


def mm(left, right):
    return jnp.dot(left, right, preferred_element_type=F32)


def mm_t(left, right):
    return lax.dot_general(left, right, (((1,), (1,)), ((), ())), preferred_element_type=F32)


STRIP = 16


def strips(rows, size=STRIP):
    return [slice(first, first + size) for first in range(0, rows, size)]


def column_of(ids):
    lanes = 128
    rows = ids.shape[1]
    column = jnp.broadcast_to(ids.astype(F32), (lanes, rows)).T.astype(jnp.int16)
    return column - lax.broadcasted_iota(jnp.int16, (rows, lanes), 1)


def column_hot(column, base, slots):
    offset = column - jnp.broadcast_to(base, column.shape).astype(jnp.int16)
    parts = [
        jnp.where(offset == jnp.int16(first), BF16(1), BF16(0))
        for first in range(0, slots, column.shape[1])
    ]
    return jnp.concatenate(parts, axis=1)


def fill_rows(hot_ref, ids, base):
    edges, points = ids.shape
    sublane = lax.broadcasted_iota(jnp.int16, (STRIP, points), 0)
    for k in range(edges):
        row = jnp.broadcast_to(ids[k : k + 1, :] - base, (STRIP, points)).astype(jnp.int16)
        offset = row - sublane
        for part in strips(hot_ref.shape[0]):
            hot_ref[part, k * points : (k + 1) * points] = jnp.where(
                offset == jnp.int16(part.start), BF16(1), BF16(0)
            )


def swap(firsts):
    return [pair for i in firsts for pair in ((i, i + 1), (i + 1, i))]


def hbm(array):
    return pltpu.with_memory_space_constraint(array, pltpu.HBM)


def call(body, places, out_places, out_shape, flops, nbytes, scratch=()):
    def specs(memories):
        return [pl.BlockSpec(memory_space=memory) for memory in memories]

    return pl.pallas_call(
        body,
        in_specs=specs(places),
        out_specs=specs(out_places),
        out_shape=out_shape,
        scratch_shapes=scratch,
        compiler_params=pltpu.CompilerParams(vmem_limit_bytes=VMEM_LIMIT),
        cost_estimate=pl.CostEstimate(flops=flops, bytes_accessed=nbytes, transcendentals=0),
    )


def near_far(low, high):
    odd = lax.axis_index("band") % 2 == 1
    return jnp.where(odd, low, high), jnp.where(odd, high, low)


def rim_bases(owned, halo):
    return near_far(owned, owned + halo)


def rows_to(array, rows):
    array = array.astype(F32)
    return jnp.concatenate([array, jnp.zeros((rows - array.shape[0], array.shape[1]), F32)], axis=0)


def pieces(rows, size):
    return [slice(first, first + size) for first in range(0, rows, size)]


def placed_rows(refs):
    first, out = 0, []
    for ref in refs:
        out.append((slice(first, first + ref.shape[0]), ref))
        first += ref.shape[0]
    return out


def join(refs, whole_ref):
    for rows, ref in placed_rows(refs):
        whole_ref[rows, :] = ref[...]


def far_kernel(held, mesh_hbm, w_src_hbm, send_hbm, *refs):
    held_hbm, (far_ref, mesh_ref, w_src_ref, *held_refs) = refs[:held], refs[held:-2]
    send_ref, sems = refs[-2:]
    owned = mesh_ref.shape[0]
    parts = pieces(owned, owned // 2)
    moves = [(send_hbm, send_ref)]
    moves += [(mesh_hbm.at[part], mesh_ref.at[part]) for part in parts]
    moves += [(w_src_hbm, w_src_ref), *zip(held_hbm, held_refs)]
    loads = [pltpu.make_async_copy(*move, sems.at[i]) for i, move in enumerate(moves)]
    for load in loads:
        load.start()
    loads[0].wait()
    far = near_far(send_ref[0:1, :], send_ref[1:2, :])[1]
    column = column_of(far)
    hots = [column_hot(column, part.start, part.stop - part.start) for part in parts]
    rows = None
    for load, part, hot in zip(loads[1:], parts, hots):
        load.wait()
        picked = mm(hot, mesh_ref[part])
        rows = picked if rows is None else rows + picked
    loads[1 + len(parts)].wait()
    far_ref[...] = mm(rows.astype(BF16), w_src_ref[...]).astype(BF16)
    for load in loads[2 + len(parts) :]:
        load.wait()


def near_kernel(mesh_ref, w_src_ref, send_ref, src_ref, *near_refs):
    src = mm(mesh_ref[...], w_src_ref[...]).astype(BF16)
    src_ref[...] = src
    near = near_far(send_ref[0:1, :], send_ref[1:2, :])[0]
    rows = mm(column_hot(column_of(near), 0, src.shape[0]), src_ref[...]).astype(BF16)
    for part, near_ref in placed_rows(near_refs):
        near_ref[...] = rows[part, :]


def ready_kernel(
    owned,
    slots_ref,
    grid_ref,
    w_dst_ref,
    w_msg_ref,
    w_src_ref,
    w_out_ref,
    target_ref,
    weight_ref,
    dst_ref,
    columns_ref,
    rows_ref,
    w_msg_t_ref,
    w_src_t_ref,
    w_out_all_ref,
    target_all_ref,
    weight_all_ref,
):
    dst_ref[...] = mm(grid_ref[...], w_dst_ref[...])
    w_msg_t_ref[...] = w_msg_ref[...].T
    w_src_t_ref[...] = w_src_ref[...].T
    fields = target_all_ref.shape[0]
    w_out_all_ref[...] = rows_to(w_out_ref[...], fields).astype(BF16)
    target_all_ref[...] = rows_to(target_ref[...], fields)
    weight = weight_ref[...]
    weight_all_ref[...] = jnp.concatenate(
        [weight, jnp.zeros((1, fields - weight.shape[1]), F32)], axis=1
    )
    edges, _, halo = columns_ref.shape
    chunks, _, width = rows_ref.shape
    far = rim_bases(owned, halo)[1]
    part = width // edges
    for c in range(chunks):
        points = slice(c * part, (c + 1) * part)
        for k in range(edges):
            column = column_of(slots_ref[k : k + 1, points])
            columns_ref[k, points, :] = column_hot(column, far, halo)
        fill_rows(rows_ref.at[c], slots_ref[:, points], far)


def own_kernel(block, slots_ref, src_ref, dst_ref, attr_ref, w_edge_ref, *refs):
    *near_refs, pre_ref, embed_ref, attr_f32, near_ref = refs
    join(near_refs, near_ref)
    edges, lanes, channels = embed_ref.shape
    feats = w_edge_ref.shape[0]
    row = lax.broadcasted_iota(jnp.int32, (lanes, channels), 0)
    w_edge = w_edge_ref[...].astype(F32)
    for k in range(edges):
        spread = jnp.zeros((lanes, channels), F32)
        for e in range(feats):
            spread = jnp.where(row == e * edges + k, w_edge[e : e + 1, :], spread)
        embed_ref[k] = spread.astype(BF16)
    for e in range(feats):
        attr_f32[e * edges : (e + 1) * edges, :] = attr_ref[e].astype(F32)
    owned = src_ref.shape[0]
    halo = near_ref.shape[0]
    base = rim_bases(owned, halo)[0]
    for rows in pieces(dst_ref.shape[0], block):
        attr = rows_to(attr_f32[:, rows], lanes).T.astype(BF16)
        for k in range(edges):
            column = column_of(slots_ref[k : k + 1, rows])
            picked = mm(column_hot(column, 0, owned), src_ref[...])
            picked = picked + mm(column_hot(column, base, halo), near_ref[...])
            embed = mm(attr, embed_ref[k])
            pre_ref[k, rows, :] = (picked + embed + dst_ref[rows, :]).astype(BF16)


def forward_kernel(
    first,
    block,
    columns_ref,
    pre_ref,
    grid_ref,
    w_msg_ref,
    gain_ref,
    w_out_ref,
    far_ref,
    pred_ref,
    pred_bf_ref,
    sg_ref,
    zhat_ref,
    rstd_ref,
):
    half = BF16(0.5)
    for rows in pieces(zhat_ref.shape[0], block):
        source = slice(first + rows.start, first + rows.stop)
        acts = []
        for k in range(columns_ref.shape[0]):
            picked = mm(columns_ref[k, source, :], far_ref[...])
            pre = pre_ref[k, source, :] + picked.astype(BF16)
            sigma = half + half * jnp.tanh(half * pre)
            act = pre * sigma
            acts.append(act)
            sg_ref[k, rows, :] = sigma + (act - act * sigma)
        while len(acts) > 1:
            acts = [sum(acts[i : i + 2][1:], acts[i]) for i in range(0, len(acts), 2)]
        z = grid_ref[source, :].astype(F32) + mm(acts[0], w_msg_ref[...])
        centre = z - jnp.mean(z, axis=1, keepdims=True)
        rstd = lax.rsqrt(jnp.mean(centre * centre, axis=1, keepdims=True) + LN_EPS)
        zhat = centre * rstd
        pred = mm_t(w_out_ref[...], (zhat * gain_ref[...]).astype(BF16))
        pred_ref[:, rows] = pred
        pred_bf_ref[:, rows] = pred[: pred_bf_ref.shape[0], :].astype(BF16)
        zhat_ref[rows, :] = zhat.astype(BF16)
        rstd_ref[rows, :] = jnp.broadcast_to(rstd, (block, rstd_ref.shape[1]))


def backward_kernel(
    chunk,
    block,
    coeff,
    given,
    hot_ref,
    pred_ref,
    others_ref,
    target_ref,
    weight_ref,
    w_out_ref,
    gain_ref,
    zhat_ref,
    rstd_ref,
    w_msg_t_ref,
    sg_ref,
    *refs,
):
    prior, (dz_ref, dpre_ref, far_ref, wide_ref) = refs[:given], refs[given:]
    size = 32 if prior else block
    fields = pred_ref.shape[0]
    edges, points, channels = dpre_ref.shape
    first = chunk * points
    gain = gain_ref[...]
    sent = others_ref.shape[1]
    for rows in pieces(points, block):
        source = slice(first + rows.start, first + rows.stop)
        pred = pred_ref[:, rows]
        spread = jnp.zeros((sent, block), F32)
        for other in range(others_ref.shape[0]):
            spread = spread + slope(pred[:sent, :] - others_ref[other, :, rows].astype(F32))
        d_pred = slope(pred - target_ref[:, source])
        d_pred = d_pred - coeff * rows_to(spread, fields)
        d_pred = (weight_ref[...] * d_pred.T).astype(BF16)
        wide_ref[rows, :] = mm(d_pred, w_out_ref[...])
        for part in strips(block, size):
            part = slice(rows.start + part.start, rows.start + part.stop)
            scaled = wide_ref[part, :] * gain
            zhat = zhat_ref[part, :].astype(F32)
            d_z = rstd_ref[part, :1] * (
                scaled
                - jnp.mean(scaled, axis=1, keepdims=True)
                - zhat * jnp.mean(scaled * zhat, axis=1, keepdims=True)
            )
            dz_ref[part, :] = d_z.astype(BF16)
        wide_ref[rows, :] = mm(dz_ref[rows, :], w_msg_t_ref[...])
        for part in strips(block, size):
            part = slice(rows.start + part.start, rows.start + part.stop)
            d_act = wide_ref[part, :].astype(BF16)
            for k in range(edges):
                dpre_ref[k, part, :] = d_act * sg_ref[k, part, :]
    far = mm(hot_ref[chunk], dpre_ref[...].reshape(edges * points, channels))
    if prior:
        far = far + prior[0][...]
    far_ref[...] = far.astype(far_ref.dtype)


def rim_kernel(owned, chunks, slots_ref, *refs):
    dpre_refs = refs[:chunks]
    *near_refs, acc, hot_ref = refs[chunks:]
    base = rim_bases(owned, acc.shape[0])[0]
    first = 0
    for c, dpre_ref in enumerate(dpre_refs):
        edges, points, channels = dpre_ref.shape
        fill_rows(hot_ref.at[c], slots_ref[:, first : first + points], base)
        first += points
        added = mm(hot_ref[c], dpre_ref[...].reshape(edges * points, channels))
        acc[...] = added if c == 0 else acc[...] + added
    for rows, near_ref in placed_rows(near_refs):
        near_ref[...] = acc[rows, :].astype(BF16)


def own_grad_kernel(chunks, slots_ref, w_dst_ref, *refs):
    grid_hbm, own_ref, grid_ref, dsum_ref, wide_ref, hot_ref, sems = refs[-7:]
    stores = []
    for c in range(chunks):
        dz_ref, dpre_ref = refs[2 * c : 2 * c + 2]
        edges, points, channels = dpre_ref.shape
        rows = slice(c * points, (c + 1) * points)
        for part in strips(points):
            d_sum = sum(dpre_ref[k, part, :].astype(F32) for k in range(edges))
            dsum_ref[part, :] = d_sum.astype(BF16)
        wide_ref[...] = mm_t(dsum_ref[...], w_dst_ref[...])
        for part in strips(points):
            d_grid = dz_ref[part, :].astype(F32) + wide_ref[part, :]
            grid_ref[rows.start + part.start : rows.start + part.stop, :] = d_grid.astype(BF16)
        stores.append(pltpu.make_async_copy(grid_ref.at[rows], grid_hbm.at[rows], sems.at[c]))
        stores[-1].start()
        fill_rows(hot_ref.at[c], slots_ref[:, rows], 0)
        added = mm(hot_ref[c], dpre_ref[...].reshape(edges * points, channels))
        own_ref[...] = added if c == 0 else own_ref[...] + added
    for store in stores:
        store.wait()


def merge_kernel(send_ref, own_ref, w_src_t_ref, *refs):
    *near_refs, base_ref, hot_ref, near_ref, near_hot = refs
    join(near_refs, near_ref)
    near, far = near_far(send_ref[0:1, :], send_ref[1:2, :])
    fill_rows(near_hot, near, 0)
    total = own_ref[...] + mm(near_hot[...], near_ref[...])
    base_ref[...] = mm(total.astype(BF16), w_src_t_ref[...])
    fill_rows(hot_ref, far, 0)


def mesh_kernel(hot_ref, base_ref, w_src_t_ref, *refs):
    *far_refs, mesh_hbm, rows_ref, out_ref, sems = refs
    owned = base_ref.shape[0]
    size = far_refs[0].shape[0]
    for i, far_ref in enumerate(far_refs):
        rows_ref[i * size : (i + 1) * size, :] = mm(far_ref[...], w_src_t_ref[...]).astype(BF16)
    stores = []
    for i, part in enumerate(pieces(owned, owned // 2)):
        out = base_ref[part, :] + mm(hot_ref[part, :], rows_ref[...])
        out_ref[part, :] = out.astype(BF16)
        stores.append(pltpu.make_async_copy(out_ref.at[part], mesh_hbm.at[part], sems.at[i]))
        stores[-1].start()
    for store in stores:
        store.wait()


def per_device(
    grid_latent,
    mesh_latent,
    edge_attr,
    neighbours,
    send_rows,
    target,
    field_weight,
    w_src,
    w_dst,
    w_edge,
    w_msg,
    ln_gain,
    w_out,
):
    grid_rows = grid_latent[0]
    mesh_rows = mesh_latent[0]
    points, channels = grid_rows.shape
    owned = mesh_rows.shape[0]
    halo = send_rows.shape[1]
    edges = neighbours.shape[1]
    feats = w_edge.shape[0]
    lanes = 128
    fields = -(-w_out.shape[1] // lanes) * lanes
    sent = -(-w_out.shape[1] // 16) * 16
    block = min(points, 512)
    sds = jax.ShapeDtypeStruct
    members = lax.axis_size("member")
    bands = lax.axis_size("band")
    near_swap = swap(range(0, bands - 1, 2))
    far_swap = swap(range(1, bands - 1, 2))
    vmem, far_memory = pltpu.VMEM, pltpu.HBM
    slots = neighbours.T
    gain = ln_gain[None, :]
    w_out = w_out.T
    weight = field_weight[None, :]

    far_shapes = [sds((halo, channels), BF16)]
    near_shapes = [sds((halo // 2, channels), BF16)] * 2
    held = [grid_rows, w_dst, w_msg, target]
    *far, mesh_rows, w_src, grid_rows, w_dst, w_msg, target = call(
        functools.partial(far_kernel, len(held)),
        [far_memory] * (3 + len(held)),
        [vmem] * (3 + len(held)),
        far_shapes + [sds(array.shape, array.dtype) for array in (mesh_rows, w_src, *held)],
        2 * owned * channels * halo,
        2 * owned * channels,
        [
            vmem((2, halo), jnp.int32),
            pltpu.SemaphoreType.DMA((4 + len(held),)),
        ],
    )(*map(hbm, (mesh_rows, w_src, send_rows, *held)))
    far = [lax.ppermute(piece, "band", far_swap) for piece in far]

    src, *near = call(
        near_kernel,
        [vmem] * 3,
        [vmem] * (1 + len(near_shapes)),
        [sds((owned, channels), BF16), *near_shapes],
        *IN_SHADOW,
    )(mesh_rows, w_src, send_rows)
    near = [lax.ppermute(piece, "band", near_swap) for piece in near]

    chunks = 2
    part = points // chunks
    dst, columns, rows, w_msg_t, w_src_t, w_out, target, weight = call(
        functools.partial(ready_kernel, owned),
        [vmem] * 8,
        [vmem] * 8,
        [
            sds((points, channels), F32),
            sds((edges, points, halo), BF16),
            sds((chunks, halo, edges * part), BF16),
            sds(w_msg.shape, BF16),
            sds(w_src.shape, BF16),
            sds((fields, channels), BF16),
            sds((fields, points), F32),
            sds((1, fields), F32),
        ],
        *IN_SHADOW,
    )(slots, grid_rows, w_dst, w_msg, w_src, w_out, target, weight)

    [pre] = call(
        functools.partial(own_kernel, block),
        [vmem] * (5 + len(near)),
        [vmem],
        [sds((edges, points, channels), BF16)],
        *IN_SHADOW,
        [
            vmem((edges, lanes, channels), BF16),
            vmem((feats * edges, points), F32),
            vmem((halo, channels), BF16),
        ],
    )(slots, src, dst, edge_attr, w_edge, *near)

    ahead = []
    for c in range(chunks):
        pred, pred_bf, sg, zhat, rstd = call(
            functools.partial(forward_kernel, c * part, block),
            [vmem] * (6 + len(far)),
            [vmem] * 5,
            [
                sds((fields, part), F32),
                sds((sent, part), BF16),
                sds((edges, part, channels), BF16),
                sds((part, channels), BF16),
                sds((part, lanes), F32),
            ],
            2 * part * channels * (edges * halo + channels),
            part * channels * edges * 4,
        )(columns, pre, grid_rows, w_msg, gain, w_out, *far)
        if members == 2:
            others = lax.ppermute(pred_bf, "member", [(0, 1), (1, 0)])[None]
        else:
            others = lax.all_gather(pred_bf[None], "member", axis=0, tiled=True)
        ahead.append((pred, others, sg, zhat, rstd))

    coeff = ALPHA / (members - 1) + (1.0 - ALPHA) / members
    far = []
    d_zs, d_pres = [], []
    for c, (pred, others, sg, zhat, rstd) in enumerate(ahead):
        rim_shapes = far_shapes if c == chunks - 1 else [sds((halo, channels), F32)]
        d_z, d_pre, *far = call(
            functools.partial(backward_kernel, c, block, coeff, len(far)),
            [vmem] * (11 + len(far)),
            [vmem] * (2 + len(rim_shapes)),
            [sds((part, channels), BF16), sds((edges, part, channels), BF16), *rim_shapes],
            2 * part * channels * (edges * halo + channels),
            part * channels * edges * 4,
            [vmem((part, channels), F32)],
        )(rows, pred, others, target, weight, w_out, gain, zhat, rstd, w_msg_t, sg, *far)
        d_zs.append(d_z)
        d_pres.append(d_pre)
    far = [lax.ppermute(piece, "band", far_swap) for piece in far]

    near = call(
        functools.partial(rim_kernel, owned, chunks),
        [vmem] * (1 + chunks),
        [vmem] * len(near_shapes),
        near_shapes,
        *IN_SHADOW,
        [vmem((halo, channels), F32), vmem((chunks, halo, edges * part), BF16)],
    )(slots, *d_pres)
    near = [lax.ppermute(piece, "band", near_swap) for piece in near]

    d_grid, own = call(
        functools.partial(own_grad_kernel, chunks),
        [vmem] * (2 + 2 * chunks),
        [far_memory, vmem],
        [sds((points, channels), BF16), sds((owned, channels), F32)],
        *IN_SHADOW,
        [
            vmem((points, channels), BF16),
            vmem((part, channels), BF16),
            vmem((part, channels), F32),
            vmem((chunks, owned, edges * part), BF16),
            pltpu.SemaphoreType.DMA((chunks,)),
        ],
    )(slots, w_dst, *[ref for pair in zip(d_zs, d_pres) for ref in pair])

    base, far_hot = call(
        merge_kernel,
        [vmem] * (3 + len(near)),
        [vmem] * 2,
        [sds((owned, channels), F32), sds((owned, halo), BF16)],
        *IN_SHADOW,
        [vmem((halo, channels), BF16), vmem((owned, halo), BF16)],
    )(send_rows, own, w_src_t, *near)

    [d_mesh] = call(
        mesh_kernel,
        [vmem] * (3 + len(far)),
        [far_memory],
        [sds((owned, channels), BF16)],
        2 * owned * channels * (channels + halo),
        owned * channels * 8,
        [
            vmem((halo, channels), BF16),
            vmem((owned, channels), BF16),
            pltpu.SemaphoreType.DMA((2,)),
        ],
    )(far_hot, base, w_src_t, *far)
    return (d_grid[None], d_mesh[None])


def solution(mesh):
    placed = (
        P("member", "band", None),
        P("member", "band", None),
        P(None, None, "band"),
        P("band", None),
        P("band", None),
        P(None, "band"),
        P(),
        P(),
        P(),
        P(),
        P(),
        P(),
        P(),
    )
    return jax.shard_map(
        per_device,
        mesh=mesh,
        in_specs=placed,
        out_specs=(P("member", "band", None), P("member", "band", None)),
        check_vma=False,
    )
```

```python
import functools

import jax
import jax.numpy as jnp
from jax import lax
from jax.experimental import pallas as pl
from jax.experimental.pallas import tpu as pltpu
from jax.sharding import PartitionSpec as P

DELTA_SQ = 0.0625
ALPHA = 0.95
LN_EPS = 1e-05
F32 = jnp.float32
BF16 = jnp.bfloat16
IN_SHADOW = (1, 1)
VMEM_LIMIT = 28 * 1024 * 1024


def slope(diff):
    return diff * lax.rsqrt(diff * diff + DELTA_SQ)


def mm(left, right):
    return jnp.dot(left, right, preferred_element_type=F32)


def mm_t(left, right):
    return lax.dot_general(left, right, (((1,), (1,)), ((), ())), preferred_element_type=F32)


STRIP = 16


def strips(rows, size=STRIP):
    return [slice(first, first + size) for first in range(0, rows, size)]


def column_of(ids):
    lanes = 128
    rows = ids.shape[1]
    column = jnp.broadcast_to(ids.astype(F32), (lanes, rows)).T.astype(jnp.int16)
    return column - lax.broadcasted_iota(jnp.int16, (rows, lanes), 1)


def column_hot(column, base, slots):
    offset = column - jnp.broadcast_to(base, column.shape).astype(jnp.int16)
    parts = [
        jnp.where(offset == jnp.int16(first), BF16(1), BF16(0))
        for first in range(0, slots, column.shape[1])
    ]
    return jnp.concatenate(parts, axis=1)


def fill_rows(hot_ref, ids, base):
    edges, points = ids.shape
    sublane = lax.broadcasted_iota(jnp.int16, (STRIP, points), 0)
    for k in range(edges):
        row = jnp.broadcast_to(ids[k : k + 1, :] - base, (STRIP, points)).astype(jnp.int16)
        offset = row - sublane
        for part in strips(hot_ref.shape[0]):
            hot_ref[part, k * points : (k + 1) * points] = jnp.where(
                offset == jnp.int16(part.start), BF16(1), BF16(0)
            )


def swap(firsts):
    return [pair for i in firsts for pair in ((i, i + 1), (i + 1, i))]


def hbm(array):
    return pltpu.with_memory_space_constraint(array, pltpu.HBM)


def call(body, places, out_places, out_shape, flops, nbytes, scratch=()):
    def specs(memories):
        return [pl.BlockSpec(memory_space=memory) for memory in memories]

    return pl.pallas_call(
        body,
        in_specs=specs(places),
        out_specs=specs(out_places),
        out_shape=out_shape,
        scratch_shapes=scratch,
        compiler_params=pltpu.CompilerParams(vmem_limit_bytes=VMEM_LIMIT),
        cost_estimate=pl.CostEstimate(flops=flops, bytes_accessed=nbytes, transcendentals=0),
    )


def near_far(low, high):
    odd = lax.axis_index("band") % 2 == 1
    return jnp.where(odd, low, high), jnp.where(odd, high, low)


def rim_bases(owned, halo):
    return near_far(owned, owned + halo)


def rows_to(array, rows):
    array = array.astype(F32)
    return jnp.concatenate([array, jnp.zeros((rows - array.shape[0], array.shape[1]), F32)], axis=0)


def pieces(rows, size):
    return [slice(first, first + size) for first in range(0, rows, size)]


def placed_rows(refs):
    first, out = 0, []
    for ref in refs:
        out.append((slice(first, first + ref.shape[0]), ref))
        first += ref.shape[0]
    return out


def join(refs, whole_ref):
    for rows, ref in placed_rows(refs):
        whole_ref[rows, :] = ref[...]


def far_kernel(mesh_hbm, w_src_hbm, send_hbm, far_ref, mesh_ref, w_src_ref, send_ref, sems):
    owned = mesh_ref.shape[0]
    parts = pieces(owned, owned // 2)
    moves = [(send_hbm, send_ref)]
    moves += [(mesh_hbm.at[part], mesh_ref.at[part]) for part in parts]
    moves += [(w_src_hbm, w_src_ref)]
    loads = [pltpu.make_async_copy(*move, sems.at[i]) for i, move in enumerate(moves)]
    for load in loads:
        load.start()
    loads[0].wait()
    column = column_of(near_far(send_ref[0:1, :], send_ref[1:2, :])[1])
    hots = [column_hot(column, part.start, part.stop - part.start) for part in parts]
    rows = None
    for load, part, hot in zip(loads[1:], parts, hots):
        load.wait()
        picked = mm(hot, mesh_ref[part])
        rows = picked if rows is None else rows + picked
    loads[-1].wait()
    far_ref[...] = mm(rows.astype(BF16), w_src_ref[...]).astype(BF16)


def near_kernel(held, mesh_ref, w_src_ref, send_ref, *refs):
    held_hbm, (src_ref, *near_refs), sems = refs[:held], refs[held : -held - 1], refs[-1]
    loads = [
        pltpu.make_async_copy(*move, sems.at[i])
        for i, move in enumerate(zip(held_hbm, refs[-held - 1 : -1]))
    ]
    for load in loads:
        load.start()
    src = mm(mesh_ref[...], w_src_ref[...]).astype(BF16)
    src_ref[...] = src
    near = near_far(send_ref[0:1, :], send_ref[1:2, :])[0]
    rows = mm(column_hot(column_of(near), 0, src.shape[0]), src_ref[...]).astype(BF16)
    for part, near_ref in placed_rows(near_refs):
        near_ref[...] = rows[part, :]
    for load in loads:
        load.wait()


def ready_kernel(
    owned,
    slots_ref,
    grid_ref,
    w_dst_ref,
    w_msg_ref,
    w_src_ref,
    w_out_ref,
    target_ref,
    weight_ref,
    dst_ref,
    columns_ref,
    rows_ref,
    w_msg_t_ref,
    w_src_t_ref,
    w_out_all_ref,
    target_all_ref,
    weight_all_ref,
):
    dst_ref[...] = mm(grid_ref[...], w_dst_ref[...])
    w_msg_t_ref[...] = w_msg_ref[...].T
    w_src_t_ref[...] = w_src_ref[...].T
    fields = target_all_ref.shape[0]
    w_out_all_ref[...] = rows_to(w_out_ref[...], fields).astype(BF16)
    target_all_ref[...] = rows_to(target_ref[...], fields)
    weight = weight_ref[...]
    weight_all_ref[...] = jnp.concatenate(
        [weight, jnp.zeros((1, fields - weight.shape[1]), F32)], axis=1
    )
    edges, _, halo = columns_ref.shape
    chunks, _, width = rows_ref.shape
    far = rim_bases(owned, halo)[1]
    part = width // edges
    for c in range(chunks):
        points = slice(c * part, (c + 1) * part)
        for k in range(edges):
            column = column_of(slots_ref[k : k + 1, points])
            columns_ref[k, points, :] = column_hot(column, far, halo)
        fill_rows(rows_ref.at[c], slots_ref[:, points], far)


def own_kernel(block, slots_ref, src_ref, dst_ref, attr_ref, w_edge_ref, *refs):
    *near_refs, pre_ref, embed_ref, attr_f32, near_ref = refs
    join(near_refs, near_ref)
    edges, lanes, channels = embed_ref.shape
    feats = w_edge_ref.shape[0]
    row = lax.broadcasted_iota(jnp.int32, (lanes, channels), 0)
    w_edge = w_edge_ref[...].astype(F32)
    for k in range(edges):
        spread = jnp.zeros((lanes, channels), F32)
        for e in range(feats):
            spread = jnp.where(row == e * edges + k, w_edge[e : e + 1, :], spread)
        embed_ref[k] = spread.astype(BF16)
    for e in range(feats):
        attr_f32[e * edges : (e + 1) * edges, :] = attr_ref[e].astype(F32)
    owned = src_ref.shape[0]
    halo = near_ref.shape[0]
    base = rim_bases(owned, halo)[0]
    for rows in pieces(dst_ref.shape[0], block):
        attr = rows_to(attr_f32[:, rows], lanes).T.astype(BF16)
        for k in range(edges):
            column = column_of(slots_ref[k : k + 1, rows])
            picked = mm(column_hot(column, 0, owned), src_ref[...])
            picked = picked + mm(column_hot(column, base, halo), near_ref[...])
            embed = mm(attr, embed_ref[k])
            pre_ref[k, rows, :] = (picked + embed + dst_ref[rows, :]).astype(BF16)


def forward_kernel(
    first,
    block,
    columns_ref,
    pre_ref,
    grid_ref,
    w_msg_ref,
    gain_ref,
    w_out_ref,
    far_ref,
    pred_ref,
    pred_bf_ref,
    sg_ref,
    zhat_ref,
    rstd_ref,
):
    half = BF16(0.5)
    for rows in pieces(zhat_ref.shape[0], block):
        source = slice(first + rows.start, first + rows.stop)
        acts = []
        for k in range(columns_ref.shape[0]):
            picked = mm(columns_ref[k, source, :], far_ref[...])
            pre = pre_ref[k, source, :] + picked.astype(BF16)
            sigma = half + half * jnp.tanh(half * pre)
            act = pre * sigma
            acts.append(act)
            sg_ref[k, rows, :] = sigma + (act - act * sigma)
        while len(acts) > 1:
            acts = [sum(acts[i : i + 2][1:], acts[i]) for i in range(0, len(acts), 2)]
        z = grid_ref[source, :].astype(F32) + mm(acts[0], w_msg_ref[...])
        centre = z - jnp.mean(z, axis=1, keepdims=True)
        rstd = lax.rsqrt(jnp.mean(centre * centre, axis=1, keepdims=True) + LN_EPS)
        zhat = centre * rstd
        pred = mm_t(w_out_ref[...], (zhat * gain_ref[...]).astype(BF16))
        pred_ref[:, rows] = pred
        pred_bf_ref[:, rows] = pred[: pred_bf_ref.shape[0], :].astype(BF16)
        zhat_ref[rows, :] = zhat.astype(BF16)
        rstd_ref[rows, :] = jnp.broadcast_to(rstd, (block, rstd_ref.shape[1]))


def backward_kernel(
    chunk,
    block,
    coeff,
    given,
    hot_ref,
    pred_ref,
    others_ref,
    target_ref,
    weight_ref,
    w_out_ref,
    gain_ref,
    zhat_ref,
    rstd_ref,
    w_msg_t_ref,
    sg_ref,
    *refs,
):
    prior, (dz_ref, dpre_ref, far_ref) = refs[:given], refs[given:]
    fields = pred_ref.shape[0]
    edges, points, channels = dpre_ref.shape
    first = chunk * points
    gain = gain_ref[...]
    sent = others_ref.shape[1]
    for rows in pieces(points, block):
        source = slice(first + rows.start, first + rows.stop)
        pred = pred_ref[:, rows]
        spread = jnp.zeros((sent, block), F32)
        for other in range(others_ref.shape[0]):
            spread = spread + slope(pred[:sent, :] - others_ref[other, :, rows].astype(F32))
        d_pred = slope(pred - target_ref[:, source])
        d_pred = d_pred - coeff * rows_to(spread, fields)
        d_pred = (weight_ref[...] * d_pred.T).astype(BF16)
        scaled = mm(d_pred, w_out_ref[...]) * gain
        zhat = zhat_ref[rows, :].astype(F32)
        d_z = rstd_ref[rows, :1] * (
            scaled
            - jnp.mean(scaled, axis=1, keepdims=True)
            - zhat * jnp.mean(scaled * zhat, axis=1, keepdims=True)
        )
        d_zb = d_z.astype(BF16)
        dz_ref[rows, :] = d_zb
        d_act = mm(d_zb, w_msg_t_ref[...]).astype(BF16)
        for k in range(edges):
            dpre_ref[k, rows, :] = d_act * sg_ref[k, rows, :]
    far = mm(hot_ref[chunk], dpre_ref[...].reshape(edges * points, channels))
    if prior:
        far = far + prior[0][...]
    far_ref[...] = far.astype(far_ref.dtype)


def rim_kernel(owned, chunks, slots_ref, *refs):
    dpre_refs = refs[:chunks]
    *near_refs, acc, hot_ref = refs[chunks:]
    base = rim_bases(owned, acc.shape[0])[0]
    first = 0
    for c, dpre_ref in enumerate(dpre_refs):
        edges, points, channels = dpre_ref.shape
        fill_rows(hot_ref.at[c], slots_ref[:, first : first + points], base)
        first += points
        added = mm(hot_ref[c], dpre_ref[...].reshape(edges * points, channels))
        acc[...] = added if c == 0 else acc[...] + added
    for rows, near_ref in placed_rows(near_refs):
        near_ref[...] = acc[rows, :].astype(BF16)


def own_grad_kernel(chunks, slots_ref, w_dst_ref, *refs):
    grid_hbm, own_ref, grid_ref, dsum_ref, wide_ref, hot_ref, sems = refs[-7:]
    stores = []
    for c in range(chunks):
        dz_ref, dpre_ref = refs[2 * c : 2 * c + 2]
        edges, points, channels = dpre_ref.shape
        rows = slice(c * points, (c + 1) * points)
        for part in strips(points):
            d_sum = sum(dpre_ref[k, part, :].astype(F32) for k in range(edges))
            dsum_ref[part, :] = d_sum.astype(BF16)
        wide_ref[...] = mm_t(dsum_ref[...], w_dst_ref[...])
        for part in strips(points):
            d_grid = dz_ref[part, :].astype(F32) + wide_ref[part, :]
            grid_ref[rows.start + part.start : rows.start + part.stop, :] = d_grid.astype(BF16)
        stores.append(pltpu.make_async_copy(grid_ref.at[rows], grid_hbm.at[rows], sems.at[c]))
        stores[-1].start()
        fill_rows(hot_ref.at[c], slots_ref[:, rows], 0)
        added = mm(hot_ref[c], dpre_ref[...].reshape(edges * points, channels))
        own_ref[...] = added if c == 0 else own_ref[...] + added
    for store in stores:
        store.wait()


def merge_kernel(send_ref, own_ref, w_src_t_ref, *refs):
    *near_refs, base_ref, hot_ref, near_ref, near_hot = refs
    join(near_refs, near_ref)
    near, far = near_far(send_ref[0:1, :], send_ref[1:2, :])
    fill_rows(near_hot, near, 0)
    total = own_ref[...] + mm(near_hot[...], near_ref[...])
    base_ref[...] = mm(total.astype(BF16), w_src_t_ref[...])
    fill_rows(hot_ref, far, 0)


def mesh_kernel(hot_ref, base_ref, w_src_t_ref, *refs):
    *far_refs, mesh_hbm, rows_ref, out_ref, sems = refs
    owned = base_ref.shape[0]
    size = far_refs[0].shape[0]
    for i, far_ref in enumerate(far_refs):
        rows_ref[i * size : (i + 1) * size, :] = mm(far_ref[...], w_src_t_ref[...]).astype(BF16)
    stores = []
    for i, part in enumerate(pieces(owned, owned // 4)):
        out = base_ref[part, :] + mm(hot_ref[part, :], rows_ref[...])
        out_ref[part, :] = out.astype(BF16)
        stores.append(pltpu.make_async_copy(out_ref.at[part], mesh_hbm.at[part], sems.at[i]))
        stores[-1].start()
    for store in stores:
        store.wait()


def per_device(
    grid_latent,
    mesh_latent,
    edge_attr,
    neighbours,
    send_rows,
    target,
    field_weight,
    w_src,
    w_dst,
    w_edge,
    w_msg,
    ln_gain,
    w_out,
):
    grid_rows = grid_latent[0]
    mesh_rows = mesh_latent[0]
    points, channels = grid_rows.shape
    owned = mesh_rows.shape[0]
    halo = send_rows.shape[1]
    edges = neighbours.shape[1]
    feats = w_edge.shape[0]
    lanes = 128
    fields = -(-w_out.shape[1] // lanes) * lanes
    sent = -(-w_out.shape[1] // 16) * 16
    block = min(points, 512)
    sds = jax.ShapeDtypeStruct
    members = lax.axis_size("member")
    bands = lax.axis_size("band")
    near_swap = swap(range(0, bands - 1, 2))
    far_swap = swap(range(1, bands - 1, 2))
    vmem, far_memory = pltpu.VMEM, pltpu.HBM
    slots = neighbours.T
    gain = ln_gain[None, :]
    w_out = w_out.T
    weight = field_weight[None, :]

    far_shapes = [sds((halo, channels), BF16)]
    near_shapes = [sds((halo // 2, channels), BF16)] * 2
    needed = [mesh_rows, w_src, send_rows]
    *far, mesh_rows, w_src, send_rows = call(
        far_kernel,
        [far_memory] * 3,
        [vmem] * 4,
        far_shapes + [sds(array.shape, array.dtype) for array in needed],
        2 * owned * channels * halo,
        2 * owned * channels,
        [pltpu.SemaphoreType.DMA((4,))],
    )(*map(hbm, needed))
    far = [lax.ppermute(piece, "band", far_swap) for piece in far]

    held = [grid_rows, w_dst, w_msg, target]
    src, *near = call(
        functools.partial(near_kernel, len(held)),
        [vmem] * 3 + [far_memory] * len(held),
        [vmem] * (1 + len(near_shapes) + len(held)),
        [sds((owned, channels), BF16), *near_shapes]
        + [sds(array.shape, array.dtype) for array in held],
        *IN_SHADOW,
        [pltpu.SemaphoreType.DMA((len(held),))],
    )(mesh_rows, w_src, send_rows, *map(hbm, held))
    *near, grid_rows, w_dst, w_msg, target = near
    near = [lax.ppermute(piece, "band", near_swap) for piece in near]

    chunks = 2
    part = points // chunks
    dst, columns, rows, w_msg_t, w_src_t, w_out, target, weight = call(
        functools.partial(ready_kernel, owned),
        [vmem] * 8,
        [vmem] * 8,
        [
            sds((points, channels), F32),
            sds((edges, points, halo), BF16),
            sds((chunks, halo, edges * part), BF16),
            sds(w_msg.shape, BF16),
            sds(w_src.shape, BF16),
            sds((fields, channels), BF16),
            sds((fields, points), F32),
            sds((1, fields), F32),
        ],
        *IN_SHADOW,
    )(slots, grid_rows, w_dst, w_msg, w_src, w_out, target, weight)

    [pre] = call(
        functools.partial(own_kernel, block),
        [vmem] * (5 + len(near)),
        [vmem],
        [sds((edges, points, channels), BF16)],
        *IN_SHADOW,
        [
            vmem((edges, lanes, channels), BF16),
            vmem((feats * edges, points), F32),
            vmem((halo, channels), BF16),
        ],
    )(slots, src, dst, edge_attr, w_edge, *near)

    ahead = []
    for c in range(chunks):
        pred, pred_bf, sg, zhat, rstd = call(
            functools.partial(forward_kernel, c * part, block),
            [vmem] * (6 + len(far)),
            [vmem] * 5,
            [
                sds((fields, part), F32),
                sds((sent, part), BF16),
                sds((edges, part, channels), BF16),
                sds((part, channels), BF16),
                sds((part, lanes), F32),
            ],
            2 * part * channels * (edges * halo + channels),
            part * channels * edges * 4,
        )(columns, pre, grid_rows, w_msg, gain, w_out, *far)
        if members == 2:
            others = lax.ppermute(pred_bf, "member", [(0, 1), (1, 0)])[None]
        else:
            others = lax.all_gather(pred_bf[None], "member", axis=0, tiled=True)
        ahead.append((pred, others, sg, zhat, rstd))

    coeff = ALPHA / (members - 1) + (1.0 - ALPHA) / members
    far = []
    d_zs, d_pres = [], []
    for c, (pred, others, sg, zhat, rstd) in enumerate(ahead):
        rim_shapes = far_shapes if c == chunks - 1 else [sds((halo, channels), F32)]
        d_z, d_pre, *far = call(
            functools.partial(backward_kernel, c, block, coeff, len(far)),
            [vmem] * (11 + len(far)),
            [vmem] * (2 + len(rim_shapes)),
            [sds((part, channels), BF16), sds((edges, part, channels), BF16), *rim_shapes],
            2 * part * channels * (edges * halo + channels),
            part * channels * edges * 4,
        )(rows, pred, others, target, weight, w_out, gain, zhat, rstd, w_msg_t, sg, *far)
        d_zs.append(d_z)
        d_pres.append(d_pre)
    far = [lax.ppermute(piece, "band", far_swap) for piece in far]

    near = call(
        functools.partial(rim_kernel, owned, chunks),
        [vmem] * (1 + chunks),
        [vmem] * len(near_shapes),
        near_shapes,
        *IN_SHADOW,
        [vmem((halo, channels), F32), vmem((chunks, halo, edges * part), BF16)],
    )(slots, *d_pres)
    near = [lax.ppermute(piece, "band", near_swap) for piece in near]

    d_grid, own = call(
        functools.partial(own_grad_kernel, chunks),
        [vmem] * (2 + 2 * chunks),
        [far_memory, vmem],
        [sds((points, channels), BF16), sds((owned, channels), F32)],
        *IN_SHADOW,
        [
            vmem((points, channels), BF16),
            vmem((part, channels), BF16),
            vmem((part, channels), F32),
            vmem((chunks, owned, edges * part), BF16),
            pltpu.SemaphoreType.DMA((chunks,)),
        ],
    )(slots, w_dst, *[ref for pair in zip(d_zs, d_pres) for ref in pair])

    base, far_hot = call(
        merge_kernel,
        [vmem] * (3 + len(near)),
        [vmem] * 2,
        [sds((owned, channels), F32), sds((owned, halo), BF16)],
        *IN_SHADOW,
        [vmem((halo, channels), BF16), vmem((owned, halo), BF16)],
    )(send_rows, own, w_src_t, *near)

    [d_mesh] = call(
        mesh_kernel,
        [vmem] * (3 + len(far)),
        [far_memory],
        [sds((owned, channels), BF16)],
        2 * owned * channels * (channels + halo),
        owned * channels * 8,
        [
            vmem((halo, channels), BF16),
            vmem((owned, channels), BF16),
            pltpu.SemaphoreType.DMA((4,)),
        ],
    )(far_hot, base, w_src_t, *far)
    return (d_grid[None], d_mesh[None])


def solution(mesh):
    placed = (
        P("member", "band", None),
        P("member", "band", None),
        P(None, None, "band"),
        P("band", None),
        P("band", None),
        P(None, "band"),
        P(),
        P(),
        P(),
        P(),
        P(),
        P(),
        P(),
    )
    return jax.shard_map(
        per_device,
        mesh=mesh,
        in_specs=placed,
        out_specs=(P("member", "band", None), P("member", "band", None)),
        check_vma=False,
    )
```

```python
import functools

import jax
import jax.numpy as jnp
from jax import lax
from jax.experimental import pallas as pl
from jax.experimental.pallas import tpu as pltpu
from jax.sharding import PartitionSpec as P

DELTA_SQ = 0.0625
ALPHA = 0.95
LN_EPS = 1e-05
F32 = jnp.float32
BF16 = jnp.bfloat16
IN_SHADOW = (1, 1)
VMEM_LIMIT = 28 * 1024 * 1024


def slope(diff):
    return diff * lax.rsqrt(diff * diff + DELTA_SQ)


def mm(left, right):
    return jnp.dot(left, right, preferred_element_type=F32)


def mm_t(left, right):
    return lax.dot_general(left, right, (((1,), (1,)), ((), ())), preferred_element_type=F32)


STRIP = 16


def strips(rows, size=STRIP):
    return [slice(first, first + size) for first in range(0, rows, size)]


def column_of(ids):
    lanes = 128
    rows = ids.shape[1]
    column = jnp.broadcast_to(ids.astype(F32), (lanes, rows)).T.astype(jnp.int16)
    return column - lax.broadcasted_iota(jnp.int16, (rows, lanes), 1)


def column_hot(column, base, slots):
    offset = column - jnp.broadcast_to(base, column.shape).astype(jnp.int16)
    parts = [
        jnp.where(offset == jnp.int16(first), BF16(1), BF16(0))
        for first in range(0, slots, column.shape[1])
    ]
    return jnp.concatenate(parts, axis=1)


def fill_rows(hot_ref, ids, base):
    edges, points = ids.shape
    sublane = lax.broadcasted_iota(jnp.int16, (STRIP, points), 0)
    for k in range(edges):
        row = jnp.broadcast_to(ids[k : k + 1, :] - base, (STRIP, points)).astype(jnp.int16)
        offset = row - sublane
        for part in strips(hot_ref.shape[0]):
            hot_ref[part, k * points : (k + 1) * points] = jnp.where(
                offset == jnp.int16(part.start), BF16(1), BF16(0)
            )


def swap(firsts):
    return [pair for i in firsts for pair in ((i, i + 1), (i + 1, i))]


def hbm(array):
    return pltpu.with_memory_space_constraint(array, pltpu.HBM)


def call(body, places, out_places, out_shape, flops, nbytes, scratch=()):
    def specs(memories):
        return [pl.BlockSpec(memory_space=memory) for memory in memories]

    return pl.pallas_call(
        body,
        in_specs=specs(places),
        out_specs=specs(out_places),
        out_shape=out_shape,
        scratch_shapes=scratch,
        compiler_params=pltpu.CompilerParams(vmem_limit_bytes=VMEM_LIMIT),
        cost_estimate=pl.CostEstimate(flops=flops, bytes_accessed=nbytes, transcendentals=0),
    )


def near_far(low, high):
    odd = lax.axis_index("band") % 2 == 1
    return jnp.where(odd, low, high), jnp.where(odd, high, low)


def rim_bases(owned, halo):
    return near_far(owned, owned + halo)


def rows_to(array, rows):
    array = array.astype(F32)
    return jnp.concatenate([array, jnp.zeros((rows - array.shape[0], array.shape[1]), F32)], axis=0)


def pieces(rows, size):
    return [slice(first, first + size) for first in range(0, rows, size)]


def placed_rows(refs):
    first, out = 0, []
    for ref in refs:
        out.append((slice(first, first + ref.shape[0]), ref))
        first += ref.shape[0]
    return out


def join(refs, whole_ref):
    for rows, ref in placed_rows(refs):
        whole_ref[rows, :] = ref[...]


def far_kernel(held, mesh_hbm, w_src_hbm, send_hbm, *refs):
    held_hbm, (far_ref, mesh_ref, w_src_ref, *held_refs) = refs[:held], refs[held:-2]
    send_ref, sems = refs[-2:]
    owned = mesh_ref.shape[0]
    parts = pieces(owned, owned // 2)
    moves = [(send_hbm, send_ref)]
    moves += [(mesh_hbm.at[part], mesh_ref.at[part]) for part in parts]
    moves += [(w_src_hbm, w_src_ref), *zip(held_hbm, held_refs)]
    loads = [pltpu.make_async_copy(*move, sems.at[i]) for i, move in enumerate(moves)]
    for load in loads:
        load.start()
    loads[0].wait()
    far = near_far(send_ref[0:1, :], send_ref[1:2, :])[1]
    column = column_of(far)
    hots = [column_hot(column, part.start, part.stop - part.start) for part in parts]
    rows = None
    for load, part, hot in zip(loads[1:], parts, hots):
        load.wait()
        picked = mm(hot, mesh_ref[part])
        rows = picked if rows is None else rows + picked
    loads[1 + len(parts)].wait()
    far_ref[...] = mm(rows.astype(BF16), w_src_ref[...]).astype(BF16)
    for load in loads[2 + len(parts) :]:
        load.wait()


def near_kernel(mesh_ref, w_src_ref, send_ref, src_ref, *near_refs):
    src = mm(mesh_ref[...], w_src_ref[...]).astype(BF16)
    src_ref[...] = src
    near = near_far(send_ref[0:1, :], send_ref[1:2, :])[0]
    rows = mm(column_hot(column_of(near), 0, src.shape[0]), src_ref[...]).astype(BF16)
    for part, near_ref in placed_rows(near_refs):
        near_ref[...] = rows[part, :]


def own_kernel(
    block,
    slots_ref,
    src_ref,
    grid_ref,
    w_dst_ref,
    attr_ref,
    w_edge_ref,
    *refs,
):
    *near_refs, pre_ref, columns_ref, rows_ref, dst_ref, embed_ref, attr_f32, near_ref = refs
    join(near_refs, near_ref)
    edges, lanes, channels = embed_ref.shape
    feats = w_edge_ref.shape[0]
    row = lax.broadcasted_iota(jnp.int32, (lanes, channels), 0)
    w_edge = w_edge_ref[...].astype(F32)
    for k in range(edges):
        spread = jnp.zeros((lanes, channels), F32)
        for e in range(feats):
            spread = jnp.where(row == e * edges + k, w_edge[e : e + 1, :], spread)
        embed_ref[k] = spread.astype(BF16)
    for e in range(feats):
        attr_f32[e * edges : (e + 1) * edges, :] = attr_ref[e].astype(F32)
    owned = src_ref.shape[0]
    halo = near_ref.shape[0]
    base, far = rim_bases(owned, halo)
    for at, rows in enumerate(pieces(grid_ref.shape[0], block)):
        dst_ref[at] = mm(grid_ref[rows, :], w_dst_ref[...])
        attr = rows_to(attr_f32[:, rows], lanes).T.astype(BF16)
        for k in range(edges):
            column = column_of(slots_ref[k : k + 1, rows])
            picked = mm(column_hot(column, 0, owned), src_ref[...])
            picked = picked + mm(column_hot(column, base, halo), near_ref[...])
            embed = mm(attr, embed_ref[k])
            pre_ref[k, rows, :] = (picked + embed + dst_ref[at]).astype(BF16)
            columns_ref[k, rows, :] = column_hot(column, far, halo)
    chunks, _, width = rows_ref.shape
    part = width // edges
    for c in range(chunks):
        fill_rows(rows_ref.at[c], slots_ref[:, c * part : (c + 1) * part], far)


def forward_kernel(
    first,
    block,
    fields,
    columns_ref,
    pre_ref,
    grid_ref,
    w_msg_ref,
    gain_ref,
    w_out_ref,
    far_ref,
    pred_ref,
    pred_bf_ref,
    sg_ref,
    zhat_ref,
    rstd_ref,
):
    half = BF16(0.5)
    w_out = rows_to(w_out_ref[...], fields).astype(BF16)
    for rows in pieces(zhat_ref.shape[0], block):
        source = slice(first + rows.start, first + rows.stop)
        acts = []
        for k in range(columns_ref.shape[0]):
            picked = mm(columns_ref[k, source, :], far_ref[...])
            pre = pre_ref[k, source, :] + picked.astype(BF16)
            sigma = half + half * jnp.tanh(half * pre)
            act = pre * sigma
            acts.append(act)
            sg_ref[k, rows, :] = sigma + (act - act * sigma)
        while len(acts) > 1:
            acts = [sum(acts[i : i + 2][1:], acts[i]) for i in range(0, len(acts), 2)]
        z = grid_ref[source, :].astype(F32) + mm(acts[0], w_msg_ref[...])
        centre = z - jnp.mean(z, axis=1, keepdims=True)
        rstd = lax.rsqrt(jnp.mean(centre * centre, axis=1, keepdims=True) + LN_EPS)
        zhat = centre * rstd
        pred = mm_t(w_out, (zhat * gain_ref[...]).astype(BF16))
        pred_ref[:, rows] = pred
        pred_bf_ref[:, rows] = pred[: pred_bf_ref.shape[0], :].astype(BF16)
        zhat_ref[rows, :] = zhat.astype(BF16)
        rstd_ref[rows, :] = jnp.broadcast_to(rstd, (block, rstd_ref.shape[1]))


def backward_kernel(
    chunk,
    block,
    coeff,
    given,
    hot_ref,
    pred_ref,
    others_ref,
    target_ref,
    weight_ref,
    w_out_ref,
    gain_ref,
    zhat_ref,
    rstd_ref,
    w_msg_ref,
    sg_ref,
    *refs,
):
    prior, (dz_ref, dpre_ref, far_ref, dpred_ref, wide_ref) = refs[:given], refs[given:]
    fields = pred_ref.shape[0]
    edges, points, channels = dpre_ref.shape
    first = chunk * points
    weight = weight_ref[...]
    weight = jnp.concatenate([weight, jnp.zeros((1, fields - weight.shape[1]), F32)], axis=1)
    w_out = rows_to(w_out_ref[...], fields).astype(BF16)
    gain = gain_ref[...]
    sent = others_ref.shape[1]
    for rows in pieces(points, block):
        for part in strips(block, 128):
            part = slice(rows.start + part.start, rows.start + part.stop)
            pred = pred_ref[:, part]
            spread = jnp.zeros((sent, 128), F32)
            for other in range(others_ref.shape[0]):
                spread = spread + slope(pred[:sent, :] - others_ref[other, :, part].astype(F32))
            target = target_ref[:, first + part.start : first + part.stop]
            d_pred = slope(pred - rows_to(target, fields)) - coeff * rows_to(spread, fields)
            dpred_ref[part, :] = (weight * d_pred.T).astype(BF16)
        wide_ref[rows, :] = mm(dpred_ref[rows, :], w_out)
        for part in strips(block, 32):
            part = slice(rows.start + part.start, rows.start + part.stop)
            scaled = wide_ref[part, :] * gain
            zhat = zhat_ref[part, :].astype(F32)
            d_z = rstd_ref[part, :1] * (
                scaled
                - jnp.mean(scaled, axis=1, keepdims=True)
                - zhat * jnp.mean(scaled * zhat, axis=1, keepdims=True)
            )
            dz_ref[part, :] = d_z.astype(BF16)
        wide_ref[rows, :] = mm_t(dz_ref[rows, :], w_msg_ref[...])
        for part in strips(block):
            part = slice(rows.start + part.start, rows.start + part.stop)
            d_act = wide_ref[part, :].astype(BF16)
            for k in range(edges):
                dpre_ref[k, part, :] = d_act * sg_ref[k, part, :]
    far = mm(hot_ref[chunk], dpre_ref[...].reshape(edges * points, channels))
    if prior:
        far = far + prior[0][...].astype(F32)
    far_ref[...] = far.astype(far_ref.dtype)


def rim_kernel(owned, chunks, slots_ref, *refs):
    dpre_refs = refs[:chunks]
    *near_refs, acc, hot_ref = refs[chunks:]
    base = rim_bases(owned, acc.shape[0])[0]
    first = 0
    for c, dpre_ref in enumerate(dpre_refs):
        edges, points, channels = dpre_ref.shape
        fill_rows(hot_ref.at[c], slots_ref[:, first : first + points], base)
        first += points
        added = mm(hot_ref[c], dpre_ref[...].reshape(edges * points, channels))
        acc[...] = added if c == 0 else acc[...] + added
    for rows, near_ref in placed_rows(near_refs):
        near_ref[...] = acc[rows, :].astype(BF16)


def own_grad_kernel(chunks, slots_ref, w_dst_ref, *refs):
    grid_hbm, own_ref, grid_ref, dsum_ref, wide_ref, hot_ref, sems = refs[-7:]
    stores = []
    for c in range(chunks):
        dz_ref, dpre_ref = refs[2 * c : 2 * c + 2]
        edges, points, channels = dpre_ref.shape
        rows = slice(c * points, (c + 1) * points)
        for part in strips(points):
            d_sum = sum(dpre_ref[k, part, :].astype(F32) for k in range(edges))
            dsum_ref[part, :] = d_sum.astype(BF16)
        wide_ref[...] = mm_t(dsum_ref[...], w_dst_ref[...])
        for part in strips(points):
            d_grid = dz_ref[part, :].astype(F32) + wide_ref[part, :]
            grid_ref[rows.start + part.start : rows.start + part.stop, :] = d_grid.astype(BF16)
        stores.append(pltpu.make_async_copy(grid_ref.at[rows], grid_hbm.at[rows], sems.at[c]))
        stores[-1].start()
        fill_rows(hot_ref.at[c], slots_ref[:, rows], 0)
        added = mm(hot_ref[c], dpre_ref[...].reshape(edges * points, channels))
        own_ref[...] = added if c == 0 else own_ref[...] + added
    for store in stores:
        store.wait()


def merge_kernel(send_ref, own_ref, w_src_ref, *refs):
    *near_refs, base_ref, hot_ref, near_ref, near_hot = refs
    join(near_refs, near_ref)
    near, far = near_far(send_ref[0:1, :], send_ref[1:2, :])
    fill_rows(near_hot, near, 0)
    total = own_ref[...] + mm(near_hot[...], near_ref[...])
    base_ref[...] = mm_t(total.astype(BF16), w_src_ref[...]).astype(BF16)
    fill_rows(hot_ref, far, 0)


def mesh_kernel(hot_ref, base_ref, w_src_ref, *refs):
    *far_refs, mesh_hbm, rows_ref, out_ref, sems = refs
    owned = base_ref.shape[0]
    size = far_refs[0].shape[0]
    for i, far_ref in enumerate(far_refs):
        rows_ref[i * size : (i + 1) * size, :] = mm_t(far_ref[...], w_src_ref[...]).astype(BF16)
    stores = []
    for i, part in enumerate(pieces(owned, owned // 4)):
        out = base_ref[part, :].astype(F32) + mm(hot_ref[part, :], rows_ref[...])
        out_ref[part, :] = out.astype(BF16)
        stores.append(pltpu.make_async_copy(out_ref.at[part], mesh_hbm.at[part], sems.at[i]))
        stores[-1].start()
    for store in stores:
        store.wait()


def per_device(
    grid_latent,
    mesh_latent,
    edge_attr,
    neighbours,
    send_rows,
    target,
    field_weight,
    w_src,
    w_dst,
    w_edge,
    w_msg,
    ln_gain,
    w_out,
):
    grid_rows = grid_latent[0]
    mesh_rows = mesh_latent[0]
    points, channels = grid_rows.shape
    owned = mesh_rows.shape[0]
    halo = send_rows.shape[1]
    edges = neighbours.shape[1]
    feats = w_edge.shape[0]
    lanes = 128
    fields = -(-w_out.shape[1] // lanes) * lanes
    sent = -(-w_out.shape[1] // 16) * 16
    block = min(points, 512)
    sds = jax.ShapeDtypeStruct
    members = lax.axis_size("member")
    bands = lax.axis_size("band")
    near_swap = swap(range(0, bands - 1, 2))
    far_swap = swap(range(1, bands - 1, 2))
    vmem, far_memory = pltpu.VMEM, pltpu.HBM
    slots = neighbours.T
    gain = ln_gain[None, :]
    w_out = w_out.T
    weight = field_weight[None, :]

    far_shapes = [sds((halo, channels), BF16)]
    near_shapes = [sds((halo // 2, channels), BF16)] * 2
    held = [grid_rows, w_dst]
    *far, mesh_rows, w_src, grid_rows, w_dst = call(
        functools.partial(far_kernel, len(held)),
        [far_memory] * (3 + len(held)),
        [vmem] * (3 + len(held)),
        far_shapes + [sds(array.shape, BF16) for array in (mesh_rows, w_src, *held)],
        2 * owned * channels * halo,
        2 * owned * channels,
        [
            vmem((2, halo), jnp.int32),
            pltpu.SemaphoreType.DMA((4 + len(held),)),
        ],
    )(*map(hbm, (mesh_rows, w_src, send_rows, *held)))
    far = [lax.ppermute(piece, "band", far_swap) for piece in far]

    src, *near = call(
        near_kernel,
        [vmem] * 3,
        [vmem] * (1 + len(near_shapes)),
        [sds((owned, channels), BF16), *near_shapes],
        *IN_SHADOW,
    )(mesh_rows, w_src, send_rows)
    near = [lax.ppermute(piece, "band", near_swap) for piece in near]

    chunks = 2
    part = points // chunks
    pre, columns, rows = call(
        functools.partial(own_kernel, block),
        [vmem] * (6 + len(near)),
        [vmem] * 3,
        [
            sds((edges, points, channels), BF16),
            sds((edges, points, halo), BF16),
            sds((chunks, halo, edges * part), BF16),
        ],
        *IN_SHADOW,
        [
            vmem((points // block, block, channels), F32),
            vmem((edges, lanes, channels), BF16),
            vmem((feats * edges, points), F32),
            vmem((halo, channels), BF16),
        ],
    )(slots, src, grid_rows, w_dst, edge_attr, w_edge, *near)

    ahead = []
    for c in range(chunks):
        pred, pred_bf, sg, zhat, rstd = call(
            functools.partial(forward_kernel, c * part, block, fields),
            [vmem] * (6 + len(far)),
            [vmem] * 5,
            [
                sds((fields, part), F32),
                sds((sent, part), BF16),
                sds((edges, part, channels), BF16),
                sds((part, channels), BF16),
                sds((part, lanes), F32),
            ],
            2 * part * channels * (edges * halo + channels),
            part * channels * edges * 4,
        )(columns, pre, grid_rows, w_msg, gain, w_out, *far)
        if members == 2:
            others = lax.ppermute(pred_bf, "member", [(0, 1), (1, 0)])[None]
        else:
            others = lax.all_gather(pred_bf[None], "member", axis=0, tiled=True)
        ahead.append((pred, others, sg, zhat, rstd))

    coeff = ALPHA / (members - 1) + (1.0 - ALPHA) / members
    far = []
    d_zs, d_pres = [], []
    for c, (pred, others, sg, zhat, rstd) in enumerate(ahead):
        rim_shapes = far_shapes if c == chunks - 1 else [sds((halo, channels), BF16)]
        d_z, d_pre, *far = call(
            functools.partial(backward_kernel, c, block, coeff, len(far)),
            [vmem] * (11 + len(far)),
            [vmem] * (2 + len(rim_shapes)),
            [sds((part, channels), BF16), sds((edges, part, channels), BF16), *rim_shapes],
            2 * part * channels * (edges * halo + channels),
            part * channels * edges * 4,
            [
                vmem((part, fields), BF16),
                vmem((part, channels), F32),
            ],
        )(rows, pred, others, target, weight, w_out, gain, zhat, rstd, w_msg, sg, *far)
        d_zs.append(d_z)
        d_pres.append(d_pre)
    far = [lax.ppermute(piece, "band", far_swap) for piece in far]

    near = call(
        functools.partial(rim_kernel, owned, chunks),
        [vmem] * (1 + chunks),
        [vmem] * len(near_shapes),
        near_shapes,
        *IN_SHADOW,
        [vmem((halo, channels), F32), vmem((chunks, halo, edges * part), BF16)],
    )(slots, *d_pres)
    near = [lax.ppermute(piece, "band", near_swap) for piece in near]

    d_grid, own = call(
        functools.partial(own_grad_kernel, chunks),
        [vmem] * (2 + 2 * chunks),
        [far_memory, vmem],
        [sds((points, channels), BF16), sds((owned, channels), F32)],
        *IN_SHADOW,
        [
            vmem((points, channels), BF16),
            vmem((part, channels), BF16),
            vmem((part, channels), F32),
            vmem((chunks, owned, edges * part), BF16),
            pltpu.SemaphoreType.DMA((chunks,)),
        ],
    )(slots, w_dst, *[ref for pair in zip(d_zs, d_pres) for ref in pair])

    base, far_hot = call(
        merge_kernel,
        [vmem] * (3 + len(near)),
        [vmem] * 2,
        [sds((owned, channels), BF16), sds((owned, halo), BF16)],
        *IN_SHADOW,
        [vmem((halo, channels), BF16), vmem((owned, halo), BF16)],
    )(send_rows, own, w_src, *near)

    [d_mesh] = call(
        mesh_kernel,
        [vmem] * (3 + len(far)),
        [far_memory],
        [sds((owned, channels), BF16)],
        2 * owned * channels * (channels + halo),
        owned * channels * 8,
        [
            vmem((halo, channels), BF16),
            vmem((owned, channels), BF16),
            pltpu.SemaphoreType.DMA((4,)),
        ],
    )(far_hot, base, w_src, *far)
    return (d_grid[None], d_mesh[None])


def solution(mesh):
    placed = (
        P("member", "band", None),
        P("member", "band", None),
        P(None, None, "band"),
        P("band", None),
        P("band", None),
        P(None, "band"),
        P(),
        P(),
        P(),
        P(),
        P(),
        P(),
        P(),
    )
    return jax.shard_map(
        per_device,
        mesh=mesh,
        in_specs=placed,
        out_specs=(P("member", "band", None), P("member", "band", None)),
        check_vma=False,
    )
```
